32 devices in a mesh: seq: 8 (over z, x), head: 4 (over y, core).
Axes of the slice: x: 2, y: 2, z: 4, core: 2. Of those that a mesh axis runs over, the one named last changes fastest.
Arguments:
- inputs: bfloat16 [8192, 2048], P('seq', 'head'), may hold values from -6 to 6
- w_qkv: bfloat16 [3, 2048, 2048], P(None, None, 'head'), may hold values from -0.125 to 0.125
- level_weight: float32 [16, 4], P('head'), may hold values from 0.5 to 2
- grad_out: bfloat16 [8192, 2048], P('seq', 'head'), may hold values from -6 to 6
Outputs:
- attn_out: bfloat16 [8192, 2048], P('seq', 'head')
- grad_query: bfloat16 [8192, 2048], P('seq', 'head')
- grad_key: bfloat16 [8192, 2048], P('seq', 'head')
- grad_value: bfloat16 [8192, 2048], P('seq', 'head')
The draws below stay inside these ranges and needn't reach their ends.
All inputs are finite; a program needn't handle non-finite values.
Results may differ from the reference program's by a relative error of at most 0.012.
Values may be sent and summed in bfloat16 or wider, within the bound.
No kernel may reach another device: no remote copies, remote signals or barrier semaphores. Data moves between devices by JAX's collectives and lax.ppermute only.
A program may use at most 128 MiB of HBM per device.

```python
import math
import jax
import jax.numpy as jnp
from jax import lax

D = 2048
H = 16
E = 128
TOK_DEV = 1024
TOKENS = 8192
LEVELS = 4
N_SEQ = 8


def levels(rng, dims, cuts, low, top_value):
    def one(position, parts):
        draws = jax.random.uniform(jax.random.fold_in(jax.random.fold_in(rng, 6), position), (parts,), jnp.float32, low / len(cuts), top_value / len(cuts))
        return jnp.repeat(jnp.exp(draws), dims[position] // parts).reshape((-1,) + (1,) * (len(dims) - position - 1))

    loudness = one(*cuts[0])
    for cut in cuts[1:]:
        loudness = loudness * one(*cut)
    return loudness


def normal_values(key, dims, deviation, limit, cuts=(), kind=jnp.bfloat16):
    result = jax.random.normal(key, dims, jnp.float32) * deviation
    if len(cuts) > 0:
        result = levels(key, dims, cuts, -0.22, 0.18) * result
    return jnp.clip(result, min=-limit, max=limit).astype(kind)


def setup_inputs(seed: int = 0) -> dict:
    key_of = jax.random.split(jax.random.key(seed), 5)
    return {
        "inputs": normal_values(key_of[0], (TOKENS, D), 1.0, 6.0, ((0, 8), (1, 4))),
        "w_qkv": normal_values(key_of[1], (3, D, H * E), D ** -0.5, 0.125, ((2, 4),)),
        "level_weight": jnp.clip(jnp.exp(math.log(2.0) - 1.3862944 * jax.random.uniform(key_of[2], (H, LEVELS), jnp.float32) ** levels(key_of[2], (H, LEVELS), ((0, 4),), -0.2, 0.2)), 0.5, 2.0),
        "grad_out": normal_values(key_of[3], (TOKENS, H * E), 1.0, 6.0, ((0, 8), (1, 4))),
    }


def reference(inputs, w_qkv, level_weight, grad_out):
    projected = [jnp.dot(inputs, w_qkv[j], preferred_element_type=jnp.float32).astype(jnp.bfloat16) for j in range(3)]
    queries = projected[0].reshape(N_SEQ, TOK_DEV, H, E)
    keys = projected[1].reshape(N_SEQ, TOK_DEV, H, E)
    values = projected[2].reshape(N_SEQ, TOK_DEV, H, E)
    grad_rows = grad_out.reshape(N_SEQ, TOK_DEV, H, E)
    key_state = jnp.einsum('cthd,cthe->chde', keys.astype(jnp.float32), values.astype(jnp.float32))
    query_state = jnp.einsum('cthd,cthe->chde', queries.astype(jnp.float32), grad_rows.astype(jnp.float32))
    forward_list = []
    backward_list = []
    for block in range(N_SEQ):
        forward_mix = jnp.zeros((H, E, E), jnp.float32)
        backward_mix = jnp.zeros((H, E, E), jnp.float32)
        for bit_level in range(LEVELS - 1):
            sibling_size = 2 ** bit_level
            parent_start = block >> bit_level + 1 << bit_level + 1
            level_scale = (level_weight[:, bit_level + 1] / math.sqrt(E * TOK_DEV * sibling_size))[:, None, None]
            if block >> bit_level & 1:
                forward_mix = forward_mix + level_scale * lax.optimization_barrier(jnp.sum(key_state[parent_start:parent_start + sibling_size], axis=0))
            else:
                backward_mix = backward_mix + level_scale * lax.optimization_barrier(jnp.sum(query_state[parent_start + sibling_size:parent_start + 2 * sibling_size], axis=0))
        forward_list.append(forward_mix.astype(jnp.bfloat16))
        backward_list.append(backward_mix.astype(jnp.bfloat16))
    forward_all = jnp.stack(forward_list)
    backward_all = jnp.stack(backward_list)
    local_scale = (level_weight[:, 0] / math.sqrt(E * TOK_DEV))[:, None, None]
    causal = jnp.arange(TOK_DEV)[:, None] >= jnp.arange(TOK_DEV)[None, :]

    def one_block(pieces):
        block_q, block_k, block_v, block_g, forward_mix, backward_mix = pieces
        query_f = block_q.astype(jnp.float32)
        key_f = block_k.astype(jnp.float32)
        value_f = block_v.astype(jnp.float32)
        grad_f = block_g.astype(jnp.float32)
        forward_f = forward_mix.astype(jnp.float32)
        backward_f = backward_mix.astype(jnp.float32)
        scores = jnp.einsum('thd,shd->hts', query_f, key_f)
        attend = jnp.where(causal[None], scores * local_scale, 0.0).astype(jnp.bfloat16)
        grad_scores = jnp.einsum('the,she->hts', grad_f, value_f)
        grad_attend = jnp.where(causal[None], grad_scores * local_scale, 0.0).astype(jnp.bfloat16)
        attend_f = attend.astype(jnp.float32)
        grad_attend_f = grad_attend.astype(jnp.float32)
        output = jnp.einsum('hts,she->the', attend_f, value_f) + jnp.einsum('thd,hde->the', query_f, forward_f)
        grad_q = jnp.einsum('hts,shd->thd', grad_attend_f, key_f) + jnp.einsum('the,hde->thd', grad_f, forward_f)
        grad_k = jnp.einsum('hts,thd->shd', grad_attend_f, query_f) + jnp.einsum('the,hde->thd', value_f, backward_f)
        grad_v = jnp.einsum('hts,the->she', attend_f, grad_f) + jnp.einsum('thd,hde->the', key_f, backward_f)
        return (output.astype(jnp.bfloat16), grad_q.astype(jnp.bfloat16), grad_k.astype(jnp.bfloat16), grad_v.astype(jnp.bfloat16))
    output, grad_q, grad_k, grad_v = lax.map(one_block, (queries, keys, values, grad_rows, forward_all, backward_all))
    return (output.reshape(TOKENS, H * E), grad_q.reshape(TOKENS, H * E), grad_k.reshape(TOKENS, H * E), grad_v.reshape(TOKENS, H * E))
```

```python
import functools
import math

import jax
import jax.numpy as jnp
from jax import lax
from jax.experimental import pallas as pl
from jax.experimental.pallas import tpu as pltpu
from jax.sharding import PartitionSpec as P

CHUNKS = 4
MIB = 2**20
VMEM = pl.BlockSpec(memory_space=pltpu.VMEM)
SMEM = pl.BlockSpec(memory_space=pltpu.SMEM)
NT = (((1,), (1,)), ((), ()))
TN = (((0,), (0,)), ((), ()))


def dot(a, b, dims=(((1,), (0,)), ((), ()))):
    return lax.dot_general(a, b, dims, preferred_element_type=jnp.float32)


def swap(value, axis, mask):
    pairs = [(source, source ^ mask) for source in range(lax.axis_size(axis))]
    return lax.ppermute(value, axis, pairs)


def in_vmem(shape, dtype):
    return pltpu.VMEM(shape, dtype)


def project_kernel(parts, heads, last, place_ref, w_ref, g_ref, *refs):
    segments, refs = refs[:parts], refs[parts:]
    if last:
        earlier, refs = refs[: last], refs[last:]
    q_ref, k_ref, v_ref, state_ref = refs[:4]
    me, odd = place_ref[0], place_ref[1]
    depth = segments[0].shape[1]
    size = q_ref.shape[1] // heads
    for j, out_ref in enumerate((q_ref, k_ref, v_ref)):
        total = None
        for k in range(parts):
            start = pl.multiple_of((me ^ k) * depth, depth)
            term = dot(segments[k][...], w_ref[j, pl.ds(start, depth), :])
            total = term if total is None else total + term
        out_ref[...] = total.astype(out_ref.dtype)
    for h in range(heads):
        cols = slice(h * size, (h + 1) * size)
        state_ref[0, h] = dot(k_ref[:, cols], v_ref[:, cols], TN)
        state_ref[1, h] = dot(q_ref[:, cols], g_ref[:, cols], TN)
    if last:
        total_ref, payload_ref = refs[4:]
        half = heads // 2
        for h in range(heads):
            for s in range(2):
                total = state_ref[s, h]
                for other in earlier:
                    total = total + other[s, h]
                total_ref[s, h] = total.astype(total_ref.dtype)
        for h in range(heads):
            payload_ref[h] = jnp.where(odd == 1, total_ref[1, h], total_ref[0, h])
        for h in range(half):
            payload_ref[heads + h] = jnp.where(odd == 1, total_ref[0, h], total_ref[1, half + h])


def local_kernel(heads, scale_ref, q_ref, k_ref, v_ref, g_ref, out_ref):
    rows = q_ref.shape[0]
    size = q_ref.shape[1] // heads
    at = lax.broadcasted_iota(jnp.int32, (rows, rows), 0)
    of = lax.broadcasted_iota(jnp.int32, (rows, rows), 1)
    causal = at >= of
    for h in range(heads):
        cols = slice(h * size, (h + 1) * size)
        q, k, v, g = q_ref[:, cols], k_ref[:, cols], v_ref[:, cols], g_ref[:, cols]
        scale = scale_ref[h]
        attend = jnp.where(causal, dot(q, k, NT) * scale, 0.0).astype(jnp.bfloat16)
        grad = jnp.where(causal, dot(g, v, NT) * scale, 0.0).astype(jnp.bfloat16)
        out_ref[0, :, cols] = dot(attend, v)
        out_ref[1, :, cols] = dot(grad, k)
        out_ref[2, :, cols] = dot(grad, q, TN)
        out_ref[3, :, cols] = dot(attend, g, TN)


def finish_kernel(chunks, heads, depth, place_ref, scale_ref, coef_ref, g_ref, near_ref, *refs):
    own, refs = refs[: depth - 1], refs[depth - 1 :]
    far_ref, refs = refs[0], refs[1:]
    q_refs, refs = refs[:chunks], refs[chunks:]
    k_refs, refs = refs[:chunks], refs[chunks:]
    v_refs, refs = refs[:chunks], refs[chunks:]
    state_refs, refs = refs[:chunks], refs[chunks:]
    part_refs, refs = refs[:chunks], refs[chunks:]
    outs, (held, mix_ref, sems) = refs[:4], refs[4:]
    odd = place_ref[1]
    rows = q_refs[0].shape[0]
    size = q_refs[0].shape[1] // heads
    half = heads // 2
    for h in range(heads):
        forward = coef_ref[0, 0, h] * near_ref[h].astype(jnp.float32)
        backward = coef_ref[1, 0, h] * near_ref[h].astype(jnp.float32)
        for level in range(1, depth):
            mine = own[level - 1][h % half].astype(jnp.float32)
            other = far_ref[level - 1, h % half].astype(jnp.float32)
            value = jnp.where(odd == h // half, mine, other)
            forward = forward + coef_ref[0, level, h] * value
            backward = backward + coef_ref[1, level, h] * value
        mix_ref[0, h] = forward
        mix_ref[1, h] = backward
    zero = jnp.zeros((size, size), jnp.bfloat16)
    copies = []
    for c in range(chunks):
        span = slice(c * rows, (c + 1) * rows)
        for h in range(0, heads, 2):
            cols = slice(h * size, (h + 2) * size)
            blocks = []
            for s in range(2):
                pair = []
                for e in (h, h + 1):
                    value = None
                    for other in (range(c) if s == 0 else range(c + 1, chunks)):
                        term = state_refs[other][s, e]
                        value = term if value is None else value + term
                    mix = mix_ref[s, e]
                    if value is not None:
                        mix = mix + scale_ref[e] * value
                    pair.append(mix.astype(jnp.bfloat16))
                blocks.append(
                    jnp.concatenate(
                        [
                            jnp.concatenate([pair[0], zero], axis=1),
                            jnp.concatenate([zero, pair[1]], axis=1),
                        ],
                        axis=0,
                    )
                )
            forward, backward = blocks
            terms = (
                dot(q_refs[c][:, cols], forward),
                dot(g_ref[span, cols], forward, NT),
                dot(v_refs[c][:, cols], backward, NT),
                dot(k_refs[c][:, cols], backward),
            )
            for j in range(4):
                value = terms[j] + part_refs[c][j, :, cols]
                held[j, span, cols] = value.astype(held.dtype)
        for j in range(4):
            copy = pltpu.make_async_copy(held.at[j, span], outs[j].at[span], sems.at[j, c])
            copy.start()
            copies.append(copy)
    for copy in copies:
        copy.wait()


def call(kernel, outs, operands, specs, limit, flops, scratch=(), out_specs=None):
    return pl.pallas_call(
        kernel,
        out_shape=outs,
        in_specs=specs,
        out_specs=[VMEM] * len(outs) if out_specs is None else out_specs,
        scratch_shapes=scratch,
        compiler_params=pltpu.CompilerParams(vmem_limit_bytes=limit),
        cost_estimate=pl.CostEstimate(flops=flops, bytes_accessed=0, transcendentals=0),
    )(*operands)


def exchange(totals, payload, heads, odd, position):
    depth = lax.axis_size("seq").bit_length() - 1
    half = heads // 2
    got = swap(payload, "seq", 1)
    near, rest = got[:heads], got[heads:]
    is_odd = odd == 1
    mine = jnp.where(is_odd, totals[:, half:], totals[:, :half]).astype(jnp.float32)
    near_half = jnp.where(is_odd, near[half:], near[:half])
    theirs = jnp.where(is_odd, jnp.stack([near_half, rest]), jnp.stack([rest, near_half]))
    sums = mine + theirs.astype(jnp.float32)
    levels = []
    bit = 1
    while bit < depth:
        count = min(2, depth - bit)
        final = bit + count >= depth
        low = sums.astype(jnp.bfloat16)
        found = [None] * count
        total = sums
        for m in sorted(range(1, 2**count), reverse=True):
            top = m.bit_length() - 1
            on = (position >> (bit + top) & 1) == 1
            if final:
                got = swap(jnp.where(on, low[1], low[0]), "seq", m << bit).astype(jnp.float32)
            else:
                both = swap(low, "seq", m << bit).astype(jnp.float32)
                total = total + both
                got = jnp.where(on, both[0], both[1])
            found[top] = got if found[top] is None else found[top] + got
        levels += [value.astype(jnp.bfloat16) for value in found]
        sums = total
        bit += count
    far = swap(jnp.stack(levels), "seq", 1)
    return near, levels, far


def per_device(inputs, w_qkv, level_weight, grad_out):
    rows, width = grad_out.shape
    heads = level_weight.shape[0]
    size = width // heads
    parts = lax.axis_size("head")
    depth = lax.axis_size("seq").bit_length() - 1
    chunk = rows // CHUNKS
    position = lax.axis_index("seq")
    odd = position & 1
    place = jnp.stack([lax.axis_index("head"), odd]).astype(jnp.int32)
    scale = level_weight[:, 0] / math.sqrt(size * rows)
    coefs = jnp.stack(
        [level_weight[:, b + 1] / math.sqrt(size * rows * 2**b) for b in range(depth)]
    )
    on = (position >> jnp.arange(depth) & 1 == 1)[:, None]
    coef = jnp.stack([jnp.where(on, coefs, 0.0), jnp.where(on, 0.0, coefs)])

    weights = pltpu.with_memory_space_constraint(w_qkv, pltpu.VMEM)
    grads = pltpu.with_memory_space_constraint(grad_out, pltpu.VMEM)

    tops = [1 << b for b in reversed(range(parts.bit_length() - 1))]
    pieces = [{0: inputs[c * chunk : (c + 1) * chunk]} for c in range(CHUNKS)]
    for c in range(CHUNKS):
        for top in tops:
            for k in sorted(pieces[c]):
                pieces[c][k | top] = swap(pieces[c][k], "head", top)

    qs, ks, vs, states, locals_ = [], [], [], [], []
    totals = payload = None
    for c in range(CHUNKS):
        last = c == CHUNKS - 1
        segments = [pieces[c][k] for k in range(parts)]
        g = grad_out[c * chunk : (c + 1) * chunk]
        flat = in_vmem((chunk, width), jnp.bfloat16)
        outs = [flat, flat, flat, in_vmem((2, heads, size, size), jnp.float32)]
        operands = [place, weights, g, *segments]
        specs = [SMEM, VMEM, VMEM] + [VMEM] * parts
        if last:
            outs += [
                in_vmem((2, heads, size, size), jnp.bfloat16),
                in_vmem((heads + heads // 2, size, size), jnp.bfloat16),
            ]
            operands += states
            specs += [VMEM] * len(states)
        got = call(
            functools.partial(project_kernel, parts, heads, len(states) if last else 0),
            outs,
            operands,
            specs,
            16 * MIB,
            2 * chunk * parts * inputs.shape[1] * 3 * width,
        )
        qs.append(got[0])
        ks.append(got[1])
        vs.append(got[2])
        states.append(got[3])
        if last:
            totals, payload = got[4:]
    for c in range(CHUNKS):
        g = grad_out[c * chunk : (c + 1) * chunk]
        locals_ += call(
            functools.partial(local_kernel, heads),
            [in_vmem((4, chunk, width), jnp.float32)],
            [scale, qs[c], ks[c], vs[c], g],
            [SMEM] + [VMEM] * 4,
            16 * MIB,
            12 * chunk * chunk * width * 2,
        )
    near, levels, far = exchange(totals, payload, heads, odd, position)
    any_space = pl.BlockSpec(memory_space=pl.ANY)
    operands = [place, scale, coef, grads, near, *levels, far]
    operands += [*qs, *ks, *vs, *states, *locals_]
    return call(
        functools.partial(finish_kernel, CHUNKS, heads, depth),
        [jax.ShapeDtypeStruct((rows, width), jnp.bfloat16)] * 4,
        operands,
        [SMEM] * 3 + [VMEM] * (len(operands) - 3),
        16 * MIB,
        16 * rows * size * width,
        [
            pltpu.VMEM((4, rows, width), jnp.bfloat16),
            pltpu.VMEM((2, heads, size, size), jnp.float32),
            pltpu.SemaphoreType.DMA((4, CHUNKS)),
        ],
        [any_space] * 4,
    )


def solution(mesh):
    in_specs = (P("seq", "head"), P(None, None, "head"), P("head", None), P("seq", "head"))
    out_specs = (P("seq", "head"), P("seq", "head"), P("seq", "head"), P("seq", "head"))
    return jax.shard_map(
        per_device, mesh=mesh, in_specs=in_specs, out_specs=out_specs, check_vma=False
    )
```

```python
import functools
import math

import jax
import jax.numpy as jnp
from jax import lax
from jax.experimental import pallas as pl
from jax.experimental.pallas import tpu as pltpu
from jax.sharding import PartitionSpec as P

SHARES = (14, 15, 17, 18)
CHUNKS = len(SHARES)
MIB = 2**20
VMEM = pl.BlockSpec(memory_space=pltpu.VMEM)
SMEM = pl.BlockSpec(memory_space=pltpu.SMEM)
ANY = pl.BlockSpec(memory_space=pl.ANY)
HBM = pl.BlockSpec(memory_space=pltpu.HBM)
NN = (((1,), (0,)), ((), ()))
NT = (((1,), (1,)), ((), ()))
TN = (((0,), (0,)), ((), ()))
BF16 = jnp.bfloat16
F32 = jnp.float32


def dot(a, b, dims=NN):
    return lax.dot_general(a, b, dims, preferred_element_type=F32)


def swap(value, axis, mask):
    pairs = [(source, source ^ mask) for source in range(lax.axis_size(axis))]
    return lax.ppermute(value, axis, pairs)


def bit_of(position, bit):
    return lax.rem(position // 2**bit, 2) == 1


def call(kernel, outs, operands, specs, flops, scratch=(), out_specs=None, limit=4, moved=0):
    return pl.pallas_call(
        kernel,
        out_shape=outs,
        in_specs=specs,
        out_specs=[VMEM] * len(outs) if out_specs is None else out_specs,
        scratch_shapes=scratch,
        compiler_params=pltpu.CompilerParams(vmem_limit_bytes=limit * MIB),
        cost_estimate=pl.CostEstimate(flops=flops, bytes_accessed=moved, transcendentals=0),
    )(*operands)


def load_kernel(copied, *refs):
    count = 1 + max(source for source, _ in copied)
    sources, refs = refs[:count], refs[-len(copied) - 1 :]
    outs, sems = refs[:-1], refs[-1]
    copies = []
    for i, (source, start) in enumerate(copied):
        ref = sources[source]
        if start is not None:
            ref = ref.at[pl.ds(start, outs[i].shape[0])]
        copies.append(pltpu.make_async_copy(ref, outs[i], sems.at[i]))
    for copy in copies:
        copy.start()
    for copy in copies:
        copy.wait()


def load(sources, copied, after=()):
    shapes = []
    for source, span in copied:
        shape = sources[source].shape
        rows = shape[0] if span is None else span[1] - span[0]
        shapes.append(pltpu.VMEM((rows, *shape[1:]), BF16))
    copied = [(source, span if span is None else span[0]) for source, span in copied]
    return call(
        functools.partial(load_kernel, copied),
        shapes,
        [*[pltpu.with_memory_space_constraint(x, pltpu.HBM) for x in sources], *after],
        [HBM] * len(sources) + [ANY] * len(after),
        0,
        [pltpu.SemaphoreType.DMA((len(copied),))],
        limit=2,
        moved=4 * sum(math.prod(shape.shape) for shape in shapes),
    )


def tie_kernel(value_ref, *refs):
    del value_ref, refs


def tie(value, *after):
    return pl.pallas_call(
        tie_kernel,
        out_shape=pltpu.VMEM(value.shape, value.dtype),
        in_specs=[VMEM] + [ANY] * len(after),
        out_specs=VMEM,
        input_output_aliases={0: 0},
        compiler_params=pltpu.CompilerParams(vmem_limit_bytes=MIB),
    )(value, *after)


def project(w_ref, segments, j):
    me = lax.axis_index("head")
    parts = lax.axis_size("head")
    depth = w_ref.shape[1] // parts
    total = None
    for k, rows in segments:
        start = pl.multiple_of((me ^ k) * depth, depth)
        term = dot(rows, w_ref[j, pl.ds(start, depth), :])
        total = term if total is None else total + term
    return total


def read_segments(refs, keys, span):
    found = []
    for k, ref in zip(keys, refs):
        whole = ref.shape[0] != span[1] - span[0]
        found.append((k, ref[span[0] : span[1], :] if whole else ref[...]))
    return found


def early_kernel(keys, span, w_ref, *refs):
    segments, total_ref = refs[:-1], refs[-1]
    for j in range(3):
        total_ref[j] = project(w_ref, read_segments(segments, keys, span), j)


def project_kernel(keys, span, heads, w_ref, g_ref, *refs):
    segments, refs = refs[: len(keys)], refs[len(keys) :]
    q_ref, k_ref, v_ref, state_ref = refs[-4:]
    for j, out_ref in enumerate((q_ref, k_ref, v_ref)):
        out_ref[...] = project(w_ref, read_segments(segments, keys, span), j).astype(BF16)
    size = q_ref.shape[1] // heads
    for h in range(heads):
        cols = slice(h * size, (h + 1) * size)
        state_ref[0, h] = dot(k_ref[:, cols], v_ref[:, cols], TN)
        state_ref[1, h] = dot(q_ref[:, cols], g_ref[span[0] : span[1], cols], TN)


def last_kernel(keys, span, heads, w_ref, g_ref, part_ref, *refs):
    segments, refs = refs[: len(keys)], refs[len(keys) :]
    earlier, refs = refs[:-6], refs[-6:]
    q_ref, k_ref, v_ref, state_ref, total_ref, payload_ref = refs
    for j, out_ref in enumerate((q_ref, k_ref, v_ref)):
        term = project(w_ref, read_segments(segments, keys, span), j)
        out_ref[...] = (part_ref[j] + term).astype(BF16)
    size = q_ref.shape[1] // heads
    half = heads // 2
    odd = bit_of(lax.axis_index("seq"), 0)
    for h in range(heads):
        cols = slice(h * size, (h + 1) * size)
        state_ref[0, h] = dot(k_ref[:, cols], v_ref[:, cols], TN)
        state_ref[1, h] = dot(q_ref[:, cols], g_ref[span[0] : span[1], cols], TN)
        for s in range(2):
            total = state_ref[s, h]
            for other in earlier:
                total = total + other[s, h]
            total_ref[s, h] = total
    for h in range(heads):
        payload_ref[h] = jnp.where(odd, total_ref[1, h], total_ref[0, h]).astype(BF16)
    for h in range(half):
        value = jnp.where(odd, total_ref[0, h], total_ref[1, half + h])
        payload_ref[heads + h] = value.astype(BF16)


def local_kernel(span, heads, weight_ref, q_ref, k_ref, v_ref, g_ref, after_ref, out_ref):
    rows = q_ref.shape[0]
    size = q_ref.shape[1] // heads
    norm = 1.0 / math.sqrt(size * g_ref.shape[0])
    at = lax.broadcasted_iota(jnp.int32, (rows, rows), 0)
    of = lax.broadcasted_iota(jnp.int32, (rows, rows), 1)
    causal = at >= of
    for h in range(heads):
        cols = slice(h * size, (h + 1) * size)
        q, k, v = q_ref[:, cols], k_ref[:, cols], v_ref[:, cols]
        g = g_ref[span[0] : span[1], cols]
        scale = weight_ref[h, 0] * norm
        attend = jnp.where(causal, dot(q, k, NT) * scale, 0.0).astype(BF16)
        grad = jnp.where(causal, dot(g, v, NT) * scale, 0.0).astype(BF16)
        out_ref[0, :, cols] = dot(attend, v)
        out_ref[1, :, cols] = dot(grad, k)
        out_ref[2, :, cols] = dot(grad, q, TN)
        out_ref[3, :, cols] = dot(attend, g, TN)


def write_payloads(sums, outs, bit, final):
    position = lax.axis_index("seq")
    for top, out in enumerate(outs):
        for e in range(len(sums[0])):
            if final:
                out[e] = jnp.where(bit_of(position, bit + top), sums[1][e], sums[0][e]).astype(BF16)
            else:
                out[0, e] = sums[0][e].astype(BF16)
                out[1, e] = sums[1][e].astype(BF16)


def pair_kernel(heads, final, total_ref, got_ref, sum_ref, *outs):
    half = heads // 2
    odd = bit_of(lax.axis_index("seq"), 0)
    sums = [[], []]
    for e in range(half):
        near = jnp.where(odd, got_ref[half + e], got_ref[e]).astype(F32)
        rest = got_ref[heads + e].astype(F32)
        for s in range(2):
            mine = jnp.where(odd, total_ref[s, half + e], total_ref[s, e])
            theirs = jnp.where(odd, near, rest) if s == 0 else jnp.where(odd, rest, near)
            value = mine + theirs
            sums[s].append(value)
            if not final:
                sum_ref[s, e] = value
    if final:
        sum_ref[...] = jnp.zeros_like(sum_ref)
    write_payloads(sums, outs, 1, final)


def group_kernel(bit, count, masks, final, next_final, *refs):
    position = lax.axis_index("seq")
    got = dict(zip(masks, refs[: len(masks)]))
    refs = refs[len(masks) :]
    if final:
        (level_ref,) = refs
        half = level_ref.shape[1]
        for top in range(count):
            for e in range(half):
                value = None
                for m in masks:
                    if m.bit_length() - 1 == top:
                        term = got[m][e].astype(F32)
                        value = term if value is None else value + term
                level_ref[top, e] = value.astype(BF16)
        return
    sum_ref, level_ref, next_ref, *outs = refs
    half = level_ref.shape[1]
    sums = [[], []]
    for e in range(half):
        total = [sum_ref[s, e] for s in range(2)]
        levels = [None] * count
        for m in masks:
            both = [got[m][s, e].astype(F32) for s in range(2)]
            total = [total[s] + both[s] for s in range(2)]
            top = m.bit_length() - 1
            term = jnp.where(bit_of(position, bit + top), both[0], both[1])
            levels[top] = term if levels[top] is None else levels[top] + term
        for top in range(count):
            level_ref[top, e] = levels[top].astype(BF16)
        for s in range(2):
            next_ref[s, e] = total[s]
            sums[s].append(total[s])
    write_payloads(sums, outs, bit + count, next_final)


def finish_kernel(spans, heads, groups, weight_ref, g_ref, near_ref, *refs):
    chunks = len(spans)
    own, refs = refs[:groups], refs[groups:]
    far, refs = refs[:groups], refs[groups:]
    q_refs, refs = refs[:chunks], refs[chunks:]
    k_refs, refs = refs[:chunks], refs[chunks:]
    v_refs, refs = refs[:chunks], refs[chunks:]
    state_refs, refs = refs[:chunks], refs[chunks:]
    part_refs, refs = refs[:chunks], refs[chunks:]
    outs, (held, mix_ref, sems) = refs[:4], refs[4:]
    position = lax.axis_index("seq")
    odd = bit_of(position, 0)
    size = q_refs[0].shape[1] // heads
    half = heads // 2
    block = g_ref.shape[0]
    norm = 1.0 / math.sqrt(size * block)
    for h in range(heads):
        values = [near_ref[h].astype(F32)]
        for mine_ref, other_ref in zip(own, far):
            for top in range(mine_ref.shape[0]):
                mine = mine_ref[top, h % half].astype(F32)
                other = other_ref[top, h % half].astype(F32)
                is_mine = odd if h // half == 1 else jnp.logical_not(odd)
                values.append(jnp.where(is_mine, mine, other))
        forward = backward = None
        for level, value in enumerate(values):
            coef = weight_ref[h, level + 1] * (1.0 / math.sqrt(size * block * 2**level))
            on = bit_of(position, level)
            to_forward = jnp.where(on, coef, 0.0) * value
            to_backward = jnp.where(on, 0.0, coef) * value
            forward = to_forward if forward is None else forward + to_forward
            backward = to_backward if backward is None else backward + to_backward
        mix_ref[0, h] = forward
        mix_ref[1, h] = backward
    zero = jnp.zeros((size, size), BF16)
    copies = []
    for c in range(chunks):
        span = slice(*spans[c])
        for h in range(0, heads, 2):
            cols = slice(h * size, (h + 2) * size)
            blocks = []
            for s in range(2):
                pair = []
                for e in (h, h + 1):
                    value = None
                    for other in range(c) if s == 0 else range(c + 1, chunks):
                        term = state_refs[other][s, e]
                        value = term if value is None else value + term
                    mix = mix_ref[s, e]
                    if value is not None:
                        mix = mix + (weight_ref[e, 0] * norm) * value
                    pair.append(mix.astype(BF16))
                top = jnp.concatenate([pair[0], zero], axis=1)
                bottom = jnp.concatenate([zero, pair[1]], axis=1)
                blocks.append(jnp.concatenate([top, bottom], axis=0))
            forward, backward = blocks
            terms = (
                dot(q_refs[c][:, cols], forward),
                dot(g_ref[span, cols], forward, NT),
                dot(v_refs[c][:, cols], backward, NT),
                dot(k_refs[c][:, cols], backward),
            )
            for j in range(4):
                held[j, span, cols] = (terms[j] + part_refs[c][j, :, cols]).astype(BF16)
        for j in range(4):
            copy = pltpu.make_async_copy(held.at[j, span], outs[j].at[span], sems.at[j, c])
            copy.start()
            copies.append(copy)
    for copy in copies:
        copy.wait()


def exchange(totals, payload, heads):
    depth = lax.axis_size("seq").bit_length() - 1
    half = heads // 2
    square = payload.shape[1:]
    groups = [(bit, min(2, depth - bit)) for bit in range(1, depth, 2)]
    finals = [bit + count >= depth for bit, count in groups]

    def payloads(index):
        count = groups[index][1]
        if finals[index]:
            return [pltpu.VMEM((half, *square), BF16)] * count
        return [pltpu.VMEM((2, half, *square), BF16)]

    near = swap(payload, "seq", 1)
    sum_shape = (1, 8, 128) if finals[0] else (2, half, *square)
    sums, *sends = call(
        functools.partial(pair_kernel, heads, finals[0]),
        [pltpu.VMEM(sum_shape, F32), *payloads(0)],
        [totals, near],
        [VMEM] * 2,
        10**6,
    )
    own, far = [], []
    for index, (bit, count) in enumerate(groups):
        final = finals[index]
        masks = sorted(range(1, 2**count), reverse=True)
        got = [
            swap(sends[m.bit_length() - 1] if final else sends[0], "seq", m << bit) for m in masks
        ]
        level = pltpu.VMEM((count, half, *square), BF16)
        if final:
            next_final, outs, operands = True, [level], got
        else:
            next_final = finals[index + 1]
            next_shape = pltpu.VMEM((2, half, *square), F32)
            outs = [level, next_shape, *payloads(index + 1)]
            operands = [*got, sums]
        found, *more = call(
            functools.partial(group_kernel, bit, count, masks, final, next_final),
            outs,
            operands,
            [VMEM] * len(operands),
            10**6,
        )
        if not final:
            sums, *sends = more
        own.append(found)
        far.append(swap(found, "seq", 1))
    return near, own, far


def per_device(inputs, w_qkv, level_weight, grad_out):
    rows, width = grad_out.shape
    heads = level_weight.shape[0]
    size = width // heads
    parts = lax.axis_size("head")
    edges = [rows * sum(SHARES[:c]) // sum(SHARES) for c in range(CHUNKS + 1)]
    spans = list(zip(edges[:-1], edges[1:]))
    copied = [(0, span) for span in spans]
    mine = load([inputs], copied[:1])
    mine += load([inputs], copied[1:], mine)
    grads, weights = load([grad_out, w_qkv], [(0, None), (1, None)], mine[1:2])
    top, *lows = [1 << b for b in reversed(range(parts.bit_length() - 1))]
    arrived = [swap(piece, "head", top) for piece in mine]
    arrived[0] = tie(arrived[0], weights)
    whole = {0: inputs}
    for low in lows:
        for k in sorted(whole):
            whole[k | low] = swap(whole[k], "head", low)
    state = pltpu.VMEM((2, heads, size, size), F32)
    qs, ks, vs, states, locals_ = [], [], [], [], []

    def local(c, after):
        chunk = spans[c][1] - spans[c][0]
        return call(
            functools.partial(local_kernel, spans[c], heads),
            [pltpu.VMEM((4, chunk, width), F32)],
            [level_weight, qs[c], ks[c], vs[c], grads, after],
            [SMEM] + [VMEM] * 4 + [ANY],
            24 * chunk * chunk * width if c >= CHUNKS - 2 else 0,
        )[0]

    after = None
    for c in range(CHUNKS):
        pieces = {**whole, 0: mine[c]}
        pieces[top] = arrived[c] if after is None else tie(arrived[c], after)
        for low in lows:
            for k in [k for k in sorted(pieces) if k & top]:
                pieces[k | low] = swap(pieces[k], "head", low)
        keys = sorted(pieces)
        chunk = spans[c][1] - spans[c][0]
        flat = pltpu.VMEM((chunk, width), BF16)
        flops = 0
        if c < CHUNKS - 1:
            if c > 0:
                locals_.append(local(c - 1, pieces[top]))
            operands = [weights, grads, *[pieces[k] for k in keys], *locals_[-1:]]
            got = call(
                functools.partial(project_kernel, keys, spans[c], heads),
                [flat, flat, flat, state],
                operands,
                [VMEM] * (2 + len(keys)) + [ANY] * len(locals_[-1:]),
                flops * len(keys),
            )
        else:
            early, late = keys[:-1], keys[-1:]
            (begun,) = call(
                functools.partial(early_kernel, early, spans[c]),
                [pltpu.VMEM((3, chunk, width), F32)],
                [weights, *[pieces[k] for k in early]],
                [VMEM] * (1 + len(early)),
                flops * len(early),
            )
            operands = [weights, grads, begun, *[pieces[k] for k in late], *states]
            *got, totals, payload = call(
                functools.partial(last_kernel, late, spans[c], heads),
                [
                    flat,
                    flat,
                    flat,
                    state,
                    state,
                    pltpu.VMEM((heads + heads // 2, size, size), BF16),
                ],
                operands,
                [VMEM] * len(operands),
                flops * len(late),
            )
        qs.append(got[0])
        ks.append(got[1])
        vs.append(got[2])
        states.append(got[3])
        after = got[3]
    for c in range(len(locals_), CHUNKS):
        locals_.append(local(c, payload))
    near, own, far = exchange(totals, payload, heads)
    operands = [level_weight, grads, near, *own, *far, *qs, *ks, *vs, *states, *locals_]
    return call(
        functools.partial(finish_kernel, spans, heads, len(own)),
        [jax.ShapeDtypeStruct((rows, width), BF16)] * 4,
        operands,
        [SMEM] + [VMEM] * (len(operands) - 1),
        16 * rows * size * width,
        [
            pltpu.VMEM((4, rows, width), BF16),
            pltpu.VMEM((2, heads, size, size), F32),
            pltpu.SemaphoreType.DMA((4, CHUNKS)),
        ],
        [ANY] * 4,
        12,
    )


def solution(mesh):
    in_specs = (P("seq", "head"), P(None, None, "head"), P("head", None), P("seq", "head"))
    out_specs = (P("seq", "head"), P("seq", "head"), P("seq", "head"), P("seq", "head"))
    return jax.shard_map(
        per_device, mesh=mesh, in_specs=in_specs, out_specs=out_specs, check_vma=False
    )
```

```python
import functools
import math

import jax
import jax.numpy as jnp
from jax import lax
from jax.experimental import pallas as pl
from jax.experimental.pallas import tpu as pltpu
from jax.sharding import PartitionSpec as P

SHARES = (14, 15, 17, 18)
CHUNKS = len(SHARES)
GROUP = 4
MIB = 2**20
VMEM = pl.BlockSpec(memory_space=pltpu.VMEM)
SMEM = pl.BlockSpec(memory_space=pltpu.SMEM)
ANY = pl.BlockSpec(memory_space=pl.ANY)
HBM = pl.BlockSpec(memory_space=pltpu.HBM)
NN = (((1,), (0,)), ((), ()))
NT = (((1,), (1,)), ((), ()))
TN = (((0,), (0,)), ((), ()))
BF16 = jnp.bfloat16
F32 = jnp.float32


def dot(a, b, dims=NN):
    return lax.dot_general(a, b, dims, preferred_element_type=F32)


def swap(value, axis, mask):
    pairs = [(source, source ^ mask) for source in range(lax.axis_size(axis))]
    return lax.ppermute(value, axis, pairs)


def bit_of(position, bit):
    return lax.rem(position // 2**bit, 2) == 1


def call(kernel, outs, operands, specs, flops, scratch=(), out_specs=None, limit=4, moved=0):
    return pl.pallas_call(
        kernel,
        out_shape=outs,
        in_specs=specs,
        out_specs=[VMEM] * len(outs) if out_specs is None else out_specs,
        scratch_shapes=scratch,
        compiler_params=pltpu.CompilerParams(vmem_limit_bytes=limit * MIB),
        cost_estimate=pl.CostEstimate(flops=flops, bytes_accessed=moved, transcendentals=0),
    )(*operands)


def load_kernel(copied, *refs):
    count = 1 + max(source for source, _ in copied)
    sources, refs = refs[:count], refs[-len(copied) - 1 :]
    outs, sems = refs[:-1], refs[-1]
    copies = []
    for i, (source, start) in enumerate(copied):
        ref = sources[source]
        if start is not None:
            ref = ref.at[pl.ds(start, outs[i].shape[0])]
        copies.append(pltpu.make_async_copy(ref, outs[i], sems.at[i]))
    for copy in copies:
        copy.start()
    for copy in copies:
        copy.wait()


def load(sources, copied, after=()):
    shapes = []
    for source, span in copied:
        shape = sources[source].shape
        rows = shape[0] if span is None else span[1] - span[0]
        shapes.append(pltpu.VMEM((rows, *shape[1:]), BF16))
    copied = [(source, span if span is None else span[0]) for source, span in copied]
    return call(
        functools.partial(load_kernel, copied),
        shapes,
        [*[pltpu.with_memory_space_constraint(x, pltpu.HBM) for x in sources], *after],
        [HBM] * len(sources) + [ANY] * len(after),
        0,
        [pltpu.SemaphoreType.DMA((len(copied),))],
        limit=2,
        moved=4 * sum(math.prod(shape.shape) for shape in shapes),
    )


def tie_kernel(value_ref, *refs):
    del value_ref, refs


def tie(value, *after):
    return pl.pallas_call(
        tie_kernel,
        out_shape=pltpu.VMEM(value.shape, value.dtype),
        in_specs=[VMEM] + [ANY] * len(after),
        out_specs=VMEM,
        input_output_aliases={0: 0},
        compiler_params=pltpu.CompilerParams(vmem_limit_bytes=MIB),
    )(value, *after)


def project(w_ref, segments, j):
    me = lax.axis_index("head")
    parts = lax.axis_size("head")
    depth = w_ref.shape[1] // parts
    total = None
    for k, rows in segments:
        start = pl.multiple_of((me ^ k) * depth, depth)
        term = dot(rows, w_ref[j, pl.ds(start, depth), :])
        total = term if total is None else total + term
    return total


def read_segments(refs, keys, span):
    found = []
    for k, ref in zip(keys, refs):
        whole = ref.shape[0] != span[1] - span[0]
        found.append((k, ref[span[0] : span[1], :] if whole else ref[...]))
    return found


def early_kernel(keys, span, w_ref, *refs):
    segments, total_ref = refs[:-1], refs[-1]
    for j in range(3):
        total_ref[j] = project(w_ref, read_segments(segments, keys, span), j)


def project_kernel(keys, span, heads, w_ref, g_ref, *refs):
    segments, refs = refs[: len(keys)], refs[len(keys) :]
    q_ref, k_ref, v_ref, state_ref = refs[-4:]
    for j, out_ref in enumerate((q_ref, k_ref, v_ref)):
        out_ref[...] = project(w_ref, read_segments(segments, keys, span), j).astype(BF16)
    size = q_ref.shape[1] // heads
    for h in range(heads):
        cols = slice(h * size, (h + 1) * size)
        state_ref[0, h] = dot(k_ref[:, cols], v_ref[:, cols], TN)
        state_ref[1, h] = dot(q_ref[:, cols], g_ref[span[0] : span[1], cols], TN)


def last_kernel(keys, span, heads, w_ref, g_ref, part_ref, *refs):
    segments, refs = refs[: len(keys)], refs[len(keys) :]
    earlier, refs = refs[: -5 - (GROUP - 1)], refs[-5 - (GROUP - 1) :]
    q_ref, k_ref, v_ref, state_ref, total_ref, *sends = refs
    for j, out_ref in enumerate((q_ref, k_ref, v_ref)):
        term = project(w_ref, read_segments(segments, keys, span), j)
        out_ref[...] = (part_ref[j] + term).astype(BF16)
    size = q_ref.shape[1] // heads
    share = heads // GROUP
    place = lax.rem(lax.axis_index("seq"), GROUP)
    for h in range(heads):
        cols = slice(h * size, (h + 1) * size)
        state_ref[0, h] = dot(k_ref[:, cols], v_ref[:, cols], TN)
        state_ref[1, h] = dot(q_ref[:, cols], g_ref[span[0] : span[1], cols], TN)
        for s in range(2):
            total = state_ref[s, h]
            for other in earlier:
                total = total + other[s, h]
            total_ref[s, h] = total
    for m, send in enumerate(sends, 1):
        for s in range(2):
            for e in range(share):
                send[s, e] = total_ref[s, (place ^ m) * share + e].astype(BF16)


def local_kernel(span, heads, weight_ref, q_ref, k_ref, v_ref, g_ref, after_ref, out_ref):
    rows = q_ref.shape[0]
    size = q_ref.shape[1] // heads
    norm = 1.0 / math.sqrt(size * g_ref.shape[0])
    at = lax.broadcasted_iota(jnp.int32, (rows, rows), 0)
    of = lax.broadcasted_iota(jnp.int32, (rows, rows), 1)
    causal = at >= of
    for h in range(heads):
        cols = slice(h * size, (h + 1) * size)
        q, k, v = q_ref[:, cols], k_ref[:, cols], v_ref[:, cols]
        g = g_ref[span[0] : span[1], cols]
        scale = weight_ref[h, 0] * norm
        attend = jnp.where(causal, dot(q, k, NT) * scale, 0.0).astype(BF16)
        grad = jnp.where(causal, dot(g, v, NT) * scale, 0.0).astype(BF16)
        out_ref[0, :, cols] = dot(attend, v)
        out_ref[1, :, cols] = dot(grad, k)
        out_ref[2, :, cols] = dot(grad, q, TN)
        out_ref[3, :, cols] = dot(attend, g, TN)


def owner_kernel(final, total_ref, *refs):
    got, (near_ref, level_ref, sum_ref, next_ref) = refs[: GROUP - 1], refs[-4:]
    position = lax.axis_index("seq")
    place = lax.rem(position, GROUP)
    heads = total_ref.shape[1]
    share = heads // GROUP
    odd, high = bit_of(position, 0), bit_of(position, 1)
    for h in range(heads):
        near_ref[h] = jnp.where(odd, total_ref[1, h], total_ref[0, h]).astype(BF16)
    for e in range(share):
        mine, other = [], []
        for s in range(2):
            mine.append(total_ref[s, place * share + e] + got[0][s, e].astype(F32))
            other.append(got[1][s, e].astype(F32) + got[2][s, e].astype(F32))
        level_ref[0, e] = jnp.where(high, other[0], other[1]).astype(BF16)
        level_ref[1, e] = jnp.where(high, mine[1], mine[0]).astype(BF16)
        sums = [mine[s] + other[s] for s in range(2)]
        write_next(sums, e, 2, final, sum_ref, next_ref)


def write_next(sums, e, bit, final, sum_ref, next_ref):
    if final:
        value = jnp.where(bit_of(lax.axis_index("seq"), bit), sums[1], sums[0])
        next_ref[0, e] = value.astype(BF16)
        return
    for s in range(2):
        sum_ref[s, e] = sums[s]
        next_ref[s, e] = sums[s].astype(BF16)


def climb_kernel(bit, next_final, got_ref, old_ref, level_ref, sum_ref, next_ref):
    on = bit_of(lax.axis_index("seq"), bit)
    for e in range(got_ref.shape[1]):
        both = [got_ref[s, e].astype(F32) for s in range(2)]
        level_ref[e] = jnp.where(on, both[0], both[1]).astype(BF16)
        sums = [old_ref[s, e] + both[s] for s in range(2)]
        write_next(sums, e, bit + 1, next_final, sum_ref, next_ref)


def return_kernel(level_ref, last_ref, *refs):
    between, (near_ref, far_ref) = refs[:-2], refs[-2:]
    for index, out_ref in enumerate((near_ref, far_ref)):
        out_ref[0] = level_ref[index]
        for b, ref in enumerate(between, 1):
            out_ref[b] = ref[...]
        out_ref[len(between) + 1] = last_ref[0]


def finish_kernel(spans, heads, weight_ref, g_ref, near_ref, *refs):
    chunks = len(spans)
    levels, refs = refs[:GROUP], refs[GROUP:]
    q_refs, refs = refs[:chunks], refs[chunks:]
    k_refs, refs = refs[:chunks], refs[chunks:]
    v_refs, refs = refs[:chunks], refs[chunks:]
    state_refs, refs = refs[:chunks], refs[chunks:]
    part_refs, refs = refs[:chunks], refs[chunks:]
    outs, (held, mix_ref, sems) = refs[:4], refs[4:]
    position = lax.axis_index("seq")
    place = lax.rem(position, GROUP)
    size = q_refs[0].shape[1] // heads
    share = heads // GROUP
    block = g_ref.shape[0]
    norm = 1.0 / math.sqrt(size * block)
    for m in range(GROUP):
        for e in range(share):
            h = (place ^ m) * share + e
            values = [near_ref[h]] + [levels[m][b, e] for b in range(levels[m].shape[0])]
            forward = backward = None
            for level, value in enumerate(values):
                coef = weight_ref[h, level + 1] * (1.0 / math.sqrt(size * block * 2**level))
                on = bit_of(position, level)
                value = value.astype(F32)
                to_forward = jnp.where(on, coef, 0.0) * value
                to_backward = jnp.where(on, 0.0, coef) * value
                forward = to_forward if forward is None else forward + to_forward
                backward = to_backward if backward is None else backward + to_backward
            mix_ref[0, h] = forward
            mix_ref[1, h] = backward
    zero = jnp.zeros((size, size), BF16)
    copies = []
    for c in range(chunks):
        span = slice(*spans[c])
        for h in range(0, heads, 2):
            cols = slice(h * size, (h + 2) * size)
            blocks = []
            for s in range(2):
                pair = []
                for e in (h, h + 1):
                    value = None
                    for other in range(c) if s == 0 else range(c + 1, chunks):
                        term = state_refs[other][s, e]
                        value = term if value is None else value + term
                    mix = mix_ref[s, e]
                    if value is not None:
                        mix = mix + (weight_ref[e, 0] * norm) * value
                    pair.append(mix.astype(BF16))
                top = jnp.concatenate([pair[0], zero], axis=1)
                bottom = jnp.concatenate([zero, pair[1]], axis=1)
                blocks.append(jnp.concatenate([top, bottom], axis=0))
            forward, backward = blocks
            terms = (
                dot(q_refs[c][:, cols], forward),
                dot(g_ref[span, cols], forward, NT),
                dot(v_refs[c][:, cols], backward, NT),
                dot(k_refs[c][:, cols], backward),
            )
            for j in range(4):
                held[j, span, cols] = (terms[j] + part_refs[c][j, :, cols]).astype(BF16)
        for j in range(4):
            copy = pltpu.make_async_copy(held.at[j, span], outs[j].at[span], sems.at[j, c])
            copy.start()
            copies.append(copy)
    for copy in copies:
        copy.wait()


def exchange(totals, sends, local, late):
    depth = lax.axis_size("seq").bit_length() - 1
    heads, square = totals.shape[1], totals.shape[2:]
    share = heads // GROUP
    last = depth - 1

    def message(bit):
        return pltpu.VMEM((1 if bit == last else 2, share, *square), BF16)

    def running(bit):
        return pltpu.VMEM((1, 8, 128) if bit == last else (2, share, *square), F32)

    got = [swap(send, "seq", m) for m, send in enumerate(sends, 1)]
    filler = local(late[0], sends[0])
    near, levels, sums, sent = call(
        functools.partial(owner_kernel, last == 2),
        [
            pltpu.VMEM((heads, *square), BF16),
            pltpu.VMEM((2, share, *square), BF16),
            running(2),
            message(2),
        ],
        [totals, *got, filler],
        [VMEM] * GROUP + [ANY],
        10**6,
    )
    fillers = [filler] + [local(c, sent) for c in late[1:]]
    between = []
    for bit in range(2, last):
        found, sums, sent = call(
            functools.partial(climb_kernel, bit, bit + 1 == last),
            [pltpu.VMEM((share, *square), BF16), running(bit + 1), message(bit + 1)],
            [swap(sent, "seq", 1 << bit), sums],
            [VMEM] * 2,
            10**6,
        )
        between.append(found)
    operands = [levels, swap(sent, "seq", 1 << last), *between]
    outs = [pltpu.VMEM((depth - 1, share, *square), BF16)] * 2
    mine, other = call(
        return_kernel_with(len(operands)),
        outs,
        [*operands, *fillers[1:]],
        [VMEM] * len(operands) + [ANY] * len(fillers[1:]),
        10**6,
    )
    near = swap(near, "seq", 1)
    returned = [swap(mine if m == 1 else other, "seq", m) for m in range(1, GROUP)]
    return near, [mine, *returned], fillers


def return_kernel_with(count):
    def kernel(*refs):
        return_kernel(*refs[:count], *refs[-2:])

    return kernel


def per_device(inputs, w_qkv, level_weight, grad_out):
    rows, width = grad_out.shape
    heads = level_weight.shape[0]
    size = width // heads
    parts = lax.axis_size("head")
    edges = [rows * sum(SHARES[:c]) // sum(SHARES) for c in range(CHUNKS + 1)]
    spans = list(zip(edges[:-1], edges[1:]))
    copied = [(0, span) for span in spans]
    mine = load([inputs], copied[:1])
    mine += load([inputs], copied[1:], mine)
    grads, weights = load([grad_out, w_qkv], [(0, None), (1, None)], mine[1:2])
    top, *lows = [1 << b for b in reversed(range(parts.bit_length() - 1))]
    arrived = [swap(piece, "head", top) for piece in mine]
    arrived[0] = tie(arrived[0], weights)
    whole = {0: inputs}
    for low in lows:
        for k in sorted(whole):
            whole[k | low] = swap(whole[k], "head", low)
    state = pltpu.VMEM((2, heads, size, size), F32)
    qs, ks, vs, states, locals_ = [], [], [], [], []

    def local(c, after):
        chunk = spans[c][1] - spans[c][0]
        return call(
            functools.partial(local_kernel, spans[c], heads),
            [pltpu.VMEM((4, chunk, width), F32)],
            [level_weight, qs[c], ks[c], vs[c], grads, after],
            [SMEM] + [VMEM] * 4 + [ANY],
            24 * chunk * chunk * width if c >= CHUNKS - 2 else 0,
        )[0]

    after = None
    for c in range(CHUNKS):
        pieces = {**whole, 0: mine[c]}
        pieces[top] = arrived[c] if after is None else tie(arrived[c], after)
        for low in lows:
            for k in [k for k in sorted(pieces) if k & top]:
                pieces[k | low] = swap(pieces[k], "head", low)
        keys = sorted(pieces)
        chunk = spans[c][1] - spans[c][0]
        flat = pltpu.VMEM((chunk, width), BF16)
        flops = 0
        if c < CHUNKS - 1:
            if c > 0:
                locals_.append(local(c - 1, pieces[top]))
            operands = [weights, grads, *[pieces[k] for k in keys], *locals_[-1:]]
            got = call(
                functools.partial(project_kernel, keys, spans[c], heads),
                [flat, flat, flat, state],
                operands,
                [VMEM] * (2 + len(keys)) + [ANY] * len(locals_[-1:]),
                flops * len(keys),
            )
        else:
            early, late = keys[:-1], keys[-1:]
            (begun,) = call(
                functools.partial(early_kernel, early, spans[c]),
                [pltpu.VMEM((3, chunk, width), F32)],
                [weights, *[pieces[k] for k in early]],
                [VMEM] * (1 + len(early)),
                flops * len(early),
            )
            operands = [weights, grads, begun, *[pieces[k] for k in late], *states]
            got = call(
                functools.partial(last_kernel, late, spans[c], heads),
                [
                    flat,
                    flat,
                    flat,
                    state,
                    state,
                    *[pltpu.VMEM((2, heads // GROUP, size, size), BF16)] * (GROUP - 1),
                ],
                operands,
                [VMEM] * len(operands),
                flops * len(late),
            )
        qs.append(got[0])
        ks.append(got[1])
        vs.append(got[2])
        states.append(got[3])
        after = got[3]
    near, levels, fillers = exchange(got[4], got[5:], local, range(len(locals_), CHUNKS))
    locals_ += fillers
    operands = [level_weight, grads, near, *levels, *qs, *ks, *vs, *states, *locals_]
    return call(
        functools.partial(finish_kernel, spans, heads),
        [jax.ShapeDtypeStruct((rows, width), BF16)] * 4,
        operands,
        [SMEM] + [VMEM] * (len(operands) - 1),
        16 * rows * size * width,
        [
            pltpu.VMEM((4, rows, width), BF16),
            pltpu.VMEM((2, heads, size, size), F32),
            pltpu.SemaphoreType.DMA((4, CHUNKS)),
        ],
        [ANY] * 4,
        12,
    )


def solution(mesh):
    in_specs = (P("seq", "head"), P(None, None, "head"), P("head", None), P("seq", "head"))
    out_specs = (P("seq", "head"), P("seq", "head"), P("seq", "head"), P("seq", "head"))
    return jax.shard_map(
        per_device, mesh=mesh, in_specs=in_specs, out_specs=out_specs, check_vma=False
    )
```

```python
import functools
import math

import jax
import jax.numpy as jnp
from jax import lax
from jax.experimental import pallas as pl
from jax.experimental.pallas import tpu as pltpu
from jax.sharding import PartitionSpec as P

SHARES = (14, 15, 17, 18)
CHUNKS = len(SHARES)
GROUP = 4
MIB = 2**20
VMEM = pl.BlockSpec(memory_space=pltpu.VMEM)
SMEM = pl.BlockSpec(memory_space=pltpu.SMEM)
ANY = pl.BlockSpec(memory_space=pl.ANY)
HBM = pl.BlockSpec(memory_space=pltpu.HBM)
NN = (((1,), (0,)), ((), ()))
NT = (((1,), (1,)), ((), ()))
TN = (((0,), (0,)), ((), ()))
BF16 = jnp.bfloat16
F32 = jnp.float32


def dot(a, b, dims=NN):
    return lax.dot_general(a, b, dims, preferred_element_type=F32)


def swap(value, axis, mask):
    pairs = [(source, source ^ mask) for source in range(lax.axis_size(axis))]
    return lax.ppermute(value, axis, pairs)


def trade(value, axis):
    count = lax.axis_size(axis)
    groups = [list(range(first, first + GROUP)) for first in range(0, count, GROUP)]
    return lax.all_to_all(value, axis, 0, 0, axis_index_groups=groups, tiled=True)


def bit_of(position, bit):
    return lax.rem(position // 2**bit, 2) == 1


def call(kernel, outs, operands, specs, flops, scratch=(), out_specs=None, limit=4, moved=0):
    return pl.pallas_call(
        kernel,
        out_shape=outs,
        in_specs=specs,
        out_specs=[VMEM] * len(outs) if out_specs is None else out_specs,
        scratch_shapes=scratch,
        compiler_params=pltpu.CompilerParams(vmem_limit_bytes=limit * MIB),
        cost_estimate=pl.CostEstimate(flops=flops, bytes_accessed=moved, transcendentals=0),
    )(*operands)


def load_kernel(copied, *refs):
    count = 1 + max(source for source, _ in copied)
    sources, refs = refs[:count], refs[-len(copied) - 1 :]
    outs, sems = refs[:-1], refs[-1]
    copies = []
    for i, (source, start) in enumerate(copied):
        ref = sources[source]
        if start is not None:
            ref = ref.at[pl.ds(start, outs[i].shape[0])]
        copies.append(pltpu.make_async_copy(ref, outs[i], sems.at[i]))
    for copy in copies:
        copy.start()
    for copy in copies:
        copy.wait()


def load(sources, copied, after=()):
    shapes = []
    for source, span in copied:
        shape = sources[source].shape
        rows = shape[0] if span is None else span[1] - span[0]
        shapes.append(pltpu.VMEM((rows, *shape[1:]), BF16))
    copied = [(source, span if span is None else span[0]) for source, span in copied]
    return call(
        functools.partial(load_kernel, copied),
        shapes,
        [*[pltpu.with_memory_space_constraint(x, pltpu.HBM) for x in sources], *after],
        [HBM] * len(sources) + [ANY] * len(after),
        0,
        [pltpu.SemaphoreType.DMA((len(copied),))],
        limit=2,
        moved=4 * sum(math.prod(shape.shape) for shape in shapes),
    )


def tie_kernel(value_ref, *refs):
    del value_ref, refs


def tie(value, *after):
    return pl.pallas_call(
        tie_kernel,
        out_shape=pltpu.VMEM(value.shape, value.dtype),
        in_specs=[VMEM] + [ANY] * len(after),
        out_specs=VMEM,
        input_output_aliases={0: 0},
        compiler_params=pltpu.CompilerParams(vmem_limit_bytes=MIB),
    )(value, *after)


def project(w_ref, segments, j):
    me = lax.axis_index("head")
    parts = lax.axis_size("head")
    depth = w_ref.shape[1] // parts
    total = None
    for k, rows in segments:
        start = pl.multiple_of((me ^ k) * depth, depth)
        term = dot(rows, w_ref[j, pl.ds(start, depth), :])
        total = term if total is None else total + term
    return total


def read_segments(refs, keys, span):
    found = []
    for k, ref in zip(keys, refs):
        whole = ref.shape[0] != span[1] - span[0]
        found.append((k, ref[span[0] : span[1], :] if whole else ref[...]))
    return found


def early_kernel(keys, span, w_ref, *refs):
    segments, total_ref = refs[:-1], refs[-1]
    for j in range(3):
        total_ref[j] = project(w_ref, read_segments(segments, keys, span), j)


def project_kernel(keys, span, heads, w_ref, g_ref, *refs):
    segments, refs = refs[: len(keys)], refs[len(keys) :]
    q_ref, k_ref, v_ref, state_ref = refs[-4:]
    for j, out_ref in enumerate((q_ref, k_ref, v_ref)):
        out_ref[...] = project(w_ref, read_segments(segments, keys, span), j).astype(BF16)
    size = q_ref.shape[1] // heads
    for h in range(heads):
        cols = slice(h * size, (h + 1) * size)
        state_ref[0, h] = dot(k_ref[:, cols], v_ref[:, cols], TN)
        state_ref[1, h] = dot(q_ref[:, cols], g_ref[span[0] : span[1], cols], TN)


def last_kernel(keys, span, heads, w_ref, g_ref, part_ref, *refs):
    segments, refs = refs[: len(keys)], refs[len(keys) :]
    earlier, refs = refs[:-6], refs[-6:]
    q_ref, k_ref, v_ref, state_ref, total_ref, send_ref = refs
    for j, out_ref in enumerate((q_ref, k_ref, v_ref)):
        term = project(w_ref, read_segments(segments, keys, span), j)
        out_ref[...] = (part_ref[j] + term).astype(BF16)
    size = q_ref.shape[1] // heads
    share = heads // GROUP
    for h in range(heads):
        cols = slice(h * size, (h + 1) * size)
        state_ref[0, h] = dot(k_ref[:, cols], v_ref[:, cols], TN)
        state_ref[1, h] = dot(q_ref[:, cols], g_ref[span[0] : span[1], cols], TN)
        for s in range(2):
            total = state_ref[s, h]
            for other in earlier:
                total = total + other[s, h]
            total_ref[s, h] = total
            send_ref[h // share, s, h % share] = total.astype(BF16)


def local_kernel(span, heads, weight_ref, q_ref, k_ref, v_ref, g_ref, after_ref, out_ref):
    rows = q_ref.shape[0]
    size = q_ref.shape[1] // heads
    norm = 1.0 / math.sqrt(size * g_ref.shape[0])
    at = lax.broadcasted_iota(jnp.int32, (rows, rows), 0)
    of = lax.broadcasted_iota(jnp.int32, (rows, rows), 1)
    causal = at >= of
    for h in range(heads):
        cols = slice(h * size, (h + 1) * size)
        q, k, v = q_ref[:, cols], k_ref[:, cols], v_ref[:, cols]
        g = g_ref[span[0] : span[1], cols]
        scale = weight_ref[h, 0] * norm
        attend = jnp.where(causal, dot(q, k, NT) * scale, 0.0).astype(BF16)
        grad = jnp.where(causal, dot(g, v, NT) * scale, 0.0).astype(BF16)
        out_ref[0, :, cols] = dot(attend, v)
        out_ref[1, :, cols] = dot(grad, k)
        out_ref[2, :, cols] = dot(grad, q, TN)
        out_ref[3, :, cols] = dot(attend, g, TN)


def owner_kernel(final, total_ref, got_ref, near_ref, level_ref, sum_ref, next_ref):
    position = lax.axis_index("seq")
    place = lax.rem(position, GROUP)
    heads = total_ref.shape[1]
    share = heads // GROUP
    odd, high = bit_of(position, 0), bit_of(position, 1)
    for h in range(heads):
        near_ref[h] = jnp.where(odd, total_ref[1, h], total_ref[0, h]).astype(BF16)
    for e in range(share):
        mine, other = [], []
        for s in range(2):
            mine.append(total_ref[s, place * share + e] + got_ref[place ^ 1, s, e].astype(F32))
            other.append(
                got_ref[place ^ 2, s, e].astype(F32) + got_ref[place ^ 3, s, e].astype(F32)
            )
        level_ref[0, e] = jnp.where(high, other[0], other[1]).astype(BF16)
        level_ref[1, e] = jnp.where(high, mine[1], mine[0]).astype(BF16)
        sums = [mine[s] + other[s] for s in range(2)]
        write_next(sums, e, 2, final, sum_ref, next_ref)


def write_next(sums, e, bit, final, sum_ref, next_ref):
    if final:
        value = jnp.where(bit_of(lax.axis_index("seq"), bit), sums[1], sums[0])
        next_ref[0, e] = value.astype(BF16)
        return
    for s in range(2):
        sum_ref[s, e] = sums[s]
        next_ref[s, e] = sums[s].astype(BF16)


def climb_kernel(bit, next_final, got_ref, old_ref, level_ref, sum_ref, next_ref):
    on = bit_of(lax.axis_index("seq"), bit)
    for e in range(got_ref.shape[1]):
        both = [got_ref[s, e].astype(F32) for s in range(2)]
        level_ref[e] = jnp.where(on, both[0], both[1]).astype(BF16)
        sums = [old_ref[s, e] + both[s] for s in range(2)]
        write_next(sums, e, bit + 1, next_final, sum_ref, next_ref)


def return_kernel(level_ref, last_ref, *refs):
    between, out_ref = refs[:-1], refs[-1]
    high = bit_of(lax.axis_index("seq"), 1)
    for slot in range(GROUP):
        same = high if slot >= 2 else jnp.logical_not(high)
        out_ref[slot, 0] = jnp.where(same, level_ref[0], level_ref[1])
        for b, ref in enumerate(between, 1):
            out_ref[slot, b] = ref[...]
        out_ref[slot, len(between) + 1] = last_ref[0]


def finish_kernel(spans, heads, weight_ref, g_ref, near_ref, *refs):
    chunks = len(spans)
    levels_ref, refs = refs[0], refs[1:]
    q_refs, refs = refs[:chunks], refs[chunks:]
    k_refs, refs = refs[:chunks], refs[chunks:]
    v_refs, refs = refs[:chunks], refs[chunks:]
    state_refs, refs = refs[:chunks], refs[chunks:]
    part_refs, refs = refs[:chunks], refs[chunks:]
    outs, (held, mix_ref, sems) = refs[:4], refs[4:]
    position = lax.axis_index("seq")
    size = q_refs[0].shape[1] // heads
    share = heads // GROUP
    block = g_ref.shape[0]
    norm = 1.0 / math.sqrt(size * block)
    for m in range(GROUP):
        for e in range(share):
            h = m * share + e
            values = [near_ref[h]] + [levels_ref[m, b, e] for b in range(levels_ref.shape[1])]
            forward = backward = None
            for level, value in enumerate(values):
                coef = weight_ref[h, level + 1] * (1.0 / math.sqrt(size * block * 2**level))
                on = bit_of(position, level)
                value = value.astype(F32)
                to_forward = jnp.where(on, coef, 0.0) * value
                to_backward = jnp.where(on, 0.0, coef) * value
                forward = to_forward if forward is None else forward + to_forward
                backward = to_backward if backward is None else backward + to_backward
            mix_ref[0, h] = forward
            mix_ref[1, h] = backward
    zero = jnp.zeros((size, size), BF16)
    copies = []
    for c in range(chunks):
        span = slice(*spans[c])
        for h in range(0, heads, 2):
            cols = slice(h * size, (h + 2) * size)
            blocks = []
            for s in range(2):
                pair = []
                for e in (h, h + 1):
                    value = None
                    for other in range(c) if s == 0 else range(c + 1, chunks):
                        term = state_refs[other][s, e]
                        value = term if value is None else value + term
                    mix = mix_ref[s, e]
                    if value is not None:
                        mix = mix + (weight_ref[e, 0] * norm) * value
                    pair.append(mix.astype(BF16))
                top = jnp.concatenate([pair[0], zero], axis=1)
                bottom = jnp.concatenate([zero, pair[1]], axis=1)
                blocks.append(jnp.concatenate([top, bottom], axis=0))
            forward, backward = blocks
            terms = (
                dot(q_refs[c][:, cols], forward),
                dot(g_ref[span, cols], forward, NT),
                dot(v_refs[c][:, cols], backward, NT),
                dot(k_refs[c][:, cols], backward),
            )
            for j in range(4):
                held[j, span, cols] = (terms[j] + part_refs[c][j, :, cols]).astype(BF16)
        for j in range(4):
            copy = pltpu.make_async_copy(held.at[j, span], outs[j].at[span], sems.at[j, c])
            copy.start()
            copies.append(copy)
    for copy in copies:
        copy.wait()


def exchange(totals, sends, local, late):
    depth = lax.axis_size("seq").bit_length() - 1
    heads, square = totals.shape[1], totals.shape[2:]
    share = heads // GROUP
    last = depth - 1

    def message(bit):
        return pltpu.VMEM((1 if bit == last else 2, share, *square), BF16)

    def running(bit):
        return pltpu.VMEM((1, 8, 128) if bit == last else (2, share, *square), F32)

    got = trade(sends, "seq")
    near, levels, sums, sent = call(
        functools.partial(owner_kernel, last == 2),
        [
            pltpu.VMEM((heads, *square), BF16),
            pltpu.VMEM((2, share, *square), BF16),
            running(2),
            message(2),
        ],
        [totals, got],
        [VMEM] * 2,
        10**6,
    )
    fillers = [local(c, sent) for c in late]
    between = []
    for bit in range(2, last):
        found, sums, sent = call(
            functools.partial(climb_kernel, bit, bit + 1 == last),
            [pltpu.VMEM((share, *square), BF16), running(bit + 1), message(bit + 1)],
            [swap(sent, "seq", 1 << bit), sums],
            [VMEM] * 2,
            10**6,
        )
        between.append(found)
    operands = [levels, swap(sent, "seq", 1 << last), *between]
    outs = [pltpu.VMEM((GROUP, depth - 1, share, *square), BF16)]
    (back,) = call(
        return_kernel_with(len(operands)),
        outs,
        [*operands, *fillers],
        [VMEM] * len(operands) + [ANY] * len(fillers),
        10**6,
    )
    near = swap(near, "seq", 1)
    return near, trade(back, "seq"), fillers


def return_kernel_with(count):
    def kernel(*refs):
        return_kernel(*refs[:count], refs[-1])

    return kernel


def per_device(inputs, w_qkv, level_weight, grad_out):
    rows, width = grad_out.shape
    heads = level_weight.shape[0]
    size = width // heads
    parts = lax.axis_size("head")
    edges = [rows * sum(SHARES[:c]) // sum(SHARES) for c in range(CHUNKS + 1)]
    spans = list(zip(edges[:-1], edges[1:]))
    copied = [(0, span) for span in spans]
    mine = load([inputs], copied[:1])
    mine += load([inputs], copied[1:], mine)
    grads, weights = load([grad_out, w_qkv], [(0, None), (1, None)], mine[1:2])
    top, *lows = [1 << b for b in reversed(range(parts.bit_length() - 1))]
    arrived = [swap(piece, "head", top) for piece in mine]
    arrived[0] = tie(arrived[0], weights)
    whole = {0: inputs}
    for low in lows:
        for k in sorted(whole):
            whole[k | low] = swap(whole[k], "head", low)
    state = pltpu.VMEM((2, heads, size, size), F32)
    qs, ks, vs, states, locals_ = [], [], [], [], []

    def local(c, after):
        chunk = spans[c][1] - spans[c][0]
        return call(
            functools.partial(local_kernel, spans[c], heads),
            [pltpu.VMEM((4, chunk, width), F32)],
            [level_weight, qs[c], ks[c], vs[c], grads, after],
            [SMEM] + [VMEM] * 4 + [ANY],
            24 * chunk * chunk * width if c >= CHUNKS - 2 else 0,
        )[0]

    after = None
    for c in range(CHUNKS):
        pieces = {**whole, 0: mine[c]}
        pieces[top] = arrived[c] if after is None else tie(arrived[c], after)
        for low in lows:
            for k in [k for k in sorted(pieces) if k & top]:
                pieces[k | low] = swap(pieces[k], "head", low)
        keys = sorted(pieces)
        chunk = spans[c][1] - spans[c][0]
        flat = pltpu.VMEM((chunk, width), BF16)
        flops = 0
        if c < CHUNKS - 1:
            if c > 0:
                locals_.append(local(c - 1, pieces[top]))
            operands = [weights, grads, *[pieces[k] for k in keys], *locals_[-1:]]
            got = call(
                functools.partial(project_kernel, keys, spans[c], heads),
                [flat, flat, flat, state],
                operands,
                [VMEM] * (2 + len(keys)) + [ANY] * len(locals_[-1:]),
                flops * len(keys),
            )
        else:
            early, late = keys[:-1], keys[-1:]
            (begun,) = call(
                functools.partial(early_kernel, early, spans[c]),
                [pltpu.VMEM((3, chunk, width), F32)],
                [weights, *[pieces[k] for k in early]],
                [VMEM] * (1 + len(early)),
                flops * len(early),
            )
            operands = [weights, grads, begun, *[pieces[k] for k in late], *states]
            got = call(
                functools.partial(last_kernel, late, spans[c], heads),
                [
                    flat,
                    flat,
                    flat,
                    state,
                    state,
                    pltpu.VMEM((GROUP, 2, heads // GROUP, size, size), BF16),
                ],
                operands,
                [VMEM] * len(operands),
                flops * len(late),
            )
        qs.append(got[0])
        ks.append(got[1])
        vs.append(got[2])
        states.append(got[3])
        after = got[3]
    near, levels, fillers = exchange(got[4], got[5], local, range(len(locals_), CHUNKS))
    locals_ += fillers
    operands = [level_weight, grads, near, levels, *qs, *ks, *vs, *states, *locals_]
    return call(
        functools.partial(finish_kernel, spans, heads),
        [jax.ShapeDtypeStruct((rows, width), BF16)] * 4,
        operands,
        [SMEM] + [VMEM] * (len(operands) - 1),
        16 * rows * size * width,
        [
            pltpu.VMEM((4, rows, width), BF16),
            pltpu.VMEM((2, heads, size, size), F32),
            pltpu.SemaphoreType.DMA((4, CHUNKS)),
        ],
        [ANY] * 4,
        12,
    )


def solution(mesh):
    in_specs = (P("seq", "head"), P(None, None, "head"), P("head", None), P("seq", "head"))
    out_specs = (P("seq", "head"), P("seq", "head"), P("seq", "head"), P("seq", "head"))
    return jax.shard_map(
        per_device, mesh=mesh, in_specs=in_specs, out_specs=out_specs, check_vma=False
    )
```

```python
import functools
import math

import jax
import jax.numpy as jnp
from jax import lax
from jax.experimental import pallas as pl
from jax.experimental.pallas import tpu as pltpu
from jax.sharding import PartitionSpec as P

SHARES = (14, 15, 17, 18)
CHUNKS = len(SHARES)
GROUP = 4
MIB = 2**20
VMEM = pl.BlockSpec(memory_space=pltpu.VMEM)
SMEM = pl.BlockSpec(memory_space=pltpu.SMEM)
ANY = pl.BlockSpec(memory_space=pl.ANY)
HBM = pl.BlockSpec(memory_space=pltpu.HBM)
NN = (((1,), (0,)), ((), ()))
NT = (((1,), (1,)), ((), ()))
TN = (((0,), (0,)), ((), ()))
BF16 = jnp.bfloat16
F32 = jnp.float32


def dot(a, b, dims=NN):
    return lax.dot_general(a, b, dims, preferred_element_type=F32)


def swap(value, axis, mask):
    pairs = [(source, source ^ mask) for source in range(lax.axis_size(axis))]
    return lax.ppermute(value, axis, pairs)


def bit_of(position, bit):
    return lax.rem(position // 2**bit, 2) == 1


def call(kernel, outs, operands, specs, flops, scratch=(), out_specs=None, limit=4, moved=0):
    return pl.pallas_call(
        kernel,
        out_shape=outs,
        in_specs=specs,
        out_specs=[VMEM] * len(outs) if out_specs is None else out_specs,
        scratch_shapes=scratch,
        compiler_params=pltpu.CompilerParams(vmem_limit_bytes=limit * MIB),
        cost_estimate=pl.CostEstimate(flops=flops, bytes_accessed=moved, transcendentals=0),
    )(*operands)


def load_kernel(copied, *refs):
    count = 1 + max(source for source, _ in copied)
    sources, refs = refs[:count], refs[-len(copied) - 1 :]
    outs, sems = refs[:-1], refs[-1]
    copies = []
    for i, (source, start) in enumerate(copied):
        ref = sources[source]
        if start is not None:
            ref = ref.at[pl.ds(start, outs[i].shape[0])]
        copies.append(pltpu.make_async_copy(ref, outs[i], sems.at[i]))
    for copy in copies:
        copy.start()
    for copy in copies:
        copy.wait()


def load(sources, copied, after=()):
    shapes = []
    for source, span in copied:
        shape = sources[source].shape
        rows = shape[0] if span is None else span[1] - span[0]
        shapes.append(pltpu.VMEM((rows, *shape[1:]), BF16))
    copied = [(source, span if span is None else span[0]) for source, span in copied]
    return call(
        functools.partial(load_kernel, copied),
        shapes,
        [*[pltpu.with_memory_space_constraint(x, pltpu.HBM) for x in sources], *after],
        [HBM] * len(sources) + [ANY] * len(after),
        0,
        [pltpu.SemaphoreType.DMA((len(copied),))],
        limit=2,
        moved=4 * sum(math.prod(shape.shape) for shape in shapes),
    )


def tie_kernel(value_ref, *refs):
    del value_ref, refs


def tie(value, *after):
    return pl.pallas_call(
        tie_kernel,
        out_shape=pltpu.VMEM(value.shape, value.dtype),
        in_specs=[VMEM] + [ANY] * len(after),
        out_specs=VMEM,
        input_output_aliases={0: 0},
        compiler_params=pltpu.CompilerParams(vmem_limit_bytes=MIB),
    )(value, *after)


def project(w_ref, segments, j):
    me = lax.axis_index("head")
    parts = lax.axis_size("head")
    depth = w_ref.shape[1] // parts
    total = None
    for k, rows in segments:
        start = pl.multiple_of((me ^ k) * depth, depth)
        term = dot(rows, w_ref[j, pl.ds(start, depth), :])
        total = term if total is None else total + term
    return total


def read_segments(refs, keys, span):
    found = []
    for k, ref in zip(keys, refs):
        whole = ref.shape[0] != span[1] - span[0]
        found.append((k, ref[span[0] : span[1], :] if whole else ref[...]))
    return found


def early_kernel(keys, span, w_ref, *refs):
    segments, total_ref = refs[:-1], refs[-1]
    for j in range(3):
        total_ref[j] = project(w_ref, read_segments(segments, keys, span), j)


def project_kernel(keys, span, heads, w_ref, g_ref, *refs):
    segments, refs = refs[: len(keys)], refs[len(keys) :]
    q_ref, k_ref, v_ref, state_ref = refs[-4:]
    for j, out_ref in enumerate((q_ref, k_ref, v_ref)):
        out_ref[...] = project(w_ref, read_segments(segments, keys, span), j).astype(BF16)
    size = q_ref.shape[1] // heads
    for h in range(heads):
        cols = slice(h * size, (h + 1) * size)
        state_ref[0, h] = dot(k_ref[:, cols], v_ref[:, cols], TN)
        state_ref[1, h] = dot(q_ref[:, cols], g_ref[span[0] : span[1], cols], TN)


def last_kernel(keys, span, heads, w_ref, g_ref, part_ref, *refs):
    segments, refs = refs[: len(keys)], refs[len(keys) :]
    earlier, refs = refs[: -6 - (GROUP - 1)], refs[-6 - (GROUP - 1) :]
    q_ref, k_ref, v_ref, state_ref, total_ref, near_ref, *sends = refs
    for j, out_ref in enumerate((q_ref, k_ref, v_ref)):
        term = project(w_ref, read_segments(segments, keys, span), j)
        out_ref[...] = (part_ref[j] + term).astype(BF16)
    size = q_ref.shape[1] // heads
    share = heads // GROUP
    place = lax.rem(lax.axis_index("seq"), GROUP)
    for h in range(heads):
        cols = slice(h * size, (h + 1) * size)
        state_ref[0, h] = dot(k_ref[:, cols], v_ref[:, cols], TN)
        state_ref[1, h] = dot(q_ref[:, cols], g_ref[span[0] : span[1], cols], TN)
        for s in range(2):
            total = state_ref[s, h]
            for other in earlier:
                total = total + other[s, h]
            total_ref[s, h] = total
    for m, send in enumerate(sends, 1):
        for s in range(2):
            for e in range(share):
                send[s, e] = total_ref[s, (place ^ m) * share + e].astype(BF16)
    odd = bit_of(lax.axis_index("seq"), 0)
    for h in range(heads):
        near_ref[h] = jnp.where(odd, total_ref[1, h], total_ref[0, h]).astype(BF16)


def local_kernel(span, heads, weight_ref, q_ref, k_ref, v_ref, g_ref, after_ref, out_ref):
    rows = q_ref.shape[0]
    size = q_ref.shape[1] // heads
    norm = 1.0 / math.sqrt(size * g_ref.shape[0])
    at = lax.broadcasted_iota(jnp.int32, (rows, rows), 0)
    of = lax.broadcasted_iota(jnp.int32, (rows, rows), 1)
    causal = at >= of
    for h in range(heads):
        cols = slice(h * size, (h + 1) * size)
        q, k, v = q_ref[:, cols], k_ref[:, cols], v_ref[:, cols]
        g = g_ref[span[0] : span[1], cols]
        scale = weight_ref[h, 0] * norm
        attend = jnp.where(causal, dot(q, k, NT) * scale, 0.0).astype(BF16)
        grad = jnp.where(causal, dot(g, v, NT) * scale, 0.0).astype(BF16)
        out_ref[0, :, cols] = dot(attend, v)
        out_ref[1, :, cols] = dot(grad, k)
        out_ref[2, :, cols] = dot(grad, q, TN)
        out_ref[3, :, cols] = dot(attend, g, TN)


def owner_kernel(final, total_ref, *refs):
    got, (level_ref, sum_ref, next_ref) = refs[: GROUP - 1], refs[-3:]
    position = lax.axis_index("seq")
    place = lax.rem(position, GROUP)
    share = total_ref.shape[1] // GROUP
    high = bit_of(position, 1)
    for e in range(share):
        mine, other = [], []
        for s in range(2):
            mine.append(total_ref[s, place * share + e] + got[0][s, e].astype(F32))
            other.append(got[1][s, e].astype(F32) + got[2][s, e].astype(F32))
        level_ref[0, e] = jnp.where(high, other[0], other[1]).astype(BF16)
        level_ref[1, e] = jnp.where(high, mine[1], mine[0]).astype(BF16)
        sums = [mine[s] + other[s] for s in range(2)]
        write_next(sums, e, 2, final, sum_ref, next_ref)


def write_next(sums, e, bit, final, sum_ref, next_ref):
    if final:
        value = jnp.where(bit_of(lax.axis_index("seq"), bit), sums[1], sums[0])
        next_ref[0, e] = value.astype(BF16)
        return
    for s in range(2):
        sum_ref[s, e] = sums[s]
        next_ref[s, e] = sums[s].astype(BF16)


def climb_kernel(bit, next_final, got_ref, old_ref, level_ref, sum_ref, next_ref):
    on = bit_of(lax.axis_index("seq"), bit)
    for e in range(got_ref.shape[1]):
        both = [got_ref[s, e].astype(F32) for s in range(2)]
        level_ref[e] = jnp.where(on, both[0], both[1]).astype(BF16)
        sums = [old_ref[s, e] + both[s] for s in range(2)]
        write_next(sums, e, bit + 1, next_final, sum_ref, next_ref)


def return_kernel(level_ref, last_ref, *refs):
    between, (near_ref, far_ref) = refs[:-2], refs[-2:]
    for index, out_ref in enumerate((near_ref, far_ref)):
        out_ref[0] = level_ref[index]
        for b, ref in enumerate(between, 1):
            out_ref[b] = ref[...]
        out_ref[len(between) + 1] = last_ref[0]


def pair_block(first, second):
    zero = jnp.zeros(first.shape, BF16)
    top = jnp.concatenate([first.astype(BF16), zero], axis=1)
    bottom = jnp.concatenate([zero, second.astype(BF16)], axis=1)
    return jnp.concatenate([top, bottom], axis=0)


def prepare_kernel(spans, heads, weight_ref, g_ref, *refs):
    chunks = len(spans)
    q_refs, refs = refs[:chunks], refs[chunks:]
    k_refs, refs = refs[:chunks], refs[chunks:]
    v_refs, refs = refs[:chunks], refs[chunks:]
    state_refs, refs = refs[:chunks], refs[chunks:]
    part_refs, refs = refs[:chunks], refs[chunks:]
    outs = refs[-chunks:]
    size = q_refs[0].shape[1] // heads
    norm = 1.0 / math.sqrt(size * g_ref.shape[0])
    for h in range(0, heads, 2):
        cols = slice(h * size, (h + 2) * size)
        for s in range(2):
            order = range(chunks) if s == 0 else range(chunks - 1, -1, -1)
            sums = None
            for c in order:
                first, second = (0, 1) if s == 0 else (2, 3)
                if sums is None:
                    for j in (first, second):
                        outs[c][j, :, cols] = part_refs[c][j, :, cols]
                else:
                    scaled = [weight_ref[h + e, 0] * norm * sums[e] for e in range(2)]
                    weight = pair_block(*scaled)
                    if s == 0:
                        terms = (
                            dot(q_refs[c][:, cols], weight),
                            dot(g_ref[slice(*spans[c]), cols], weight, NT),
                        )
                    else:
                        terms = (
                            dot(v_refs[c][:, cols], weight, NT),
                            dot(k_refs[c][:, cols], weight),
                        )
                    for j, term in zip((first, second), terms):
                        outs[c][j, :, cols] = part_refs[c][j, :, cols] + term
                found = [state_refs[c][s, h + e] for e in range(2)]
                sums = found if sums is None else [sums[e] + found[e] for e in range(2)]


def finish_kernel(spans, heads, weight_ref, g_ref, near_ref, *refs):
    chunks = len(spans)
    levels, refs = refs[:GROUP], refs[GROUP:]
    q_refs, refs = refs[:chunks], refs[chunks:]
    k_refs, refs = refs[:chunks], refs[chunks:]
    v_refs, refs = refs[:chunks], refs[chunks:]
    part_refs, refs = refs[:chunks], refs[chunks:]
    outs, (held, mix_ref, sems) = refs[:4], refs[4:]
    position = lax.axis_index("seq")
    place = lax.rem(position, GROUP)
    size = q_refs[0].shape[1] // heads
    share = heads // GROUP
    block = g_ref.shape[0]
    for m in range(GROUP):
        for e in range(share):
            h = (place ^ m) * share + e
            values = [near_ref[h]] + [levels[m][b, e] for b in range(levels[m].shape[0])]
            forward = backward = None
            for level, value in enumerate(values):
                coef = weight_ref[h, level + 1] * (1.0 / math.sqrt(size * block * 2**level))
                on = bit_of(position, level)
                value = value.astype(F32)
                to_forward = jnp.where(on, coef, 0.0) * value
                to_backward = jnp.where(on, 0.0, coef) * value
                forward = to_forward if forward is None else forward + to_forward
                backward = to_backward if backward is None else backward + to_backward
            mix_ref[0, h] = forward.astype(BF16)
            mix_ref[1, h] = backward.astype(BF16)
    weights = [
        [pair_block(mix_ref[s, h], mix_ref[s, h + 1]) for h in range(0, heads, 2)] for s in range(2)
    ]
    copies = []
    for j in range(4):
        for c in range(chunks):
            span = slice(*spans[c])
            for h in range(0, heads, 2):
                cols = slice(h * size, (h + 2) * size)
                weight = weights[j // 2][h // 2]
                if j == 0:
                    term = dot(q_refs[c][:, cols], weight)
                elif j == 1:
                    term = dot(g_ref[span, cols], weight, NT)
                elif j == 2:
                    term = dot(v_refs[c][:, cols], weight, NT)
                else:
                    term = dot(k_refs[c][:, cols], weight)
                held[j, span, cols] = (term + part_refs[c][j, :, cols]).astype(BF16)
            copy = pltpu.make_async_copy(held.at[j, span], outs[j].at[span], sems.at[j, c])
            copy.start()
            copies.append(copy)
    for copy in copies:
        copy.wait()


def exchange(totals, near, sends, local, late):
    depth = lax.axis_size("seq").bit_length() - 1
    heads, square = totals.shape[1], totals.shape[2:]
    share = heads // GROUP
    last = depth - 1

    def message(bit):
        return pltpu.VMEM((1 if bit == last else 2, share, *square), BF16)

    def running(bit):
        return pltpu.VMEM((1, 8, 128) if bit == last else (2, share, *square), F32)

    got = [swap(send, "seq", m) for m, send in enumerate(sends, 1)]
    filler = local(late[0], sends[0])
    near = swap(near, "seq", 1)
    levels, sums, sent = call(
        functools.partial(owner_kernel, last == 2),
        [
            pltpu.VMEM((2, share, *square), BF16),
            running(2),
            message(2),
        ],
        [totals, *got, filler],
        [VMEM] * GROUP + [ANY],
        10**6,
    )
    fillers = [filler] + [local(c, sent) for c in late[1:]]
    between = []
    for bit in range(2, last):
        found, sums, sent = call(
            functools.partial(climb_kernel, bit, bit + 1 == last),
            [pltpu.VMEM((share, *square), BF16), running(bit + 1), message(bit + 1)],
            [swap(sent, "seq", 1 << bit), sums],
            [VMEM] * 2,
            10**6,
        )
        between.append(found)
    operands = [levels, swap(sent, "seq", 1 << last), *between]
    outs = [pltpu.VMEM((depth - 1, share, *square), BF16)] * 2
    mine, other = call(
        return_kernel_with(len(operands)),
        outs,
        [*operands, *fillers[1:], near],
        [VMEM] * len(operands) + [ANY] * len(fillers),
        10**6,
    )
    returned = [swap(mine if m == 1 else other, "seq", m) for m in range(1, GROUP)]
    return near, [mine, *returned], fillers


def return_kernel_with(count):
    def kernel(*refs):
        return_kernel(*refs[:count], *refs[-2:])

    return kernel


def per_device(inputs, w_qkv, level_weight, grad_out):
    rows, width = grad_out.shape
    heads = level_weight.shape[0]
    size = width // heads
    parts = lax.axis_size("head")
    edges = [rows * sum(SHARES[:c]) // sum(SHARES) for c in range(CHUNKS + 1)]
    spans = list(zip(edges[:-1], edges[1:]))
    copied = [(0, span) for span in spans]
    mine = load([inputs], copied[:1])
    mine = [*mine, *load([inputs], copied[1:], mine)]
    grads, weights = load([grad_out, w_qkv], [(0, None), (1, None)], mine[1:2])
    top, *lows = [1 << b for b in reversed(range(parts.bit_length() - 1))]
    arrived = [swap(piece, "head", top) for piece in mine]
    arrived[0] = tie(arrived[0], weights)
    whole = {0: inputs}
    for low in lows:
        for k in sorted(whole):
            whole[k | low] = swap(whole[k], "head", low)
    state = pltpu.VMEM((2, heads, size, size), F32)
    qs, ks, vs, states, locals_ = [], [], [], [], []

    def local(c, after):
        chunk = spans[c][1] - spans[c][0]
        return call(
            functools.partial(local_kernel, spans[c], heads),
            [pltpu.VMEM((4, chunk, width), F32)],
            [level_weight, qs[c], ks[c], vs[c], grads, after],
            [SMEM] + [VMEM] * 4 + [ANY],
            24 * chunk * chunk * width if c >= CHUNKS - 2 else 0,
        )[0]

    after = None
    for c in range(CHUNKS):
        pieces = {**whole, 0: mine[c]}
        pieces[top] = arrived[c] if after is None else tie(arrived[c], after)
        for low in lows:
            for k in [k for k in sorted(pieces) if k & top]:
                pieces[k | low] = swap(pieces[k], "head", low)
        keys = sorted(pieces)
        chunk = spans[c][1] - spans[c][0]
        flat = pltpu.VMEM((chunk, width), BF16)
        flops = 0
        if c < CHUNKS - 1:
            if c > 0:
                locals_.append(local(c - 1, pieces[top]))
            operands = [weights, grads, *[pieces[k] for k in keys], *locals_[-1:]]
            got = call(
                functools.partial(project_kernel, keys, spans[c], heads),
                [flat, flat, flat, state],
                operands,
                [VMEM] * (2 + len(keys)) + [ANY] * len(locals_[-1:]),
                flops * len(keys),
            )
        else:
            early, late = keys[:-1], keys[-1:]
            (begun,) = call(
                functools.partial(early_kernel, early, spans[c]),
                [pltpu.VMEM((3, chunk, width), F32)],
                [weights, *[pieces[k] for k in early]],
                [VMEM] * (1 + len(early)),
                flops * len(early),
            )
            operands = [weights, grads, begun, *[pieces[k] for k in late], *states]
            got = call(
                functools.partial(last_kernel, late, spans[c], heads),
                [
                    flat,
                    flat,
                    flat,
                    state,
                    state,
                    pltpu.VMEM((heads, size, size), BF16),
                    *[pltpu.VMEM((2, heads // GROUP, size, size), BF16)] * (GROUP - 1),
                ],
                operands,
                [VMEM] * len(operands),
                flops * len(late),
            )
        qs.append(got[0])
        ks.append(got[1])
        vs.append(got[2])
        states.append(got[3])
        after = got[3]
    near, levels, fillers = exchange(got[4], got[5], got[6:], local, range(len(locals_), CHUNKS))
    locals_ += fillers
    operands = [level_weight, grads, *qs, *ks, *vs, *states, *locals_, levels[0]]
    sums = call(
        functools.partial(prepare_kernel, spans, heads),
        [pltpu.VMEM(part.shape, F32) for part in locals_],
        operands,
        [SMEM] + [VMEM] * (len(operands) - 2) + [ANY],
        12 * rows * size * width,
        limit=8,
    )
    operands = [level_weight, grads, near, *levels, *qs, *ks, *vs, *sums]
    return call(
        functools.partial(finish_kernel, spans, heads),
        [jax.ShapeDtypeStruct((rows, width), BF16)] * 4,
        operands,
        [SMEM] + [VMEM] * (len(operands) - 1),
        16 * rows * size * width,
        [
            pltpu.VMEM((4, rows, width), BF16),
            pltpu.VMEM((2, heads, size, size), BF16),
            pltpu.SemaphoreType.DMA((4, CHUNKS)),
        ],
        [ANY] * 4,
        12,
    )


def solution(mesh):
    in_specs = (P("seq", "head"), P(None, None, "head"), P("head", None), P("seq", "head"))
    out_specs = (P("seq", "head"), P("seq", "head"), P("seq", "head"), P("seq", "head"))
    return jax.shard_map(
        per_device, mesh=mesh, in_specs=in_specs, out_specs=out_specs, check_vma=False
    )
```

```python
import functools
import math

import jax
import jax.numpy as jnp
from jax import lax
from jax.experimental import pallas as pl
from jax.experimental.pallas import tpu as pltpu
from jax.sharding import PartitionSpec as P

SHARES = (10, 12, 13, 14, 15)
CHUNKS = len(SHARES)
GROUP = 4
MIB = 2**20
VMEM = pl.BlockSpec(memory_space=pltpu.VMEM)
SMEM = pl.BlockSpec(memory_space=pltpu.SMEM)
ANY = pl.BlockSpec(memory_space=pl.ANY)
HBM = pl.BlockSpec(memory_space=pltpu.HBM)
NN = (((1,), (0,)), ((), ()))
NT = (((1,), (1,)), ((), ()))
TN = (((0,), (0,)), ((), ()))
BF16 = jnp.bfloat16
F32 = jnp.float32


def dot(a, b, dims=NN):
    return lax.dot_general(a, b, dims, preferred_element_type=F32)


def swap(value, axis, mask):
    pairs = [(source, source ^ mask) for source in range(lax.axis_size(axis))]
    return lax.ppermute(value, axis, pairs)


def bit_of(position, bit):
    return lax.rem(position // 2**bit, 2) == 1


def call(kernel, outs, operands, specs, flops, scratch=(), out_specs=None, limit=4, moved=0):
    return pl.pallas_call(
        kernel,
        out_shape=outs,
        in_specs=specs,
        out_specs=[VMEM] * len(outs) if out_specs is None else out_specs,
        scratch_shapes=scratch,
        compiler_params=pltpu.CompilerParams(vmem_limit_bytes=limit * MIB),
        cost_estimate=pl.CostEstimate(flops=flops, bytes_accessed=moved, transcendentals=0),
    )(*operands)


def load_kernel(copied, *refs):
    count = 1 + max(source for source, _ in copied)
    sources, refs = refs[:count], refs[-len(copied) - 1 :]
    outs, sems = refs[:-1], refs[-1]
    copies = []
    for i, (source, start) in enumerate(copied):
        ref = sources[source]
        if start is not None:
            ref = ref.at[pl.ds(start, outs[i].shape[0])]
        copies.append(pltpu.make_async_copy(ref, outs[i], sems.at[i]))
    for copy in copies:
        copy.start()
    for copy in copies:
        copy.wait()


def load(sources, copied, after=()):
    shapes = []
    for source, span in copied:
        shape = sources[source].shape
        rows = shape[0] if span is None else span[1] - span[0]
        shapes.append(pltpu.VMEM((rows, *shape[1:]), BF16))
    copied = [(source, span if span is None else span[0]) for source, span in copied]
    return call(
        functools.partial(load_kernel, copied),
        shapes,
        [*[pltpu.with_memory_space_constraint(x, pltpu.HBM) for x in sources], *after],
        [HBM] * len(sources) + [ANY] * len(after),
        0,
        [pltpu.SemaphoreType.DMA((len(copied),))],
        limit=2,
        moved=4 * sum(math.prod(shape.shape) for shape in shapes),
    )


def tie_kernel(value_ref, *refs):
    del value_ref, refs


def tie(value, *after):
    return pl.pallas_call(
        tie_kernel,
        out_shape=pltpu.VMEM(value.shape, value.dtype),
        in_specs=[VMEM] + [ANY] * len(after),
        out_specs=VMEM,
        input_output_aliases={0: 0},
        compiler_params=pltpu.CompilerParams(vmem_limit_bytes=MIB),
    )(value, *after)


def project(w_ref, segments, j):
    me = lax.axis_index("head")
    parts = lax.axis_size("head")
    depth = w_ref.shape[1] // parts
    total = None
    for k, rows in segments:
        start = pl.multiple_of((me ^ k) * depth, depth)
        term = dot(rows, w_ref[j, pl.ds(start, depth), :])
        total = term if total is None else total + term
    return total


def read_segments(refs, keys, span):
    found = []
    for k, ref in zip(keys, refs):
        whole = ref.shape[0] != span[1] - span[0]
        found.append((k, ref[span[0] : span[1], :] if whole else ref[...]))
    return found


def early_kernel(keys, span, w_ref, *refs):
    segments, total_ref = refs[:-1], refs[-1]
    for j in range(3):
        total_ref[j] = project(w_ref, read_segments(segments, keys, span), j)


def project_kernel(keys, span, heads, w_ref, g_ref, *refs):
    segments, refs = refs[: len(keys)], refs[len(keys) :]
    q_ref, k_ref, v_ref, state_ref = refs[-4:]
    for j, out_ref in enumerate((q_ref, k_ref, v_ref)):
        out_ref[...] = project(w_ref, read_segments(segments, keys, span), j).astype(BF16)
    size = q_ref.shape[1] // heads
    for h in range(heads):
        cols = slice(h * size, (h + 1) * size)
        state_ref[0, h] = dot(k_ref[:, cols], v_ref[:, cols], TN)
        state_ref[1, h] = dot(q_ref[:, cols], g_ref[span[0] : span[1], cols], TN)


def last_kernel(keys, span, heads, w_ref, g_ref, part_ref, *refs):
    segments, refs = refs[: len(keys)], refs[len(keys) :]
    earlier, refs = refs[: -6 - (GROUP - 1)], refs[-6 - (GROUP - 1) :]
    q_ref, k_ref, v_ref, state_ref, total_ref, near_ref, *sends = refs
    for j, out_ref in enumerate((q_ref, k_ref, v_ref)):
        term = project(w_ref, read_segments(segments, keys, span), j)
        out_ref[...] = (part_ref[j] + term).astype(BF16)
    size = q_ref.shape[1] // heads
    share = heads // GROUP
    place = lax.rem(lax.axis_index("seq"), GROUP)
    for h in range(heads):
        cols = slice(h * size, (h + 1) * size)
        state_ref[0, h] = dot(k_ref[:, cols], v_ref[:, cols], TN)
        state_ref[1, h] = dot(q_ref[:, cols], g_ref[span[0] : span[1], cols], TN)
        for s in range(2):
            total = state_ref[s, h]
            for other in earlier:
                total = total + other[s, h]
            total_ref[s, h] = total
    for m, send in enumerate(sends, 1):
        for s in range(2):
            for e in range(share):
                send[s, e] = total_ref[s, (place ^ m) * share + e].astype(BF16)
    odd = bit_of(lax.axis_index("seq"), 0)
    for h in range(heads):
        near_ref[h] = jnp.where(odd, total_ref[1, h], total_ref[0, h]).astype(BF16)


def local_kernel(span, heads, weight_ref, q_ref, k_ref, v_ref, g_ref, after_ref, out_ref):
    rows = q_ref.shape[0]
    size = q_ref.shape[1] // heads
    norm = 1.0 / math.sqrt(size * g_ref.shape[0])
    at = lax.broadcasted_iota(jnp.int32, (rows, rows), 0)
    of = lax.broadcasted_iota(jnp.int32, (rows, rows), 1)
    columns = [slice(h * size, (h + 1) * size) for h in range(heads)]
    masked = []
    for h, cols in enumerate(columns):
        q, k, v = q_ref[:, cols], k_ref[:, cols], v_ref[:, cols]
        g = g_ref[span[0] : span[1], cols]
        scale = weight_ref[h, 0] * norm
        found = []
        for left, right, causal in (
            (q, k, at >= of),
            (g, v, at >= of),
            (v, g, of >= at),
            (k, q, of >= at),
        ):
            found.append(jnp.where(causal, dot(left, right, NT) * scale, 0.0).astype(BF16))
        masked.append(found)
    for h, cols in enumerate(columns):
        q, k, v = q_ref[:, cols], k_ref[:, cols], v_ref[:, cols]
        g = g_ref[span[0] : span[1], cols]
        for j, value in enumerate((v, k, q, g)):
            out_ref[j, :, cols] = dot(masked[h][j], value)


def owner_kernel(final, total_ref, *refs):
    got, (near_ref, far_ref, sum_ref, next_ref) = refs[: GROUP - 1], refs[-4:]
    position = lax.axis_index("seq")
    place = lax.rem(position, GROUP)
    share = total_ref.shape[1] // GROUP
    high = bit_of(position, 1)
    for e in range(share):
        mine, other = [], []
        for s in range(2):
            mine.append(total_ref[s, place * share + e] + got[0][s, e].astype(F32))
            other.append(got[1][s, e].astype(F32) + got[2][s, e].astype(F32))
        near_ref[e] = jnp.where(high, other[0], other[1]).astype(BF16)
        far_ref[e] = jnp.where(high, mine[1], mine[0]).astype(BF16)
        sums = [mine[s] + other[s] for s in range(2)]
        write_next(sums, e, 2, final, sum_ref, next_ref)


def write_next(sums, e, bit, final, sum_ref, next_ref):
    if final:
        value = jnp.where(bit_of(lax.axis_index("seq"), bit), sums[1], sums[0])
        next_ref[e] = value.astype(BF16)
        return
    for s in range(2):
        sum_ref[s, e] = sums[s]
        next_ref[s, e] = sums[s].astype(BF16)


def climb_kernel(bit, next_final, got_ref, old_ref, level_ref, sum_ref, next_ref):
    on = bit_of(lax.axis_index("seq"), bit)
    for e in range(got_ref.shape[1]):
        both = [got_ref[s, e].astype(F32) for s in range(2)]
        level_ref[e] = jnp.where(on, both[0], both[1]).astype(BF16)
        sums = [old_ref[s, e] + both[s] for s in range(2)]
        write_next(sums, e, bit + 1, next_final, sum_ref, next_ref)


def pair_block(first, second):
    zero = jnp.zeros(first.shape, BF16)
    top = jnp.concatenate([first.astype(BF16), zero], axis=1)
    bottom = jnp.concatenate([zero, second.astype(BF16)], axis=1)
    return jnp.concatenate([top, bottom], axis=0)


def finish_kernel(spans, heads, groups, weight_ref, g_ref, near_ref, *refs):
    chunks = len(spans)
    levels, refs = refs[: groups * GROUP], refs[groups * GROUP :]
    q_refs, refs = refs[:chunks], refs[chunks:]
    k_refs, refs = refs[:chunks], refs[chunks:]
    v_refs, refs = refs[:chunks], refs[chunks:]
    state_refs, refs = refs[:chunks], refs[chunks:]
    part_refs, refs = refs[:chunks], refs[chunks:]
    outs, (held, mix_ref, sems) = refs[:4], refs[4:]
    position = lax.axis_index("seq")
    place = lax.rem(position, GROUP)
    size = q_refs[0].shape[1] // heads
    share = heads // GROUP
    block = g_ref.shape[0]
    norm = 1.0 / math.sqrt(size * block)
    for m in range(GROUP):
        for e in range(share):
            h = (place ^ m) * share + e
            values = [near_ref[h]] + [levels[b * GROUP + m][e] for b in range(groups)]
            forward = backward = None
            for level, value in enumerate(values):
                coef = weight_ref[h, level + 1] * (1.0 / math.sqrt(size * block * 2**level))
                on = bit_of(position, level)
                value = value.astype(F32)
                to_forward = jnp.where(on, coef, 0.0) * value
                to_backward = jnp.where(on, 0.0, coef) * value
                forward = to_forward if forward is None else forward + to_forward
                backward = to_backward if backward is None else backward + to_backward
            mix_ref[0, h] = forward
            mix_ref[1, h] = backward
    copies = []
    for s in range(2):
        sums = [mix_ref[s, h] for h in range(heads)]
        for c in range(chunks) if s == 0 else reversed(range(chunks)):
            span = slice(*spans[c])
            weights = [pair_block(sums[h], sums[h + 1]) for h in range(0, heads, 2)]
            for j in (2 * s, 2 * s + 1):
                for h in range(0, heads, 2):
                    cols = slice(h * size, (h + 2) * size)
                    weight = weights[h // 2]
                    if j == 0:
                        term = dot(q_refs[c][:, cols], weight)
                    elif j == 1:
                        term = dot(g_ref[span, cols], weight, NT)
                    elif j == 2:
                        term = dot(v_refs[c][:, cols], weight, NT)
                    else:
                        term = dot(k_refs[c][:, cols], weight)
                    held[j, span, cols] = (term + part_refs[c][j, :, cols]).astype(BF16)
                copy = pltpu.make_async_copy(held.at[j, span], outs[j].at[span], sems.at[j, c])
                copy.start()
                copies.append(copy)
            sums = [
                total + weight_ref[h, 0] * norm * state_refs[c][s, h]
                for h, total in enumerate(sums)
            ]
    for copy in copies:
        copy.wait()


def exchange(totals, near, sends, local, late):
    depth = lax.axis_size("seq").bit_length() - 1
    heads, square = totals.shape[1], totals.shape[2:]
    share = heads // GROUP
    last = depth - 1

    def message(bit):
        return pltpu.VMEM((share, *square) if bit == last else (2, share, *square), BF16)

    def running(bit):
        return pltpu.VMEM((1, 8, 128) if bit == last else (2, share, *square), F32)

    def spread(mine, other):
        return [mine, *[swap(mine if m == 1 else other, "seq", m) for m in range(1, GROUP)]]

    one = pltpu.VMEM((share, *square), BF16)
    got = [swap(send, "seq", m) for m, send in enumerate(sends, 1)]
    near = swap(near, "seq", 1)
    fillers = [local(late[0], sends[0])]
    mine, other, sums, sent = call(
        functools.partial(owner_kernel, last == 2),
        [one, one, running(2), message(2)],
        [totals, *got, fillers[0]],
        [VMEM] * GROUP + [ANY],
        10**6,
    )
    levels = spread(mine, other)
    for bit in range(2, last):
        found, sums, sent = call(
            functools.partial(climb_kernel, bit, bit + 1 == last),
            [one, running(bit + 1), message(bit + 1)],
            [swap(sent, "seq", 1 << bit), sums],
            [VMEM] * 2,
            10**6,
        )
        levels += spread(found, found)
    found = tie(swap(sent, "seq", 1 << last), near, *levels)
    levels += spread(found, found)
    fillers += [local(c, found) for c in late[1:]]
    return near, levels, fillers


def per_device(inputs, w_qkv, level_weight, grad_out):
    rows, width = grad_out.shape
    heads = level_weight.shape[0]
    size = width // heads
    parts = lax.axis_size("head")
    edges = [rows * sum(SHARES[:c]) // sum(SHARES) for c in range(CHUNKS + 1)]
    spans = list(zip(edges[:-1], edges[1:]))
    copied = [(0, span) for span in spans]
    mine = load([inputs], copied[:1])
    mine = [*mine, *load([inputs], copied[1:], mine)]
    grads, weights = load([grad_out, w_qkv], [(0, None), (1, None)], mine[1:2])
    top, *lows = [1 << b for b in reversed(range(parts.bit_length() - 1))]
    arrived = [swap(piece, "head", top) for piece in mine]
    arrived[0] = tie(arrived[0], weights)
    whole = {0: inputs}
    for low in lows:
        for k in sorted(whole):
            whole[k | low] = swap(whole[k], "head", low)
    state = pltpu.VMEM((2, heads, size, size), F32)
    qs, ks, vs, states, locals_ = [], [], [], [], []

    def local(c, after):
        chunk = spans[c][1] - spans[c][0]
        return call(
            functools.partial(local_kernel, spans[c], heads),
            [pltpu.VMEM((4, chunk, width), F32)],
            [level_weight, qs[c], ks[c], vs[c], grads, after],
            [SMEM] + [VMEM] * 4 + [ANY],
            100 * chunk * chunk * width if c >= CHUNKS - 2 else 0,
        )[0]

    after = None
    for c in range(CHUNKS):
        pieces = {**whole, 0: mine[c]}
        pieces[top] = arrived[c] if after is None else tie(arrived[c], after)
        for low in lows:
            for k in [k for k in sorted(pieces) if k & top]:
                pieces[k | low] = swap(pieces[k], "head", low)
        keys = sorted(pieces)
        chunk = spans[c][1] - spans[c][0]
        flat = pltpu.VMEM((chunk, width), BF16)
        flops = 0
        if c < CHUNKS - 1:
            if c > 0:
                locals_.append(local(c - 1, pieces[top]))
            operands = [weights, grads, *[pieces[k] for k in keys], *locals_[-1:]]
            got = call(
                functools.partial(project_kernel, keys, spans[c], heads),
                [flat, flat, flat, state],
                operands,
                [VMEM] * (2 + len(keys)) + [ANY] * len(locals_[-1:]),
                flops * len(keys),
            )
        else:
            early, late = keys[:-1], keys[-1:]
            (begun,) = call(
                functools.partial(early_kernel, early, spans[c]),
                [pltpu.VMEM((3, chunk, width), F32)],
                [weights, *[pieces[k] for k in early]],
                [VMEM] * (1 + len(early)),
                flops * len(early),
            )
            operands = [weights, grads, begun, *[pieces[k] for k in late], *states]
            got = call(
                functools.partial(last_kernel, late, spans[c], heads),
                [
                    flat,
                    flat,
                    flat,
                    state,
                    state,
                    pltpu.VMEM((heads, size, size), BF16),
                    *[pltpu.VMEM((2, heads // GROUP, size, size), BF16)] * (GROUP - 1),
                ],
                operands,
                [VMEM] * len(operands),
                flops * len(late),
            )
        qs.append(got[0])
        ks.append(got[1])
        vs.append(got[2])
        states.append(got[3])
        after = got[3]
    near, levels, fillers = exchange(got[4], got[5], got[6:], local, range(len(locals_), CHUNKS))
    locals_ += fillers
    operands = [level_weight, grads, near, *levels, *qs, *ks, *vs, *states, *locals_]
    return call(
        functools.partial(finish_kernel, spans, heads, len(levels) // GROUP),
        [jax.ShapeDtypeStruct((rows, width), BF16)] * 4,
        operands,
        [SMEM] + [VMEM] * (len(operands) - 1),
        16 * rows * size * width,
        [
            pltpu.VMEM((4, rows, width), BF16),
            pltpu.VMEM((2, heads, size, size), F32),
            pltpu.SemaphoreType.DMA((4, CHUNKS)),
        ],
        [ANY] * 4,
        12,
    )


def solution(mesh):
    in_specs = (P("seq", "head"), P(None, None, "head"), P("head", None), P("seq", "head"))
    out_specs = (P("seq", "head"), P("seq", "head"), P("seq", "head"), P("seq", "head"))
    return jax.shard_map(
        per_device, mesh=mesh, in_specs=in_specs, out_specs=out_specs, check_vma=False
    )
```

```python
import functools
import math

import jax
import jax.numpy as jnp
from jax import lax
from jax.experimental import pallas as pl
from jax.experimental.pallas import tpu as pltpu
from jax.sharding import PartitionSpec as P

SHARES = (10, 12, 13, 14, 15)
CHUNKS = len(SHARES)
GROUP = 4
MIB = 2**20
VMEM = pl.BlockSpec(memory_space=pltpu.VMEM)
SMEM = pl.BlockSpec(memory_space=pltpu.SMEM)
ANY = pl.BlockSpec(memory_space=pl.ANY)
HBM = pl.BlockSpec(memory_space=pltpu.HBM)
NN = (((1,), (0,)), ((), ()))
NT = (((1,), (1,)), ((), ()))
TN = (((0,), (0,)), ((), ()))
BF16 = jnp.bfloat16
F32 = jnp.float32


def dot(a, b, dims=NN):
    return lax.dot_general(a, b, dims, preferred_element_type=F32)


def swap(value, axis, mask):
    pairs = [(source, source ^ mask) for source in range(lax.axis_size(axis))]
    return lax.ppermute(value, axis, pairs)


def bit_of(position, bit):
    return lax.rem(position // 2**bit, 2) == 1


def call(kernel, outs, operands, specs, flops, scratch=(), out_specs=None, limit=4, moved=0):
    return pl.pallas_call(
        kernel,
        out_shape=outs,
        in_specs=specs,
        out_specs=[VMEM] * len(outs) if out_specs is None else out_specs,
        scratch_shapes=scratch,
        compiler_params=pltpu.CompilerParams(vmem_limit_bytes=limit * MIB),
        cost_estimate=pl.CostEstimate(flops=flops, bytes_accessed=moved, transcendentals=0),
    )(*operands)


def load_kernel(copied, *refs):
    count = 1 + max(source for source, _ in copied)
    sources, refs = refs[:count], refs[-len(copied) - 1 :]
    outs, sems = refs[:-1], refs[-1]
    copies = []
    for i, (source, start) in enumerate(copied):
        ref = sources[source]
        if start is not None:
            ref = ref.at[pl.ds(start, outs[i].shape[0])]
        copies.append(pltpu.make_async_copy(ref, outs[i], sems.at[i]))
    for copy in copies:
        copy.start()
    for copy in copies:
        copy.wait()


def load(sources, copied, after=()):
    shapes = []
    for source, span in copied:
        shape = sources[source].shape
        rows = shape[0] if span is None else span[1] - span[0]
        shapes.append(pltpu.VMEM((rows, *shape[1:]), BF16))
    copied = [(source, span if span is None else span[0]) for source, span in copied]
    return call(
        functools.partial(load_kernel, copied),
        shapes,
        [*[pltpu.with_memory_space_constraint(x, pltpu.HBM) for x in sources], *after],
        [HBM] * len(sources) + [ANY] * len(after),
        0,
        [pltpu.SemaphoreType.DMA((len(copied),))],
        limit=2,
        moved=4 * sum(math.prod(shape.shape) for shape in shapes),
    )


def tie_kernel(value_ref, *refs):
    del value_ref, refs


def tie(value, *after):
    return pl.pallas_call(
        tie_kernel,
        out_shape=pltpu.VMEM(value.shape, value.dtype),
        in_specs=[VMEM] + [ANY] * len(after),
        out_specs=VMEM,
        input_output_aliases={0: 0},
        compiler_params=pltpu.CompilerParams(vmem_limit_bytes=MIB),
    )(value, *after)


def project(w_ref, segments, j):
    me = lax.axis_index("head")
    parts = lax.axis_size("head")
    depth = w_ref.shape[1] // parts
    total = None
    for k, rows in segments:
        start = pl.multiple_of((me ^ k) * depth, depth)
        term = dot(rows, w_ref[j, pl.ds(start, depth), :])
        total = term if total is None else total + term
    return total


def read_segments(refs, keys, span):
    found = []
    for k, ref in zip(keys, refs):
        whole = ref.shape[0] != span[1] - span[0]
        found.append((k, ref[span[0] : span[1], :] if whole else ref[...]))
    return found


def early_kernel(keys, span, w_ref, *refs):
    segments, total_ref = refs[:-1], refs[-1]
    for j in range(3):
        total_ref[j] = project(w_ref, read_segments(segments, keys, span), j)


def project_kernel(keys, span, heads, w_ref, g_ref, *refs):
    segments, refs = refs[: len(keys)], refs[len(keys) :]
    q_ref, k_ref, v_ref, state_ref = refs[-4:]
    for j, out_ref in enumerate((q_ref, k_ref, v_ref)):
        out_ref[...] = project(w_ref, read_segments(segments, keys, span), j).astype(BF16)
    size = q_ref.shape[1] // heads
    for h in range(heads):
        cols = slice(h * size, (h + 1) * size)
        state_ref[0, h] = dot(k_ref[:, cols], v_ref[:, cols], TN)
        state_ref[1, h] = dot(q_ref[:, cols], g_ref[span[0] : span[1], cols], TN)


def last_kernel(keys, span, heads, w_ref, g_ref, part_ref, *refs):
    segments, refs = refs[: len(keys)], refs[len(keys) :]
    earlier, refs = refs[: -6 - (GROUP - 1)], refs[-6 - (GROUP - 1) :]
    q_ref, k_ref, v_ref, state_ref, total_ref, near_ref, *sends = refs
    for j, out_ref in enumerate((q_ref, k_ref, v_ref)):
        term = project(w_ref, read_segments(segments, keys, span), j)
        out_ref[...] = (part_ref[j] + term).astype(BF16)
    size = q_ref.shape[1] // heads
    share = heads // GROUP
    place = lax.rem(lax.axis_index("seq"), GROUP)
    for h in range(heads):
        cols = slice(h * size, (h + 1) * size)
        state_ref[0, h] = dot(k_ref[:, cols], v_ref[:, cols], TN)
        state_ref[1, h] = dot(q_ref[:, cols], g_ref[span[0] : span[1], cols], TN)
        for s in range(2):
            total = state_ref[s, h]
            for other in earlier:
                total = total + other[s, h]
            total_ref[s, h] = total
    for m, send in enumerate(sends, 1):
        for s in range(2):
            for e in range(share):
                send[s, e] = total_ref[s, (place ^ m) * share + e].astype(BF16)
    odd = bit_of(lax.axis_index("seq"), 0)
    for h in range(heads):
        near_ref[h] = jnp.where(odd, total_ref[1, h], total_ref[0, h]).astype(BF16)


def local_kernel(span, heads, weight_ref, q_ref, k_ref, v_ref, g_ref, after_ref, out_ref):
    rows = q_ref.shape[0]
    size = q_ref.shape[1] // heads
    norm = 1.0 / math.sqrt(size * g_ref.shape[0])
    at = lax.broadcasted_iota(jnp.int32, (rows, rows), 0)
    of = lax.broadcasted_iota(jnp.int32, (rows, rows), 1)
    columns = [slice(h * size, (h + 1) * size) for h in range(heads)]
    masked = []
    for h, cols in enumerate(columns):
        q, k, v = q_ref[:, cols], k_ref[:, cols], v_ref[:, cols]
        g = g_ref[span[0] : span[1], cols]
        scale = weight_ref[h, 0] * norm
        found = []
        for left, right, causal in (
            (q, k, at >= of),
            (g, v, at >= of),
            (v, g, of >= at),
            (k, q, of >= at),
        ):
            found.append(jnp.where(causal, dot(left, right, NT) * scale, 0.0).astype(BF16))
        masked.append(found)
    for h, cols in enumerate(columns):
        q, k, v = q_ref[:, cols], k_ref[:, cols], v_ref[:, cols]
        g = g_ref[span[0] : span[1], cols]
        for j, value in enumerate((v, k, q, g)):
            out_ref[j, :, cols] = dot(masked[h][j], value)


def owner_kernel(final, total_ref, *refs):
    got, (near_ref, far_ref, sum_ref, next_ref) = refs[: GROUP - 1], refs[-4:]
    position = lax.axis_index("seq")
    place = lax.rem(position, GROUP)
    share = total_ref.shape[1] // GROUP
    high = bit_of(position, 1)
    for e in range(share):
        mine, other = [], []
        for s in range(2):
            mine.append(total_ref[s, place * share + e] + got[0][s, e].astype(F32))
            other.append(got[1][s, e].astype(F32) + got[2][s, e].astype(F32))
        near_ref[e] = jnp.where(high, other[0], other[1]).astype(BF16)
        far_ref[e] = jnp.where(high, mine[1], mine[0]).astype(BF16)
        sums = [mine[s] + other[s] for s in range(2)]
        write_next(sums, e, 2, final, sum_ref, next_ref)


def write_next(sums, e, bit, final, sum_ref, next_ref):
    if final:
        value = jnp.where(bit_of(lax.axis_index("seq"), bit), sums[1], sums[0])
        next_ref[e] = value.astype(BF16)
        return
    for s in range(2):
        sum_ref[s, e] = sums[s]
        next_ref[s, e] = sums[s].astype(BF16)


def climb_kernel(bit, next_final, got_ref, old_ref, level_ref, sum_ref, next_ref):
    on = bit_of(lax.axis_index("seq"), bit)
    for e in range(got_ref.shape[1]):
        both = [got_ref[s, e].astype(F32) for s in range(2)]
        level_ref[e] = jnp.where(on, both[0], both[1]).astype(BF16)
        sums = [old_ref[s, e] + both[s] for s in range(2)]
        write_next(sums, e, bit + 1, next_final, sum_ref, next_ref)


def pair_block(first, second):
    zero = jnp.zeros(first.shape, BF16)
    top = jnp.concatenate([first.astype(BF16), zero], axis=1)
    bottom = jnp.concatenate([zero, second.astype(BF16)], axis=1)
    return jnp.concatenate([top, bottom], axis=0)


def finish_kernel(spans, heads, groups, weight_ref, g_ref, near_ref, *refs):
    chunks = len(spans)
    levels, refs = refs[: groups * GROUP], refs[groups * GROUP :]
    q_refs, refs = refs[:chunks], refs[chunks:]
    k_refs, refs = refs[:chunks], refs[chunks:]
    v_refs, refs = refs[:chunks], refs[chunks:]
    state_refs, refs = refs[:chunks], refs[chunks:]
    part_refs, refs = refs[:chunks], refs[chunks:]
    outs, (held, mix_ref, sems) = refs[:4], refs[4:]
    position = lax.axis_index("seq")
    place = lax.rem(position, GROUP)
    size = q_refs[0].shape[1] // heads
    share = heads // GROUP
    block = g_ref.shape[0]
    norm = 1.0 / math.sqrt(size * block)
    for m in range(GROUP):
        for e in range(share):
            h = (place ^ m) * share + e
            values = [near_ref[h]] + [levels[b * GROUP + m][e] for b in range(groups)]
            forward = backward = None
            for level, value in enumerate(values):
                coef = weight_ref[h, level + 1] * (1.0 / math.sqrt(size * block * 2**level))
                on = bit_of(position, level)
                value = value.astype(F32)
                to_forward = jnp.where(on, coef, 0.0) * value
                to_backward = jnp.where(on, 0.0, coef) * value
                forward = to_forward if forward is None else forward + to_forward
                backward = to_backward if backward is None else backward + to_backward
            mix_ref[0, h] = forward
            mix_ref[1, h] = backward
    copies = []
    for s in range(2):
        sums = [mix_ref[s, h] for h in range(heads)]
        for c in range(chunks) if s == 0 else reversed(range(chunks)):
            span = slice(*spans[c])
            weights = [pair_block(sums[h], sums[h + 1]) for h in range(0, heads, 2)]
            for j in (2 * s, 2 * s + 1):
                for h in range(0, heads, 2):
                    cols = slice(h * size, (h + 2) * size)
                    weight = weights[h // 2]
                    if j == 0:
                        term = dot(q_refs[c][:, cols], weight)
                    elif j == 1:
                        term = dot(g_ref[span, cols], weight, NT)
                    elif j == 2:
                        term = dot(v_refs[c][:, cols], weight, NT)
                    else:
                        term = dot(k_refs[c][:, cols], weight)
                    held[j, span, cols] = (term + part_refs[c][j, :, cols]).astype(BF16)
                copy = pltpu.make_async_copy(held.at[j, span], outs[j].at[span], sems.at[j, c])
                copy.start()
                copies.append(copy)
            sums = [
                total + weight_ref[h, 0] * norm * state_refs[c][s, h]
                for h, total in enumerate(sums)
            ]
    for copy in copies:
        copy.wait()


def exchange(totals, near, sends, local, late):
    depth = lax.axis_size("seq").bit_length() - 1
    heads, square = totals.shape[1], totals.shape[2:]
    share = heads // GROUP
    last = depth - 1

    def message(bit):
        return pltpu.VMEM((share, *square) if bit == last else (2, share, *square), BF16)

    def running(bit):
        return pltpu.VMEM((1, 8, 128) if bit == last else (2, share, *square), F32)

    def spread(mine, other):
        return [mine, *[swap(mine if m == 1 else other, "seq", m) for m in range(1, GROUP)]]

    one = pltpu.VMEM((share, *square), BF16)
    got = [swap(send, "seq", m) for m, send in enumerate(sends, 1)]
    fillers = [local(late[0], sends[0])]
    near = swap(tie(near, fillers[0]), "seq", 1)
    mine, other, sums, sent = call(
        functools.partial(owner_kernel, last == 2),
        [one, one, running(2), message(2)],
        [totals, *got, fillers[0]],
        [VMEM] * GROUP + [ANY],
        5 * 10**9,
    )
    levels = spread(mine, other)
    for bit in range(2, last):
        found, sums, sent = call(
            functools.partial(climb_kernel, bit, bit + 1 == last),
            [one, running(bit + 1), message(bit + 1)],
            [swap(sent, "seq", 1 << bit), sums],
            [VMEM] * 2,
            10**6,
        )
        levels += spread(found, found)
    found = tie(swap(sent, "seq", 1 << last), near)
    levels += spread(found, found)
    fillers += [local(c, found) for c in late[1:]]
    return near, levels, fillers


def per_device(inputs, w_qkv, level_weight, grad_out):
    rows, width = grad_out.shape
    heads = level_weight.shape[0]
    size = width // heads
    parts = lax.axis_size("head")
    edges = [rows * sum(SHARES[:c]) // sum(SHARES) for c in range(CHUNKS + 1)]
    spans = list(zip(edges[:-1], edges[1:]))
    copied = [(0, span) for span in spans]
    mine = load([inputs], copied[:1])
    mine = [*mine, *load([inputs], copied[1:], mine)]
    grads, weights = load([grad_out, w_qkv], [(0, None), (1, None)], mine[1:2])
    top, *lows = [1 << b for b in reversed(range(parts.bit_length() - 1))]
    arrived = [swap(piece, "head", top) for piece in mine]
    arrived[0] = tie(arrived[0], weights)
    whole = {0: inputs}
    for low in lows:
        for k in sorted(whole):
            whole[k | low] = swap(whole[k], "head", low)
    state = pltpu.VMEM((2, heads, size, size), F32)
    qs, ks, vs, states, locals_ = [], [], [], [], []

    def local(c, after):
        chunk = spans[c][1] - spans[c][0]
        return call(
            functools.partial(local_kernel, spans[c], heads),
            [pltpu.VMEM((4, chunk, width), F32)],
            [level_weight, qs[c], ks[c], vs[c], grads, after],
            [SMEM] + [VMEM] * 4 + [ANY],
            100 * chunk * chunk * width if c >= CHUNKS - 2 else 0,
        )[0]

    after = None
    for c in range(CHUNKS):
        pieces = {**whole, 0: mine[c]}
        pieces[top] = arrived[c] if after is None else tie(arrived[c], after)
        for low in lows:
            for k in [k for k in sorted(pieces) if k & top]:
                pieces[k | low] = swap(pieces[k], "head", low)
        keys = sorted(pieces)
        chunk = spans[c][1] - spans[c][0]
        flat = pltpu.VMEM((chunk, width), BF16)
        flops = 0
        if c < CHUNKS - 1:
            if c > 0:
                locals_.append(local(c - 1, pieces[top]))
            operands = [weights, grads, *[pieces[k] for k in keys], *locals_[-1:]]
            got = call(
                functools.partial(project_kernel, keys, spans[c], heads),
                [flat, flat, flat, state],
                operands,
                [VMEM] * (2 + len(keys)) + [ANY] * len(locals_[-1:]),
                flops * len(keys),
            )
        else:
            early, late = keys[:-1], keys[-1:]
            (begun,) = call(
                functools.partial(early_kernel, early, spans[c]),
                [pltpu.VMEM((3, chunk, width), F32)],
                [weights, *[pieces[k] for k in early]],
                [VMEM] * (1 + len(early)),
                flops * len(early),
            )
            operands = [weights, grads, begun, *[pieces[k] for k in late], *states]
            got = call(
                functools.partial(last_kernel, late, spans[c], heads),
                [
                    flat,
                    flat,
                    flat,
                    state,
                    state,
                    pltpu.VMEM((heads, size, size), BF16),
                    *[pltpu.VMEM((2, heads // GROUP, size, size), BF16)] * (GROUP - 1),
                ],
                operands,
                [VMEM] * len(operands),
                flops * len(late),
            )
        qs.append(got[0])
        ks.append(got[1])
        vs.append(got[2])
        states.append(got[3])
        after = got[3]
    near, levels, fillers = exchange(got[4], got[5], got[6:], local, range(len(locals_), CHUNKS))
    locals_ += fillers
    operands = [level_weight, grads, near, *levels, *qs, *ks, *vs, *states, *locals_]
    return call(
        functools.partial(finish_kernel, spans, heads, len(levels) // GROUP),
        [jax.ShapeDtypeStruct((rows, width), BF16)] * 4,
        operands,
        [SMEM] + [VMEM] * (len(operands) - 1),
        16 * rows * size * width,
        [
            pltpu.VMEM((4, rows, width), BF16),
            pltpu.VMEM((2, heads, size, size), F32),
            pltpu.SemaphoreType.DMA((4, CHUNKS)),
        ],
        [ANY] * 4,
        12,
    )


def solution(mesh):
    in_specs = (P("seq", "head"), P(None, None, "head"), P("head", None), P("seq", "head"))
    out_specs = (P("seq", "head"), P("seq", "head"), P("seq", "head"), P("seq", "head"))
    return jax.shard_map(
        per_device, mesh=mesh, in_specs=in_specs, out_specs=out_specs, check_vma=False
    )
```

```python
import functools
import math

import jax
import jax.numpy as jnp
from jax import lax
from jax.experimental import pallas as pl
from jax.experimental.pallas import tpu as pltpu
from jax.sharding import PartitionSpec as P

SHARES = (10, 12, 13, 14, 15)
CHUNKS = len(SHARES)
GROUP = 4
MIB = 2**20
VMEM = pl.BlockSpec(memory_space=pltpu.VMEM)
SMEM = pl.BlockSpec(memory_space=pltpu.SMEM)
ANY = pl.BlockSpec(memory_space=pl.ANY)
HBM = pl.BlockSpec(memory_space=pltpu.HBM)
NN = (((1,), (0,)), ((), ()))
NT = (((1,), (1,)), ((), ()))
TN = (((0,), (0,)), ((), ()))
BF16 = jnp.bfloat16
F32 = jnp.float32


def dot(a, b, dims=NN):
    return lax.dot_general(a, b, dims, preferred_element_type=F32)


def swap(value, axis, mask):
    pairs = [(source, source ^ mask) for source in range(lax.axis_size(axis))]
    return lax.ppermute(value, axis, pairs)


def bit_of(position, bit):
    return lax.rem(position // 2**bit, 2) == 1


def call(kernel, outs, operands, specs, flops, scratch=(), out_specs=None, limit=4, moved=0, aliases=()):
    return pl.pallas_call(
        kernel,
        out_shape=outs,
        in_specs=specs,
        out_specs=[VMEM] * len(outs) if out_specs is None else out_specs,
        scratch_shapes=scratch,
        input_output_aliases=dict(aliases),
        compiler_params=pltpu.CompilerParams(vmem_limit_bytes=limit * MIB),
        cost_estimate=pl.CostEstimate(flops=flops, bytes_accessed=moved, transcendentals=0),
    )(*operands)


def load_kernel(copied, *refs):
    count = 1 + max(source for source, _ in copied)
    sources, refs = refs[:count], refs[-len(copied) - 1 :]
    outs, sems = refs[:-1], refs[-1]
    copies = []
    for i, (source, start) in enumerate(copied):
        ref = sources[source]
        if start is not None:
            ref = ref.at[pl.ds(start, outs[i].shape[0])]
        copies.append(pltpu.make_async_copy(ref, outs[i], sems.at[i]))
    for copy in copies:
        copy.start()
    for copy in copies:
        copy.wait()


def load(sources, copied, after=()):
    shapes = []
    for source, span in copied:
        shape = sources[source].shape
        rows = shape[0] if span is None else span[1] - span[0]
        shapes.append(pltpu.VMEM((rows, *shape[1:]), BF16))
    copied = [(source, span if span is None else span[0]) for source, span in copied]
    return call(
        functools.partial(load_kernel, copied),
        shapes,
        [*[pltpu.with_memory_space_constraint(x, pltpu.HBM) for x in sources], *after],
        [HBM] * len(sources) + [ANY] * len(after),
        0,
        [pltpu.SemaphoreType.DMA((len(copied),))],
        limit=2,
        moved=4 * sum(math.prod(shape.shape) for shape in shapes),
    )


def tie_kernel(value_ref, *refs):
    del value_ref, refs


def tie(value, *after):
    return pl.pallas_call(
        tie_kernel,
        out_shape=pltpu.VMEM(value.shape, value.dtype),
        in_specs=[VMEM] + [ANY] * len(after),
        out_specs=VMEM,
        input_output_aliases={0: 0},
        compiler_params=pltpu.CompilerParams(vmem_limit_bytes=MIB),
    )(value, *after)


def project(w_ref, segments, j):
    me = lax.axis_index("head")
    parts = lax.axis_size("head")
    depth = w_ref.shape[1] // parts
    total = None
    for k, rows in segments:
        start = pl.multiple_of((me ^ k) * depth, depth)
        term = dot(rows, w_ref[j, pl.ds(start, depth), :])
        total = term if total is None else total + term
    return total


def read_segments(refs, keys, span):
    found = []
    for k, ref in zip(keys, refs):
        whole = ref.shape[0] != span[1] - span[0]
        found.append((k, ref[span[0] : span[1], :] if whole else ref[...]))
    return found


def early_kernel(keys, span, w_ref, *refs):
    segments, total_ref = refs[:-1], refs[-1]
    for j in range(3):
        total_ref[j] = project(w_ref, read_segments(segments, keys, span), j)


def project_kernel(keys, span, heads, w_ref, g_ref, *refs):
    segments, refs = refs[: len(keys)], refs[len(keys) :]
    q_ref, k_ref, v_ref, state_ref = refs[-4:]
    for j, out_ref in enumerate((q_ref, k_ref, v_ref)):
        out_ref[...] = project(w_ref, read_segments(segments, keys, span), j).astype(BF16)
    size = q_ref.shape[1] // heads
    for h in range(heads):
        cols = slice(h * size, (h + 1) * size)
        state_ref[0, h] = dot(k_ref[:, cols], v_ref[:, cols], TN)
        state_ref[1, h] = dot(q_ref[:, cols], g_ref[span[0] : span[1], cols], TN)


def last_kernel(keys, span, heads, w_ref, g_ref, part_ref, *refs):
    segments, refs = refs[: len(keys)], refs[len(keys) :]
    earlier, refs = refs[: -6 - (GROUP - 1)], refs[-6 - (GROUP - 1) :]
    q_ref, k_ref, v_ref, state_ref, total_ref, near_ref, *sends = refs
    for j, out_ref in enumerate((q_ref, k_ref, v_ref)):
        term = project(w_ref, read_segments(segments, keys, span), j)
        out_ref[...] = (part_ref[j] + term).astype(BF16)
    size = q_ref.shape[1] // heads
    share = heads // GROUP
    place = lax.rem(lax.axis_index("seq"), GROUP)
    for h in range(heads):
        cols = slice(h * size, (h + 1) * size)
        state_ref[0, h] = dot(k_ref[:, cols], v_ref[:, cols], TN)
        state_ref[1, h] = dot(q_ref[:, cols], g_ref[span[0] : span[1], cols], TN)
        for s in range(2):
            total = state_ref[s, h]
            for other in earlier:
                total = total + other[s, h]
            total_ref[s, h] = total
    for m, send in enumerate(sends, 1):
        for s in range(2):
            for e in range(share):
                send[s, e] = total_ref[s, (place ^ m) * share + e].astype(BF16)
    odd = bit_of(lax.axis_index("seq"), 0)
    for h in range(heads):
        near_ref[h] = jnp.where(odd, total_ref[1, h], total_ref[0, h]).astype(BF16)


def local_kernel(span, heads, weight_ref, q_ref, k_ref, v_ref, g_ref, after_ref, out_ref):
    rows = q_ref.shape[0]
    size = q_ref.shape[1] // heads
    norm = 1.0 / math.sqrt(size * g_ref.shape[0])
    at = lax.broadcasted_iota(jnp.int32, (rows, rows), 0)
    of = lax.broadcasted_iota(jnp.int32, (rows, rows), 1)
    columns = [slice(h * size, (h + 1) * size) for h in range(heads)]
    masked = []
    for h, cols in enumerate(columns):
        q, k, v = q_ref[:, cols], k_ref[:, cols], v_ref[:, cols]
        g = g_ref[span[0] : span[1], cols]
        scale = weight_ref[h, 0] * norm
        found = []
        for left, right, causal in (
            (q, k, at >= of),
            (g, v, at >= of),
            (v, g, of >= at),
            (k, q, of >= at),
        ):
            found.append(jnp.where(causal, dot(left, right, NT) * scale, 0.0).astype(BF16))
        masked.append(found)
    for h, cols in enumerate(columns):
        q, k, v = q_ref[:, cols], k_ref[:, cols], v_ref[:, cols]
        g = g_ref[span[0] : span[1], cols]
        for j, value in enumerate((v, k, q, g)):
            out_ref[j, :, cols] = dot(masked[h][j], value)


def owner_kernel(final, total_ref, *refs):
    got, (near_ref, far_ref, sum_ref, next_ref) = refs[: GROUP - 1], refs[-4:]
    position = lax.axis_index("seq")
    place = lax.rem(position, GROUP)
    share = total_ref.shape[1] // GROUP
    high = bit_of(position, 1)
    for e in range(share):
        mine, other = [], []
        for s in range(2):
            mine.append(total_ref[s, place * share + e] + got[0][s, e].astype(F32))
            other.append(got[1][s, e].astype(F32) + got[2][s, e].astype(F32))
        near_ref[e] = jnp.where(high, other[0], other[1]).astype(BF16)
        far_ref[e] = jnp.where(high, mine[1], mine[0]).astype(BF16)
        sums = [mine[s] + other[s] for s in range(2)]
        write_next(sums, e, 2, final, sum_ref, next_ref)


def write_next(sums, e, bit, final, sum_ref, next_ref):
    if final:
        value = jnp.where(bit_of(lax.axis_index("seq"), bit), sums[1], sums[0])
        next_ref[e] = value.astype(BF16)
        return
    for s in range(2):
        sum_ref[s, e] = sums[s]
        next_ref[s, e] = sums[s].astype(BF16)


def climb_kernel(bit, next_final, got_ref, old_ref, level_ref, sum_ref, next_ref):
    on = bit_of(lax.axis_index("seq"), bit)
    for e in range(got_ref.shape[1]):
        both = [got_ref[s, e].astype(F32) for s in range(2)]
        level_ref[e] = jnp.where(on, both[0], both[1]).astype(BF16)
        sums = [old_ref[s, e] + both[s] for s in range(2)]
        write_next(sums, e, bit + 1, next_final, sum_ref, next_ref)


def pair_block(first, second):
    zero = jnp.zeros(first.shape, BF16)
    top = jnp.concatenate([first.astype(BF16), zero], axis=1)
    bottom = jnp.concatenate([zero, second.astype(BF16)], axis=1)
    return jnp.concatenate([top, bottom], axis=0)


def finish_kernel(spans, heads, group, groups, weight_ref, g_ref, near_ref, *refs):
    chunks = len(spans)
    count = len(group)
    levels, refs = refs[: groups * count], refs[groups * count :]
    q_refs, refs = refs[:chunks], refs[chunks:]
    k_refs, refs = refs[:chunks], refs[chunks:]
    v_refs, refs = refs[:chunks], refs[chunks:]
    state_refs, refs = refs[:chunks], refs[chunks:]
    part_refs, refs = refs[:chunks], refs[chunks:]
    outs, (held, sems) = refs[-6:-2], refs[-2:]
    position = lax.axis_index("seq")
    place = lax.rem(position, GROUP)
    size = q_refs[0].shape[1] // heads
    share = heads // GROUP
    block = g_ref.shape[0]
    norm = 1.0 / math.sqrt(size * block)
    mine = [((place ^ m) * share + e, i, e) for i, m in enumerate(group) for e in range(share)]
    columns = [pl.ds(pl.multiple_of(h * size, size), size) for h, _, _ in mine]
    mixes = [[], []]
    for h, i, e in mine:
        values = [near_ref[h]] + [levels[b * count + i][e] for b in range(groups)]
        sums = [None, None]
        for level, value in enumerate(values):
            coef = weight_ref[h, level + 1] * (1.0 / math.sqrt(size * block * 2**level))
            on = bit_of(position, level)
            value = value.astype(F32)
            for s in range(2):
                term = (jnp.where(on, coef, 0.0) if s == 0 else jnp.where(on, 0.0, coef)) * value
                sums[s] = term if sums[s] is None else sums[s] + term
        for s in range(2):
            mixes[s].append(sums[s])
    copies = []
    for s in range(2):
        sums = mixes[s]
        for c in range(chunks) if s == 0 else reversed(range(chunks)):
            span = slice(*spans[c])
            for j in (2 * s, 2 * s + 1):
                for p in range(0, len(mine), 2):
                    weight = pair_block(sums[p], sums[p + 1])
                    both = columns[p : p + 2]
                    ref = (q_refs[c], g_ref, v_refs[c], k_refs[c])[j]
                    rows = span if j == 1 else slice(None)
                    left = jnp.concatenate([ref[rows, cols] for cols in both], axis=1)
                    term = dot(left, weight, NT if j in (1, 2) else NN)
                    for i, cols in enumerate(both):
                        value = term[:, i * size : (i + 1) * size] + part_refs[c][j, :, cols]
                        held[j, p + i, span] = value.astype(BF16)
            sums = [
                total + weight_ref[h, 0] * norm * state_refs[c][s, h]
                for (h, _, _), total in zip(mine, sums)
            ]
        for j in (2 * s, 2 * s + 1):
            for i, cols in enumerate(columns):
                copy = pltpu.make_async_copy(held.at[j, i], outs[j].at[:, cols], sems.at[j, i])
                copy.start()
                copies.append(copy)
    for copy in copies:
        copy.wait()


def exchange(totals, near, sends, local, late):
    depth = lax.axis_size("seq").bit_length() - 1
    heads, square = totals.shape[1], totals.shape[2:]
    share = heads // GROUP
    last = depth - 1

    def message(bit):
        return pltpu.VMEM((share, *square) if bit == last else (2, share, *square), BF16)

    def running(bit):
        return pltpu.VMEM((1, 8, 128) if bit == last else (2, share, *square), F32)

    def spread(mine, other):
        return [mine, *[swap(mine if m == 1 else other, "seq", m) for m in range(1, GROUP)]]

    one = pltpu.VMEM((share, *square), BF16)
    got = [swap(send, "seq", m) for m, send in enumerate(sends, 1)]
    fillers = [local(late[0], sends[0])]
    near = swap(tie(near, fillers[0]), "seq", 1)
    mine, other, sums, sent = call(
        functools.partial(owner_kernel, last == 2),
        [one, one, running(2), message(2)],
        [totals, *got, fillers[0]],
        [VMEM] * GROUP + [ANY],
        5 * 10**9,
    )
    levels = spread(mine, other)
    for bit in range(2, last):
        found, sums, sent = call(
            functools.partial(climb_kernel, bit, bit + 1 == last),
            [one, running(bit + 1), message(bit + 1)],
            [swap(sent, "seq", 1 << bit), sums],
            [VMEM] * 2,
            10**6,
        )
        levels += spread(found, found)
    found = tie(swap(sent, "seq", 1 << last), near)
    levels += spread(found, found)
    fillers += [local(c, found) for c in late[1:]]
    return near, levels, fillers


def per_device(inputs, w_qkv, level_weight, grad_out):
    rows, width = grad_out.shape
    heads = level_weight.shape[0]
    size = width // heads
    parts = lax.axis_size("head")
    edges = [rows * sum(SHARES[:c]) // sum(SHARES) for c in range(CHUNKS + 1)]
    spans = list(zip(edges[:-1], edges[1:]))
    copied = [(0, span) for span in spans]
    mine = load([inputs], copied[:1])
    mine = [*mine, *load([inputs], copied[1:], mine)]
    grads, weights = load([grad_out, w_qkv], [(0, None), (1, None)], mine[1:2])
    top, *lows = [1 << b for b in reversed(range(parts.bit_length() - 1))]
    arrived = [swap(piece, "head", top) for piece in mine]
    arrived[0] = tie(arrived[0], weights)
    whole = {0: inputs}
    for low in lows:
        for k in sorted(whole):
            whole[k | low] = swap(whole[k], "head", low)
    state = pltpu.VMEM((2, heads, size, size), F32)
    qs, ks, vs, states, locals_ = [], [], [], [], []

    def local(c, after):
        chunk = spans[c][1] - spans[c][0]
        return call(
            functools.partial(local_kernel, spans[c], heads),
            [pltpu.VMEM((4, chunk, width), F32)],
            [level_weight, qs[c], ks[c], vs[c], grads, after],
            [SMEM] + [VMEM] * 4 + [ANY],
            100 * chunk * chunk * width if c == CHUNKS - 2 else 0,
        )[0]

    after = None
    for c in range(CHUNKS):
        pieces = {**whole, 0: mine[c]}
        pieces[top] = arrived[c] if after is None else tie(arrived[c], after)
        for low in lows:
            for k in [k for k in sorted(pieces) if k & top]:
                pieces[k | low] = swap(pieces[k], "head", low)
        keys = sorted(pieces)
        chunk = spans[c][1] - spans[c][0]
        flat = pltpu.VMEM((chunk, width), BF16)
        flops = 0
        if c < CHUNKS - 1:
            if c > 0:
                locals_.append(local(c - 1, pieces[top]))
            operands = [weights, grads, *[pieces[k] for k in keys], *locals_[-1:]]
            got = call(
                functools.partial(project_kernel, keys, spans[c], heads),
                [flat, flat, flat, state],
                operands,
                [VMEM] * (2 + len(keys)) + [ANY] * len(locals_[-1:]),
                flops * len(keys),
            )
        else:
            early, late = keys[:-1], keys[-1:]
            (begun,) = call(
                functools.partial(early_kernel, early, spans[c]),
                [pltpu.VMEM((3, chunk, width), F32)],
                [weights, *[pieces[k] for k in early]],
                [VMEM] * (1 + len(early)),
                flops * len(early),
            )
            operands = [weights, grads, begun, *[pieces[k] for k in late], *states]
            got = call(
                functools.partial(last_kernel, late, spans[c], heads),
                [
                    flat,
                    flat,
                    flat,
                    state,
                    state,
                    pltpu.VMEM((heads, size, size), BF16),
                    *[pltpu.VMEM((2, heads // GROUP, size, size), BF16)] * (GROUP - 1),
                ],
                operands,
                [VMEM] * len(operands),
                flops * len(late),
            )
        qs.append(got[0])
        ks.append(got[1])
        vs.append(got[2])
        states.append(got[3])
        after = got[3]
    near, levels, fillers = exchange(got[4], got[5], got[6:], local, range(len(locals_), CHUNKS))
    locals_ += fillers
    shapes = [jax.ShapeDtypeStruct((rows, width), BF16)] * 4
    groups = len(levels) // GROUP
    written = []
    for group in ((0, 3), (2, 1)):
        found = [levels[b * GROUP + m] for b in range(groups) for m in group]
        operands = [level_weight, grads, near, *found, *qs, *ks, *vs, *states, *locals_]
        count = len(group) * heads // GROUP
        written = call(
            functools.partial(finish_kernel, spans, heads, group, groups),
            shapes,
            [*operands, *written, *levels[:-GROUP]],
            [SMEM] + [VMEM] * (len(operands) - 1) + [ANY] * (len(written) + len(levels) - GROUP),
            0,
            [
                pltpu.VMEM((4, count, rows, size), BF16),
                pltpu.SemaphoreType.DMA((4, count)),
            ],
            [ANY] * 4,
            12,
            aliases={len(operands) + j: j for j in range(len(written))},
        )
    return written


def solution(mesh):
    in_specs = (P("seq", "head"), P(None, None, "head"), P("head", None), P("seq", "head"))
    out_specs = (P("seq", "head"), P("seq", "head"), P("seq", "head"), P("seq", "head"))
    return jax.shard_map(
        per_device, mesh=mesh, in_specs=in_specs, out_specs=out_specs, check_vma=False
    )
```

```python
import functools
import math

import jax
import jax.numpy as jnp
from jax import lax
from jax.experimental import pallas as pl
from jax.experimental.pallas import tpu as pltpu
from jax.sharding import PartitionSpec as P

SHARES = (10, 12, 13, 14, 15)
CHUNKS = len(SHARES)
GROUP = 4
MIB = 2**20
VMEM = pl.BlockSpec(memory_space=pltpu.VMEM)
SMEM = pl.BlockSpec(memory_space=pltpu.SMEM)
ANY = pl.BlockSpec(memory_space=pl.ANY)
HBM = pl.BlockSpec(memory_space=pltpu.HBM)
NN = (((1,), (0,)), ((), ()))
NT = (((1,), (1,)), ((), ()))
TN = (((0,), (0,)), ((), ()))
BF16 = jnp.bfloat16
F32 = jnp.float32


def dot(a, b, dims=NN):
    return lax.dot_general(a, b, dims, preferred_element_type=F32)


def swap(value, axis, mask):
    pairs = [(source, source ^ mask) for source in range(lax.axis_size(axis))]
    return lax.ppermute(value, axis, pairs)


def bit_of(position, bit):
    return lax.rem(position // 2**bit, 2) == 1


def call(kernel, outs, operands, specs, flops, scratch=(), out_specs=None, limit=4, moved=0, aliases=()):
    return pl.pallas_call(
        kernel,
        out_shape=outs,
        in_specs=specs,
        out_specs=[VMEM] * len(outs) if out_specs is None else out_specs,
        scratch_shapes=scratch,
        input_output_aliases=dict(aliases),
        compiler_params=pltpu.CompilerParams(vmem_limit_bytes=limit * MIB),
        cost_estimate=pl.CostEstimate(flops=flops, bytes_accessed=moved, transcendentals=0),
    )(*operands)


def load_kernel(copied, *refs):
    count = 1 + max(source for source, _ in copied)
    sources, refs = refs[:count], refs[-len(copied) - 1 :]
    outs, sems = refs[:-1], refs[-1]
    copies = []
    for i, (source, start) in enumerate(copied):
        ref = sources[source]
        if start is not None:
            ref = ref.at[pl.ds(start, outs[i].shape[0])]
        copies.append(pltpu.make_async_copy(ref, outs[i], sems.at[i]))
    for copy in copies:
        copy.start()
    for copy in copies:
        copy.wait()


def load(sources, copied, after=()):
    shapes = []
    for source, span in copied:
        shape = sources[source].shape
        rows = shape[0] if span is None else span[1] - span[0]
        shapes.append(pltpu.VMEM((rows, *shape[1:]), BF16))
    copied = [(source, span if span is None else span[0]) for source, span in copied]
    return call(
        functools.partial(load_kernel, copied),
        shapes,
        [*[pltpu.with_memory_space_constraint(x, pltpu.HBM) for x in sources], *after],
        [HBM] * len(sources) + [ANY] * len(after),
        0,
        [pltpu.SemaphoreType.DMA((len(copied),))],
        limit=2,
        moved=4 * sum(math.prod(shape.shape) for shape in shapes),
    )


def tie_kernel(value_ref, *refs):
    del value_ref, refs


def tie(value, *after):
    return pl.pallas_call(
        tie_kernel,
        out_shape=pltpu.VMEM(value.shape, value.dtype),
        in_specs=[VMEM] + [ANY] * len(after),
        out_specs=VMEM,
        input_output_aliases={0: 0},
        compiler_params=pltpu.CompilerParams(vmem_limit_bytes=MIB),
    )(value, *after)


def project(w_ref, segments, j):
    me = lax.axis_index("head")
    parts = lax.axis_size("head")
    depth = w_ref.shape[1] // parts
    total = None
    for k, rows in segments:
        start = pl.multiple_of((me ^ k) * depth, depth)
        term = dot(rows, w_ref[j, pl.ds(start, depth), :])
        total = term if total is None else total + term
    return total


def read_segments(refs, keys, span):
    found = []
    for k, ref in zip(keys, refs):
        whole = ref.shape[0] != span[1] - span[0]
        found.append((k, ref[span[0] : span[1], :] if whole else ref[...]))
    return found


def early_kernel(keys, span, w_ref, *refs):
    segments, total_ref = refs[:-1], refs[-1]
    for j in range(3):
        total_ref[j] = project(w_ref, read_segments(segments, keys, span), j)


def project_kernel(keys, span, heads, w_ref, g_ref, *refs):
    segments, refs = refs[: len(keys)], refs[len(keys) :]
    q_ref, k_ref, v_ref, state_ref = refs[-4:]
    for j, out_ref in enumerate((q_ref, k_ref, v_ref)):
        out_ref[...] = project(w_ref, read_segments(segments, keys, span), j).astype(BF16)
    size = q_ref.shape[1] // heads
    for h in range(heads):
        cols = slice(h * size, (h + 1) * size)
        state_ref[0, h] = dot(k_ref[:, cols], v_ref[:, cols], TN)
        state_ref[1, h] = dot(q_ref[:, cols], g_ref[span[0] : span[1], cols], TN)


def last_kernel(keys, span, heads, w_ref, g_ref, part_ref, *refs):
    segments, refs = refs[: len(keys)], refs[len(keys) :]
    earlier, refs = refs[: -6 - (GROUP - 1)], refs[-6 - (GROUP - 1) :]
    q_ref, k_ref, v_ref, state_ref, total_ref, near_ref, *sends = refs
    for j, out_ref in enumerate((q_ref, k_ref, v_ref)):
        term = project(w_ref, read_segments(segments, keys, span), j)
        out_ref[...] = (part_ref[j] + term).astype(BF16)
    size = q_ref.shape[1] // heads
    share = heads // GROUP
    place = lax.rem(lax.axis_index("seq"), GROUP)
    for h in range(heads):
        cols = slice(h * size, (h + 1) * size)
        state_ref[0, h] = dot(k_ref[:, cols], v_ref[:, cols], TN)
        state_ref[1, h] = dot(q_ref[:, cols], g_ref[span[0] : span[1], cols], TN)
        for s in range(2):
            total = state_ref[s, h]
            for other in earlier:
                total = total + other[s, h]
            total_ref[s, h] = total
    for m, send in enumerate(sends, 1):
        for s in range(2):
            for e in range(share):
                send[s, e] = total_ref[s, (place ^ m) * share + e].astype(BF16)
    odd = bit_of(lax.axis_index("seq"), 0)
    for h in range(heads):
        near_ref[h] = jnp.where(odd, total_ref[1, h], total_ref[0, h]).astype(BF16)


def local_kernel(span, heads, weight_ref, q_ref, k_ref, v_ref, g_ref, after_ref, out_ref):
    rows = q_ref.shape[0]
    size = q_ref.shape[1] // heads
    norm = 1.0 / math.sqrt(size * g_ref.shape[0])
    at = lax.broadcasted_iota(jnp.int32, (rows, rows), 0)
    of = lax.broadcasted_iota(jnp.int32, (rows, rows), 1)
    columns = [slice(h * size, (h + 1) * size) for h in range(heads)]
    masked = []
    for h, cols in enumerate(columns):
        q, k, v = q_ref[:, cols], k_ref[:, cols], v_ref[:, cols]
        g = g_ref[span[0] : span[1], cols]
        scale = weight_ref[h, 0] * norm
        found = []
        for left, right, causal in (
            (q, k, at >= of),
            (g, v, at >= of),
            (v, g, of >= at),
            (k, q, of >= at),
        ):
            found.append(jnp.where(causal, dot(left, right, NT) * scale, 0.0).astype(BF16))
        masked.append(found)
    for h, cols in enumerate(columns):
        q, k, v = q_ref[:, cols], k_ref[:, cols], v_ref[:, cols]
        g = g_ref[span[0] : span[1], cols]
        for j, value in enumerate((v, k, q, g)):
            out_ref[j, :, cols] = dot(masked[h][j], value)


def owner_kernel(final, total_ref, *refs):
    got, (near_ref, far_ref, sum_ref, next_ref) = refs[: GROUP - 1], refs[-4:]
    position = lax.axis_index("seq")
    place = lax.rem(position, GROUP)
    share = total_ref.shape[1] // GROUP
    high = bit_of(position, 1)
    for e in range(share):
        mine, other = [], []
        for s in range(2):
            mine.append(total_ref[s, place * share + e] + got[0][s, e].astype(F32))
            other.append(got[1][s, e].astype(F32) + got[2][s, e].astype(F32))
        near_ref[e] = jnp.where(high, other[0], other[1]).astype(BF16)
        far_ref[e] = jnp.where(high, mine[1], mine[0]).astype(BF16)
        sums = [mine[s] + other[s] for s in range(2)]
        write_next(sums, e, 2, final, sum_ref, next_ref)


def write_next(sums, e, bit, final, sum_ref, next_ref):
    if final:
        value = jnp.where(bit_of(lax.axis_index("seq"), bit), sums[1], sums[0])
        next_ref[e] = value.astype(BF16)
        return
    for s in range(2):
        sum_ref[s, e] = sums[s]
        next_ref[s, e] = sums[s].astype(BF16)


def climb_kernel(bit, next_final, got_ref, old_ref, level_ref, sum_ref, next_ref):
    on = bit_of(lax.axis_index("seq"), bit)
    for e in range(got_ref.shape[1]):
        both = [got_ref[s, e].astype(F32) for s in range(2)]
        level_ref[e] = jnp.where(on, both[0], both[1]).astype(BF16)
        sums = [old_ref[s, e] + both[s] for s in range(2)]
        write_next(sums, e, bit + 1, next_final, sum_ref, next_ref)


def pair_block(first, second):
    zero = jnp.zeros(first.shape, BF16)
    top = jnp.concatenate([first.astype(BF16), zero], axis=1)
    bottom = jnp.concatenate([zero, second.astype(BF16)], axis=1)
    return jnp.concatenate([top, bottom], axis=0)


def gather_mixes(levels, first, side, weight_ref, block, mix_ref):
    position = lax.axis_index("seq")
    place = lax.rem(position, GROUP)
    heads, size = mix_ref.shape[:2]
    share = heads // GROUP
    for m in range(GROUP):
        for e in range(share):
            h = (place ^ m) * share + e
            total = None
            for b in range(len(levels) // GROUP):
                level = first + b
                coef = weight_ref[h, level + 1] * (1.0 / math.sqrt(size * block * 2**level))
                taken = bit_of(position, level)
                if side == 1:
                    taken = jnp.logical_not(taken)
                term = jnp.where(taken, coef, 0.0) * levels[b * GROUP + m][e].astype(F32)
                total = term if total is None else total + term
            mix_ref[h] = total


def write_side(spans, side, weight_of, q_refs, k_refs, v_refs, g_ref, part_refs, outs, held, sems):
    chunks = len(spans)
    size = held.shape[-1]
    copies = []
    for c in range(chunks) if side == 0 else reversed(range(chunks)):
        span = slice(*spans[c])
        weights = weight_of(c)
        for j in range(2):
            ref = (q_refs[c], g_ref, v_refs[c], k_refs[c])[2 * side + j]
            rows = span if ref is g_ref else slice(None)
            for p, weight in enumerate(weights):
                cols = slice(p * weight.shape[0], (p + 1) * weight.shape[0])
                term = dot(ref[rows, cols], weight, NT if 2 * side + j in (1, 2) else NN)
                held[j, span, cols] = (term + part_refs[c][2 * side + j, :, cols]).astype(BF16)
            copy = pltpu.make_async_copy(
                held.at[j, span], outs[2 * side + j].at[span], sems.at[j, c]
            )
            copy.start()
            copies.append(copy)
    for copy in copies:
        copy.wait()


def early_side_kernel(spans, heads, top, weight_ref, g_ref, near_ref, *refs):
    chunks = len(spans)
    levels, refs = refs[: (top - 1) * GROUP], refs[(top - 1) * GROUP :]
    q_refs, refs = refs[:chunks], refs[chunks:]
    k_refs, refs = refs[:chunks], refs[chunks:]
    v_refs, refs = refs[:chunks], refs[chunks:]
    state_refs, refs = refs[:chunks], refs[chunks:]
    part_refs, refs = refs[:chunks], refs[chunks:]
    outs, (base_ref, held, mix_ref, sems) = refs[:4], refs[4:]
    position = lax.axis_index("seq")
    block = g_ref.shape[0]
    size = mix_ref.shape[-1]
    norm = 1.0 / math.sqrt(size * block)

    def sums_of(side):
        gather_mixes(levels, 1, side, weight_ref, block, mix_ref)
        taken = bit_of(position, 0)
        if side == 1:
            taken = jnp.logical_not(taken)
        found = []
        for h in range(heads):
            coef = jnp.where(taken, weight_ref[h, 1] * norm, 0.0)
            found.append(mix_ref[h] + coef * near_ref[h].astype(F32))
        return found

    def add(sums, side, c):
        return [
            total + weight_ref[h, 0] * norm * state_refs[c][side, h] for h, total in enumerate(sums)
        ]

    for side in range(2):
        reached = bit_of(position, top)

        @pl.when(reached if side == 1 else jnp.logical_not(reached))
        def _():
            sums = [sums_of(side)]

            def weight_of(c):
                weights = [pair_block(*sums[0][h : h + 2]) for h in range(0, heads, 2)]
                sums[0] = add(sums[0], side, c)
                return weights

            write_side(
                spans, side, weight_of, q_refs, k_refs, v_refs, g_ref, part_refs, outs, held, sems
            )
            other = sums_of(1 - side)
            for c in range(chunks) if side == 1 else reversed(range(chunks)):
                for h in range(heads):
                    base_ref[c, h] = other[h]
                other = add(other, 1 - side, c)


def late_side_kernel(spans, heads, top, weight_ref, g_ref, base_ref, *refs):
    chunks = len(spans)
    levels, refs = refs[:GROUP], refs[GROUP:]
    q_refs, refs = refs[:chunks], refs[chunks:]
    k_refs, refs = refs[:chunks], refs[chunks:]
    v_refs, refs = refs[:chunks], refs[chunks:]
    part_refs, refs = refs[:chunks], refs[chunks:]
    outs, (held, mix_ref, sems) = refs[-7:-3], refs[-3:]
    block = g_ref.shape[0]
    reached = bit_of(lax.axis_index("seq"), top)
    for side in range(2):

        @pl.when(reached if side == 0 else jnp.logical_not(reached))
        def _():
            gather_mixes(levels, top, side, weight_ref, block, mix_ref)

            def weight_of(c):
                sums = [base_ref[c, h] + mix_ref[h] for h in range(heads)]
                return [pair_block(*sums[h : h + 2]) for h in range(0, heads, 2)]

            write_side(
                spans, side, weight_of, q_refs, k_refs, v_refs, g_ref, part_refs, outs, held, sems
            )


def exchange(totals, near, sends, local, late):
    depth = lax.axis_size("seq").bit_length() - 1
    heads, square = totals.shape[1], totals.shape[2:]
    share = heads // GROUP
    last = depth - 1

    def message(bit):
        return pltpu.VMEM((share, *square) if bit == last else (2, share, *square), BF16)

    def running(bit):
        return pltpu.VMEM((1, 8, 128) if bit == last else (2, share, *square), F32)

    def spread(mine, other):
        return [mine, *[swap(mine if m == 1 else other, "seq", m) for m in range(1, GROUP)]]

    one = pltpu.VMEM((share, *square), BF16)
    got = [swap(send, "seq", m) for m, send in enumerate(sends, 1)]
    fillers = [local(c, sends[0]) for c in late]
    near = swap(tie(near, *fillers), "seq", 1)
    mine, other, sums, sent = call(
        functools.partial(owner_kernel, last == 2),
        [one, one, running(2), message(2)],
        [totals, *got, *fillers],
        [VMEM] * GROUP + [ANY] * len(fillers),
        5 * 10**9,
    )
    levels = spread(mine, other)
    for bit in range(2, last):
        found, sums, sent = call(
            functools.partial(climb_kernel, bit, bit + 1 == last),
            [one, running(bit + 1), message(bit + 1)],
            [swap(sent, "seq", 1 << bit), sums],
            [VMEM] * 2,
            10**6,
        )
        levels += spread(found, found)
    found = tie(swap(sent, "seq", 1 << last), near)
    levels += spread(found, found)
    return near, levels, fillers


def per_device(inputs, w_qkv, level_weight, grad_out):
    rows, width = grad_out.shape
    heads = level_weight.shape[0]
    size = width // heads
    parts = lax.axis_size("head")
    edges = [rows * sum(SHARES[:c]) // sum(SHARES) for c in range(CHUNKS + 1)]
    spans = list(zip(edges[:-1], edges[1:]))
    copied = [(0, span) for span in spans]
    mine = load([inputs], copied[:1])
    mine = [*mine, *load([inputs], copied[1:], mine)]
    grads, weights = load([grad_out, w_qkv], [(0, None), (1, None)], mine[1:2])
    top, *lows = [1 << b for b in reversed(range(parts.bit_length() - 1))]
    arrived = [swap(piece, "head", top) for piece in mine]
    arrived[0] = tie(arrived[0], weights)
    whole = {0: inputs}
    for low in lows:
        for k in sorted(whole):
            whole[k | low] = swap(whole[k], "head", low)
    state = pltpu.VMEM((2, heads, size, size), F32)
    qs, ks, vs, states, locals_ = [], [], [], [], []

    def local(c, after):
        chunk = spans[c][1] - spans[c][0]
        return call(
            functools.partial(local_kernel, spans[c], heads),
            [pltpu.VMEM((4, chunk, width), F32)],
            [level_weight, qs[c], ks[c], vs[c], grads, after],
            [SMEM] + [VMEM] * 4 + [ANY],
            100 * chunk * chunk * width if c >= CHUNKS - 2 else 0,
        )[0]

    after = None
    for c in range(CHUNKS):
        pieces = {**whole, 0: mine[c]}
        pieces[top] = arrived[c] if after is None else tie(arrived[c], after)
        for low in lows:
            for k in [k for k in sorted(pieces) if k & top]:
                pieces[k | low] = swap(pieces[k], "head", low)
        keys = sorted(pieces)
        chunk = spans[c][1] - spans[c][0]
        flat = pltpu.VMEM((chunk, width), BF16)
        flops = 0
        if c < CHUNKS - 1:
            if c > 0:
                locals_.append(local(c - 1, pieces[top]))
            operands = [weights, grads, *[pieces[k] for k in keys], *locals_[-1:]]
            got = call(
                functools.partial(project_kernel, keys, spans[c], heads),
                [flat, flat, flat, state],
                operands,
                [VMEM] * (2 + len(keys)) + [ANY] * len(locals_[-1:]),
                flops * len(keys),
            )
        else:
            early, late = keys[:-1], keys[-1:]
            (begun,) = call(
                functools.partial(early_kernel, early, spans[c]),
                [pltpu.VMEM((3, chunk, width), F32)],
                [weights, *[pieces[k] for k in early]],
                [VMEM] * (1 + len(early)),
                flops * len(early),
            )
            operands = [weights, grads, begun, *[pieces[k] for k in late], *states]
            got = call(
                functools.partial(last_kernel, late, spans[c], heads),
                [
                    flat,
                    flat,
                    flat,
                    state,
                    state,
                    pltpu.VMEM((heads, size, size), BF16),
                    *[pltpu.VMEM((2, heads // GROUP, size, size), BF16)] * (GROUP - 1),
                ],
                operands,
                [VMEM] * len(operands),
                flops * len(late),
            )
        qs.append(got[0])
        ks.append(got[1])
        vs.append(got[2])
        states.append(got[3])
        after = got[3]
    near, levels, fillers = exchange(got[4], got[5], got[6:], local, range(len(locals_), CHUNKS))
    locals_ += fillers
    shapes = [jax.ShapeDtypeStruct((rows, width), BF16)] * 4
    top = len(levels) // GROUP
    flats = [*qs, *ks, *vs]
    scratch = [
        pltpu.VMEM((2, rows, width), BF16),
        pltpu.VMEM((heads, size, size), F32),
        pltpu.SemaphoreType.DMA((2, CHUNKS)),
    ]
    operands = [level_weight, grads, near, *levels[:-GROUP], *flats, *states, *locals_]
    *written, base = call(
        functools.partial(early_side_kernel, spans, heads, top),
        [*shapes, pltpu.VMEM((CHUNKS, heads, size, size), F32)],
        operands,
        [SMEM] + [VMEM] * (len(operands) - 1),
        0,
        scratch,
        [ANY] * 4 + [VMEM],
        8,
    )
    operands = [level_weight, grads, base, *levels[-GROUP:], *flats, *locals_]
    return call(
        functools.partial(late_side_kernel, spans, heads, top),
        shapes,
        [*operands, *written],
        [SMEM] + [VMEM] * (len(operands) - 1) + [ANY] * 4,
        0,
        scratch,
        [ANY] * 4,
        8,
        aliases={len(operands) + j: j for j in range(4)},
    )


def solution(mesh):
    in_specs = (P("seq", "head"), P(None, None, "head"), P("head", None), P("seq", "head"))
    out_specs = (P("seq", "head"), P("seq", "head"), P("seq", "head"), P("seq", "head"))
    return jax.shard_map(
        per_device, mesh=mesh, in_specs=in_specs, out_specs=out_specs, check_vma=False
    )
```

```python
import functools
import math

import jax
import jax.numpy as jnp
from jax import lax
from jax.experimental import pallas as pl
from jax.experimental.pallas import tpu as pltpu
from jax.sharding import PartitionSpec as P

SHARES = (10, 12, 13, 14, 15)
CHUNKS = len(SHARES)
GROUP = 4
MIB = 2**20
VMEM = pl.BlockSpec(memory_space=pltpu.VMEM)
SMEM = pl.BlockSpec(memory_space=pltpu.SMEM)
ANY = pl.BlockSpec(memory_space=pl.ANY)
HBM = pl.BlockSpec(memory_space=pltpu.HBM)
NN = (((1,), (0,)), ((), ()))
NT = (((1,), (1,)), ((), ()))
TN = (((0,), (0,)), ((), ()))
BF16 = jnp.bfloat16
F32 = jnp.float32


def dot(a, b, dims=NN):
    return lax.dot_general(a, b, dims, preferred_element_type=F32)


def swap(value, axis, mask):
    pairs = [(source, source ^ mask) for source in range(lax.axis_size(axis))]
    return lax.ppermute(value, axis, pairs)


def bit_of(position, bit):
    return lax.rem(position // 2**bit, 2) == 1


def call(kernel, outs, operands, specs, flops, scratch=(), out_specs=None, limit=4, moved=0, aliases=()):
    return pl.pallas_call(
        kernel,
        out_shape=outs,
        in_specs=specs,
        out_specs=[VMEM] * len(outs) if out_specs is None else out_specs,
        scratch_shapes=scratch,
        input_output_aliases=dict(aliases),
        compiler_params=pltpu.CompilerParams(vmem_limit_bytes=limit * MIB),
        cost_estimate=pl.CostEstimate(flops=flops, bytes_accessed=moved, transcendentals=0),
    )(*operands)


def load_kernel(copied, *refs):
    count = 1 + max(source for source, _ in copied)
    sources, refs = refs[:count], refs[-len(copied) - 1 :]
    outs, sems = refs[:-1], refs[-1]
    copies = []
    for i, (source, start) in enumerate(copied):
        ref = sources[source]
        if start is not None:
            ref = ref.at[pl.ds(start, outs[i].shape[0])]
        copies.append(pltpu.make_async_copy(ref, outs[i], sems.at[i]))
    for copy in copies:
        copy.start()
    for copy in copies:
        copy.wait()


def load(sources, copied, after=()):
    shapes = []
    for source, span in copied:
        shape = sources[source].shape
        rows = shape[0] if span is None else span[1] - span[0]
        shapes.append(pltpu.VMEM((rows, *shape[1:]), BF16))
    copied = [(source, span if span is None else span[0]) for source, span in copied]
    return call(
        functools.partial(load_kernel, copied),
        shapes,
        [*[pltpu.with_memory_space_constraint(x, pltpu.HBM) for x in sources], *after],
        [HBM] * len(sources) + [ANY] * len(after),
        0,
        [pltpu.SemaphoreType.DMA((len(copied),))],
        limit=2,
        moved=4 * sum(math.prod(shape.shape) for shape in shapes),
    )


def tie_kernel(value_ref, *refs):
    del value_ref, refs


def tie(value, *after, flops=0):
    return pl.pallas_call(
        tie_kernel,
        out_shape=pltpu.VMEM(value.shape, value.dtype),
        in_specs=[VMEM] + [ANY] * len(after),
        out_specs=VMEM,
        input_output_aliases={0: 0},
        compiler_params=pltpu.CompilerParams(vmem_limit_bytes=MIB),
        cost_estimate=pl.CostEstimate(flops=flops, bytes_accessed=0, transcendentals=0),
    )(value, *after)


def project(w_ref, segments, j):
    me = lax.axis_index("head")
    parts = lax.axis_size("head")
    depth = w_ref.shape[1] // parts
    total = None
    for k, rows in segments:
        start = pl.multiple_of((me ^ k) * depth, depth)
        term = dot(rows, w_ref[j, pl.ds(start, depth), :])
        total = term if total is None else total + term
    return total


def read_segments(refs, keys, span):
    found = []
    for k, ref in zip(keys, refs):
        whole = ref.shape[0] != span[1] - span[0]
        found.append((k, ref[span[0] : span[1], :] if whole else ref[...]))
    return found


def early_kernel(keys, span, w_ref, *refs):
    segments, total_ref = refs[:-1], refs[-1]
    for j in range(3):
        total_ref[j] = project(w_ref, read_segments(segments, keys, span), j)


def project_kernel(keys, span, heads, w_ref, g_ref, *refs):
    segments, refs = refs[: len(keys)], refs[len(keys) :]
    q_ref, k_ref, v_ref, state_ref = refs[-4:]
    for j, out_ref in enumerate((q_ref, k_ref, v_ref)):
        out_ref[...] = project(w_ref, read_segments(segments, keys, span), j).astype(BF16)
    size = q_ref.shape[1] // heads
    for h in range(heads):
        cols = slice(h * size, (h + 1) * size)
        state_ref[0, h] = dot(k_ref[:, cols], v_ref[:, cols], TN)
        state_ref[1, h] = dot(q_ref[:, cols], g_ref[span[0] : span[1], cols], TN)


def last_kernel(keys, span, heads, w_ref, g_ref, part_ref, *refs):
    segments, refs = refs[: len(keys)], refs[len(keys) :]
    earlier, refs = refs[: -5 - (GROUP - 1)], refs[-5 - (GROUP - 1) :]
    q_ref, k_ref, v_ref, state_ref, total_ref, *sends = refs
    for j, out_ref in enumerate((q_ref, k_ref, v_ref)):
        term = project(w_ref, read_segments(segments, keys, span), j)
        out_ref[...] = (part_ref[j] + term).astype(BF16)
    size = q_ref.shape[1] // heads
    share = heads // GROUP
    place = lax.rem(lax.axis_index("seq"), GROUP)
    for h in range(heads):
        cols = slice(h * size, (h + 1) * size)
        state_ref[0, h] = dot(k_ref[:, cols], v_ref[:, cols], TN)
        state_ref[1, h] = dot(q_ref[:, cols], g_ref[span[0] : span[1], cols], TN)
        for s in range(2):
            total = state_ref[s, h]
            for other in earlier:
                total = total + other[s, h]
            total_ref[s, h] = total
    for m, send in enumerate(sends, 1):
        for s in range(2):
            for e in range(share):
                send[s, e] = total_ref[s, (place ^ m) * share + e].astype(BF16)


def local_kernel(span, heads, weight_ref, q_ref, k_ref, v_ref, g_ref, after_ref, out_ref):
    rows = q_ref.shape[0]
    size = q_ref.shape[1] // heads
    norm = 1.0 / math.sqrt(size * g_ref.shape[0])
    at = lax.broadcasted_iota(jnp.int32, (rows, rows), 0)
    of = lax.broadcasted_iota(jnp.int32, (rows, rows), 1)
    columns = [slice(h * size, (h + 1) * size) for h in range(heads)]
    masked = []
    for h, cols in enumerate(columns):
        q, k, v = q_ref[:, cols], k_ref[:, cols], v_ref[:, cols]
        g = g_ref[span[0] : span[1], cols]
        scale = weight_ref[h, 0] * norm
        found = []
        for left, right, causal in (
            (q, k, at >= of),
            (g, v, at >= of),
            (v, g, of >= at),
            (k, q, of >= at),
        ):
            found.append(jnp.where(causal, dot(left, right, NT) * scale, 0.0).astype(BF16))
        masked.append(found)
    for h, cols in enumerate(columns):
        q, k, v = q_ref[:, cols], k_ref[:, cols], v_ref[:, cols]
        g = g_ref[span[0] : span[1], cols]
        for j, value in enumerate((v, k, q, g)):
            out_ref[j, :, cols] = dot(masked[h][j], value)


def owner_kernel(final, total_ref, *refs):
    got, refs = refs[: GROUP - 1], refs[GROUP - 1 :]
    near_ref, far_ref, *nexts = refs[-3 if final else -4 :]
    position = lax.axis_index("seq")
    place = lax.rem(position, GROUP)
    heads = total_ref.shape[1]
    share = heads // GROUP
    odd, high = bit_of(position, 0), bit_of(position, 1)
    for e in range(share):
        mine, other = [], []
        for s in range(2):
            mine.append(total_ref[s, place * share + e] + got[0][s, e].astype(F32))
            other.append(got[1][s, e].astype(F32) + got[2][s, e].astype(F32))
        sums = [mine[s] + other[s] for s in range(2)]
        write_next(sums, e, 2, final, *nexts)
        near_ref[e] = jnp.where(high, other[0], other[1]).astype(BF16)
        far_ref[e] = jnp.where(high, mine[1], mine[0]).astype(BF16)
    for h in range(heads):
        near_ref[share + h] = jnp.where(odd, total_ref[1, h], total_ref[0, h]).astype(BF16)


def write_next(sums, e, bit, final, next_ref, sum_ref=None):
    if final:
        value = jnp.where(bit_of(lax.axis_index("seq"), bit), sums[1], sums[0])
        next_ref[e] = value.astype(BF16)
        return
    for s in range(2):
        sum_ref[s, e] = sums[s]
        next_ref[s, e] = sums[s].astype(BF16)


def climb_kernel(bit, next_final, got_ref, old_ref, level_ref, *nexts):
    on = bit_of(lax.axis_index("seq"), bit)
    for e in range(got_ref.shape[1]):
        both = [got_ref[s, e].astype(F32) for s in range(2)]
        level_ref[e] = jnp.where(on, both[0], both[1]).astype(BF16)
        sums = [old_ref[s, e] + both[s] for s in range(2)]
        write_next(sums, e, bit + 1, next_final, *nexts)


def pair_block(first, second):
    zero = jnp.zeros(first.shape, BF16)
    top = jnp.concatenate([first.astype(BF16), zero], axis=1)
    bottom = jnp.concatenate([zero, second.astype(BF16)], axis=1)
    return jnp.concatenate([top, bottom], axis=0)


def gather_mixes(levels, first, side, weight_ref, block, mix_ref):
    position = lax.axis_index("seq")
    place = lax.rem(position, GROUP)
    heads, size = mix_ref.shape[:2]
    share = heads // GROUP
    for m in range(GROUP):
        for e in range(share):
            h = (place ^ m) * share + e
            total = None
            for b in range(len(levels) // GROUP):
                level = first + b
                coef = weight_ref[h, level + 1] * (1.0 / math.sqrt(size * block * 2**level))
                taken = bit_of(position, level)
                if side == 1:
                    taken = jnp.logical_not(taken)
                term = jnp.where(taken, coef, 0.0) * levels[b * GROUP + m][e].astype(F32)
                total = term if total is None else total + term
            mix_ref[h] = total


def write_side(spans, side, weight_of, q_refs, k_refs, v_refs, g_ref, part_refs, outs, held, sems):
    chunks = len(spans)
    size = held.shape[-1]
    copies = []
    for c in range(chunks) if side == 0 else reversed(range(chunks)):
        span = slice(*spans[c])
        weights = weight_of(c)
        for j in range(2):
            ref = (q_refs[c], g_ref, v_refs[c], k_refs[c])[2 * side + j]
            rows = span if ref is g_ref else slice(None)
            for p, weight in enumerate(weights):
                cols = slice(p * weight.shape[0], (p + 1) * weight.shape[0])
                term = dot(ref[rows, cols], weight, NT if 2 * side + j in (1, 2) else NN)
                held[j, span, cols] = (term + part_refs[c][2 * side + j, :, cols]).astype(BF16)
            copy = pltpu.make_async_copy(
                held.at[j, span], outs[2 * side + j].at[span], sems.at[j, c]
            )
            copy.start()
            copies.append(copy)
    for copy in copies:
        copy.wait()


def early_side_kernel(spans, heads, top, weight_ref, g_ref, *refs):
    chunks = len(spans)
    levels, refs = refs[: (top - 1) * GROUP], refs[(top - 1) * GROUP :]
    q_refs, refs = refs[:chunks], refs[chunks:]
    k_refs, refs = refs[:chunks], refs[chunks:]
    v_refs, refs = refs[:chunks], refs[chunks:]
    state_refs, refs = refs[:chunks], refs[chunks:]
    part_refs, refs = refs[:chunks], refs[chunks:]
    outs, (base_ref, held, mix_ref, sems) = refs[:4], refs[4:]
    position = lax.axis_index("seq")
    block = g_ref.shape[0]
    size = mix_ref.shape[-1]
    norm = 1.0 / math.sqrt(size * block)

    def sums_of(side):
        gather_mixes(levels, 1, side, weight_ref, block, mix_ref)
        taken = bit_of(position, 0)
        if side == 1:
            taken = jnp.logical_not(taken)
        found = []
        for h in range(heads):
            coef = jnp.where(taken, weight_ref[h, 1] * norm, 0.0)
            found.append(mix_ref[h] + coef * levels[1][heads // GROUP + h].astype(F32))
        return found

    def add(sums, side, c):
        return [
            total + weight_ref[h, 0] * norm * state_refs[c][side, h] for h, total in enumerate(sums)
        ]

    for side in range(2):
        reached = bit_of(position, top)

        @pl.when(reached if side == 1 else jnp.logical_not(reached))
        def _():
            sums = [sums_of(side)]

            def weight_of(c):
                weights = [pair_block(*sums[0][h : h + 2]) for h in range(0, heads, 2)]
                sums[0] = add(sums[0], side, c)
                return weights

            write_side(
                spans, side, weight_of, q_refs, k_refs, v_refs, g_ref, part_refs, outs, held, sems
            )
            other = sums_of(1 - side)
            for c in range(chunks) if side == 1 else reversed(range(chunks)):
                for h in range(heads):
                    base_ref[c, h] = other[h]
                other = add(other, 1 - side, c)


def late_side_kernel(spans, heads, top, weight_ref, g_ref, base_ref, *refs):
    chunks = len(spans)
    levels, refs = refs[:GROUP], refs[GROUP:]
    q_refs, refs = refs[:chunks], refs[chunks:]
    k_refs, refs = refs[:chunks], refs[chunks:]
    v_refs, refs = refs[:chunks], refs[chunks:]
    part_refs, refs = refs[:chunks], refs[chunks:]
    outs, (held, mix_ref, sems) = refs[-7:-3], refs[-3:]
    block = g_ref.shape[0]
    reached = bit_of(lax.axis_index("seq"), top)
    for side in range(2):

        @pl.when(reached if side == 0 else jnp.logical_not(reached))
        def _():
            gather_mixes(levels, top, side, weight_ref, block, mix_ref)

            def weight_of(c):
                sums = [base_ref[c, h] + mix_ref[h] for h in range(heads)]
                return [pair_block(*sums[h : h + 2]) for h in range(0, heads, 2)]

            write_side(
                spans, side, weight_of, q_refs, k_refs, v_refs, g_ref, part_refs, outs, held, sems
            )


def exchange(totals, sends, local, late):
    depth = lax.axis_size("seq").bit_length() - 1
    heads, square = totals.shape[1], totals.shape[2:]
    share = heads // GROUP
    last = depth - 1

    def nexts(bit):
        if bit == last:
            return [pltpu.VMEM((share, *square), BF16)]
        return [pltpu.VMEM((2, share, *square), BF16), pltpu.VMEM((2, share, *square), F32)]

    def spread(mine, other):
        return [mine, *[swap(mine if m == 1 else other, "seq", m) for m in range(1, GROUP)]]

    one = pltpu.VMEM((share, *square), BF16)
    got = [swap(send, "seq", m) for m, send in enumerate(sends, 1)]
    fillers = [local(c, sends[0]) for c in late]
    mine, other, sent, *sums = call(
        functools.partial(owner_kernel, last == 2),
        [pltpu.VMEM((share + heads, *square), BF16), one, *nexts(2)],
        [totals, *got, *fillers],
        [VMEM] * GROUP + [ANY] * len(fillers),
        10**6,
    )
    levels = spread(mine, other)
    for bit in range(2, last):
        found, sent, *sums = call(
            functools.partial(climb_kernel, bit, bit + 1 == last),
            [one, *nexts(bit + 1)],
            [swap(sent, "seq", 1 << bit), *sums],
            [VMEM] * 2,
            10**6,
        )
        levels += spread(found, found)
    found = tie(swap(sent, "seq", 1 << last), mine, flops=12 * 10**8)
    levels += spread(found, found)
    return levels, fillers


def per_device(inputs, w_qkv, level_weight, grad_out):
    rows, width = grad_out.shape
    heads = level_weight.shape[0]
    size = width // heads
    parts = lax.axis_size("head")
    edges = [rows * sum(SHARES[:c]) // sum(SHARES) for c in range(CHUNKS + 1)]
    spans = list(zip(edges[:-1], edges[1:]))
    copied = [(0, span) for span in spans]
    mine = load([inputs], copied[:1])
    mine = [*mine, *load([inputs], copied[1:], mine)]
    grads, weights = load([grad_out, w_qkv], [(0, None), (1, None)], mine[1:2])
    top, *lows = [1 << b for b in reversed(range(parts.bit_length() - 1))]
    arrived = [swap(piece, "head", top) for piece in mine]
    arrived[0] = tie(arrived[0], weights)
    whole = {0: inputs}
    for low in lows:
        for k in sorted(whole):
            whole[k | low] = swap(whole[k], "head", low)
    state = pltpu.VMEM((2, heads, size, size), F32)
    qs, ks, vs, states, locals_ = [], [], [], [], []

    def local(c, after):
        chunk = spans[c][1] - spans[c][0]
        return call(
            functools.partial(local_kernel, spans[c], heads),
            [pltpu.VMEM((4, chunk, width), F32)],
            [level_weight, qs[c], ks[c], vs[c], grads, after],
            [SMEM] + [VMEM] * 4 + [ANY],
            100 * chunk * chunk * width if c >= CHUNKS - 2 else 0,
        )[0]

    after = None
    for c in range(CHUNKS):
        pieces = {**whole, 0: mine[c]}
        pieces[top] = arrived[c] if after is None else tie(arrived[c], after)
        for low in lows:
            for k in [k for k in sorted(pieces) if k & top]:
                pieces[k | low] = swap(pieces[k], "head", low)
        keys = sorted(pieces)
        chunk = spans[c][1] - spans[c][0]
        flat = pltpu.VMEM((chunk, width), BF16)
        flops = 0
        if c < CHUNKS - 1:
            if c > 0:
                locals_.append(local(c - 1, pieces[top]))
            operands = [weights, grads, *[pieces[k] for k in keys], *locals_[-1:]]
            got = call(
                functools.partial(project_kernel, keys, spans[c], heads),
                [flat, flat, flat, state],
                operands,
                [VMEM] * (2 + len(keys)) + [ANY] * len(locals_[-1:]),
                flops * len(keys),
            )
        else:
            early, late = keys[:-1], keys[-1:]
            (begun,) = call(
                functools.partial(early_kernel, early, spans[c]),
                [pltpu.VMEM((3, chunk, width), F32)],
                [weights, *[pieces[k] for k in early]],
                [VMEM] * (1 + len(early)),
                flops * len(early),
            )
            operands = [weights, grads, begun, *[pieces[k] for k in late], *states]
            got = call(
                functools.partial(last_kernel, late, spans[c], heads),
                [
                    flat,
                    flat,
                    flat,
                    state,
                    state,
                    *[pltpu.VMEM((2, heads // GROUP, size, size), BF16)] * (GROUP - 1),
                ],
                operands,
                [VMEM] * len(operands),
                flops * len(late),
            )
        qs.append(got[0])
        ks.append(got[1])
        vs.append(got[2])
        states.append(got[3])
        after = got[3]
    levels, fillers = exchange(got[4], got[5:], local, range(len(locals_), CHUNKS))
    locals_ += fillers
    shapes = [jax.ShapeDtypeStruct((rows, width), BF16)] * 4
    top = len(levels) // GROUP
    flats = [*qs, *ks, *vs]
    scratch = [
        pltpu.VMEM((2, rows, width), BF16),
        pltpu.VMEM((heads, size, size), F32),
        pltpu.SemaphoreType.DMA((2, CHUNKS)),
    ]
    operands = [level_weight, grads, *levels[:-GROUP], *flats, *states, *locals_]
    *written, base = call(
        functools.partial(early_side_kernel, spans, heads, top),
        [*shapes, pltpu.VMEM((CHUNKS, heads, size, size), F32)],
        operands,
        [SMEM] + [VMEM] * (len(operands) - 1),
        0,
        scratch,
        [ANY] * 4 + [VMEM],
        8,
    )
    operands = [level_weight, grads, base, *levels[-GROUP:], *flats, *locals_]
    return call(
        functools.partial(late_side_kernel, spans, heads, top),
        shapes,
        [*operands, *written],
        [SMEM] + [VMEM] * (len(operands) - 1) + [ANY] * 4,
        0,
        scratch,
        [ANY] * 4,
        8,
        aliases={len(operands) + j: j for j in range(4)},
    )


def solution(mesh):
    in_specs = (P("seq", "head"), P(None, None, "head"), P("head", None), P("seq", "head"))
    out_specs = (P("seq", "head"), P("seq", "head"), P("seq", "head"), P("seq", "head"))
    return jax.shard_map(
        per_device, mesh=mesh, in_specs=in_specs, out_specs=out_specs, check_vma=False
    )
```

```python
import functools
import math

import jax
import jax.numpy as jnp
from jax import lax
from jax.experimental import pallas as pl
from jax.experimental.pallas import tpu as pltpu
from jax.sharding import PartitionSpec as P

SHARES = (10, 12, 13, 14, 15)
CHUNKS = len(SHARES)
GROUP = 4
MIB = 2**20
VMEM = pl.BlockSpec(memory_space=pltpu.VMEM)
SMEM = pl.BlockSpec(memory_space=pltpu.SMEM)
ANY = pl.BlockSpec(memory_space=pl.ANY)
HBM = pl.BlockSpec(memory_space=pltpu.HBM)
NN = (((1,), (0,)), ((), ()))
NT = (((1,), (1,)), ((), ()))
TN = (((0,), (0,)), ((), ()))
BF16 = jnp.bfloat16
F32 = jnp.float32


def dot(a, b, dims=NN):
    return lax.dot_general(a, b, dims, preferred_element_type=F32)


def swap(value, axis, mask):
    pairs = [(source, source ^ mask) for source in range(lax.axis_size(axis))]
    return lax.ppermute(value, axis, pairs)


def bit_of(position, bit):
    return lax.rem(position // 2**bit, 2) == 1


def call(kernel, outs, operands, specs, flops, scratch=(), out_specs=None, limit=4, moved=0, aliases=()):
    return pl.pallas_call(
        kernel,
        out_shape=outs,
        in_specs=specs,
        out_specs=[VMEM] * len(outs) if out_specs is None else out_specs,
        scratch_shapes=scratch,
        input_output_aliases=dict(aliases),
        compiler_params=pltpu.CompilerParams(vmem_limit_bytes=limit * MIB),
        cost_estimate=pl.CostEstimate(flops=flops, bytes_accessed=moved, transcendentals=0),
    )(*operands)


def load_kernel(spans, x_ref, *refs):
    outs, sems = refs[-len(spans) - 1 : -1], refs[-1]
    copies = []
    for i, (first, last) in enumerate(spans):
        rows = x_ref.at[pl.ds(first, last - first)]
        copies.append(pltpu.make_async_copy(rows, outs[i], sems.at[i]))
    for copy in copies:
        copy.start()
    for copy in copies:
        copy.wait()


def load(source, spans, after=()):
    return call(
        functools.partial(load_kernel, spans),
        [pltpu.VMEM((last - first, *source.shape[1:]), BF16) for first, last in spans],
        [pltpu.with_memory_space_constraint(source, pltpu.HBM), *after],
        [HBM] + [ANY] * len(after),
        0,
        [pltpu.SemaphoreType.DMA((len(spans),))],
        limit=2,
        moved=4 * source.size,
    )


def load_weights_kernel(parts, g_ref, w_ref, after_ref, g_out, w_out, sems):
    me = lax.axis_index("head")
    depth = w_ref.shape[1] // parts
    width = w_ref.shape[2]
    copies = [pltpu.make_async_copy(g_ref, g_out, sems.at[3 * parts])]
    for k in range(parts):
        rows = pl.ds(pl.multiple_of((me ^ k) * depth, depth), depth)
        for j in range(3):
            copies.append(
                pltpu.make_async_copy(
                    w_ref.at[j, rows],
                    w_out.at[pl.ds(k * depth, depth), pl.ds(j * width, width)],
                    sems.at[3 * k + j],
                )
            )
    for copy in copies:
        copy.start()
    for copy in copies:
        copy.wait()


def tie_kernel(value_ref, *refs):
    del value_ref, refs


def tie(value, *after, flops=0):
    return pl.pallas_call(
        tie_kernel,
        out_shape=pltpu.VMEM(value.shape, value.dtype),
        in_specs=[VMEM] + [ANY] * len(after),
        out_specs=VMEM,
        input_output_aliases={0: 0},
        compiler_params=pltpu.CompilerParams(vmem_limit_bytes=MIB),
        cost_estimate=pl.CostEstimate(flops=flops, bytes_accessed=0, transcendentals=0),
    )(value, *after)


def beside(refs, span):
    count = span[1] - span[0]
    found = [ref[...] if ref.shape[0] == count else ref[span[0] : span[1], :] for ref in refs]
    return found[0] if len(found) == 1 else jnp.concatenate(found, axis=1)


def write_states(span, heads, q_ref, k_ref, v_ref, g_ref, state_ref):
    size = q_ref.shape[1] // heads
    for h in range(heads):
        cols = slice(h * size, (h + 1) * size)
        state_ref[0, h] = dot(k_ref[:, cols], v_ref[:, cols], TN)
        state_ref[1, h] = dot(q_ref[:, cols], g_ref[span[0] : span[1], cols], TN)


def early_kernel(span, count, w_ref, *refs):
    segments, states = refs[:count], refs[count:-2]
    total_ref, sum_ref = refs[-2:]
    rows = beside(segments, span)
    total_ref[...] = dot(rows, w_ref[: rows.shape[1], :])
    sums = states[0][...]
    for state in states[1:]:
        sums = sums + state[...]
    sum_ref[...] = sums


def project_kernel(span, count, heads, w_ref, g_ref, *refs):
    outs, state_ref = refs[-4:-1], refs[-1]
    width = outs[0].shape[1]
    total = dot(beside(refs[:count], span), w_ref[...])
    for j, out_ref in enumerate(outs):
        out_ref[...] = total[:, j * width : (j + 1) * width].astype(BF16)
    write_states(span, heads, *outs, g_ref, state_ref)


def last_kernel(span, heads, w_ref, g_ref, part_ref, sum_ref, late_ref, *refs):
    outs, state_ref, total_ref, sends = refs[:3], refs[3], refs[4], refs[5:]
    width = outs[0].shape[1]
    start = w_ref.shape[0] - late_ref.shape[1]
    total = part_ref[...] + dot(late_ref[...], w_ref[start:, :])
    for j, out_ref in enumerate(outs):
        out_ref[...] = total[:, j * width : (j + 1) * width].astype(BF16)
    write_states(span, heads, *outs, g_ref, state_ref)
    share = heads // GROUP
    place = lax.rem(lax.axis_index("seq"), GROUP)
    total_ref[...] = sum_ref[...] + state_ref[...]
    for m, send in enumerate(sends, 1):
        for s in range(2):
            for e in range(share):
                send[s, e] = total_ref[s, (place ^ m) * share + e].astype(BF16)


def local_kernel(span, heads, weight_ref, q_ref, k_ref, v_ref, g_ref, after_ref, out_ref):
    rows = q_ref.shape[0]
    size = q_ref.shape[1] // heads
    norm = 1.0 / math.sqrt(size * g_ref.shape[0])
    at = lax.broadcasted_iota(jnp.int32, (rows, rows), 0)
    of = lax.broadcasted_iota(jnp.int32, (rows, rows), 1)
    columns = [slice(h * size, (h + 1) * size) for h in range(heads)]
    masked = []
    for h, cols in enumerate(columns):
        q, k, v = q_ref[:, cols], k_ref[:, cols], v_ref[:, cols]
        g = g_ref[span[0] : span[1], cols]
        scale = weight_ref[h, 0] * norm
        found = []
        for left, right, causal in (
            (q, k, at >= of),
            (g, v, at >= of),
            (v, g, of >= at),
            (k, q, of >= at),
        ):
            found.append(jnp.where(causal, dot(left, right, NT) * scale, 0.0).astype(BF16))
        masked.append(found)
    for h, cols in enumerate(columns):
        q, k, v = q_ref[:, cols], k_ref[:, cols], v_ref[:, cols]
        g = g_ref[span[0] : span[1], cols]
        for j, value in enumerate((v, k, q, g)):
            out_ref[j, :, cols] = dot(masked[h][j], value)


def owner_kernel(final, total_ref, *refs):
    got, refs = refs[: GROUP - 1], refs[GROUP - 1 :]
    near_ref, far_ref, *nexts = refs[-3 if final else -4 :]
    position = lax.axis_index("seq")
    place = lax.rem(position, GROUP)
    heads = total_ref.shape[1]
    share = heads // GROUP
    odd, high = bit_of(position, 0), bit_of(position, 1)
    for e in range(share):
        mine, other = [], []
        for s in range(2):
            mine.append(total_ref[s, place * share + e] + got[0][s, e].astype(F32))
            other.append(got[1][s, e].astype(F32) + got[2][s, e].astype(F32))
        sums = [mine[s] + other[s] for s in range(2)]
        write_next(sums, e, 2, final, *nexts)
        near_ref[e] = jnp.where(high, other[0], other[1]).astype(BF16)
        far_ref[e] = jnp.where(high, mine[1], mine[0]).astype(BF16)
    for h in range(heads):
        near_ref[share + h] = jnp.where(odd, total_ref[1, h], total_ref[0, h]).astype(BF16)


def write_next(sums, e, bit, final, next_ref, sum_ref=None):
    if final:
        value = jnp.where(bit_of(lax.axis_index("seq"), bit), sums[1], sums[0])
        next_ref[e] = value.astype(BF16)
        return
    for s in range(2):
        sum_ref[s, e] = sums[s]
        next_ref[s, e] = sums[s].astype(BF16)


def climb_kernel(bit, next_final, got_ref, old_ref, level_ref, *nexts):
    on = bit_of(lax.axis_index("seq"), bit)
    for e in range(got_ref.shape[1]):
        both = [got_ref[s, e].astype(F32) for s in range(2)]
        level_ref[e] = jnp.where(on, both[0], both[1]).astype(BF16)
        sums = [old_ref[s, e] + both[s] for s in range(2)]
        write_next(sums, e, bit + 1, next_final, *nexts)


def pair_block(first, second):
    zero = jnp.zeros(first.shape, BF16)
    top = jnp.concatenate([first.astype(BF16), zero], axis=1)
    bottom = jnp.concatenate([zero, second.astype(BF16)], axis=1)
    return jnp.concatenate([top, bottom], axis=0)


def gather_mixes(levels, first, side, weight_ref, block, mix_ref):
    position = lax.axis_index("seq")
    place = lax.rem(position, GROUP)
    heads, size = mix_ref.shape[:2]
    share = heads // GROUP
    for m in range(GROUP):
        for e in range(share):
            h = (place ^ m) * share + e
            total = None
            for b in range(len(levels) // GROUP):
                level = first + b
                coef = weight_ref[h, level + 1] * (1.0 / math.sqrt(size * block * 2**level))
                taken = bit_of(position, level)
                if side == 1:
                    taken = jnp.logical_not(taken)
                term = jnp.where(taken, coef, 0.0) * levels[b * GROUP + m][e].astype(F32)
                total = term if total is None else total + term
            mix_ref[h] = total


def write_side(spans, side, ascending, weight_of, rows_of, part_refs, outs, held, sems):
    chunks = len(spans)
    size = held.shape[-1]
    copies = []
    for c in range(chunks) if ascending else reversed(range(chunks)):
        span = slice(*spans[c])
        weights = weight_of(c)
        for j in range(2):
            ref = rows_of[2 * side + j][c]
            rows = span if ref.shape[0] != spans[c][1] - spans[c][0] else slice(None)
            for p, weight in enumerate(weights):
                cols = slice(p * weight.shape[0], (p + 1) * weight.shape[0])
                term = dot(ref[rows, cols], weight, NT if 2 * side + j in (1, 2) else NN)
                held[j, span, cols] = (term + part_refs[c][2 * side + j, :, cols]).astype(BF16)
            copy = pltpu.make_async_copy(
                held.at[j, span], outs[2 * side + j].at[span], sems.at[j, c]
            )
            copy.start()
            copies.append(copy)
    for copy in copies:
        copy.wait()


def early_side_kernel(spans, heads, top, weight_ref, g_ref, *refs):
    chunks = len(spans)
    levels, refs = refs[: (top - 1) * GROUP], refs[(top - 1) * GROUP :]
    q_refs, refs = refs[:chunks], refs[chunks:]
    k_refs, refs = refs[:chunks], refs[chunks:]
    v_refs, refs = refs[:chunks], refs[chunks:]
    state_refs, refs = refs[:chunks], refs[chunks:]
    part_refs, refs = refs[:chunks], refs[chunks:]
    outs, (base_ref, held, mix_ref, sems) = refs[:4], refs[4:]
    position = lax.axis_index("seq")
    block = g_ref.shape[0]
    size = mix_ref.shape[-1]
    norm = 1.0 / math.sqrt(size * block)

    def sums_of(side):
        gather_mixes(levels, 1, side, weight_ref, block, mix_ref)
        taken = bit_of(position, 0)
        if side == 1:
            taken = jnp.logical_not(taken)
        found = []
        for h in range(heads):
            coef = jnp.where(taken, weight_ref[h, 1] * norm, 0.0)
            found.append(mix_ref[h] + coef * levels[1][heads // GROUP + h].astype(F32))
        return found

    def add(sums, side, c):
        return [
            total + weight_ref[h, 0] * norm * state_refs[c][side, h] for h, total in enumerate(sums)
        ]

    for side in range(2):
        reached = bit_of(position, top)

        @pl.when(reached if side == 1 else jnp.logical_not(reached))
        def _():
            sums = [sums_of(side)]

            def weight_of(c):
                weights = [pair_block(*sums[0][h : h + 2]) for h in range(0, heads, 2)]
                sums[0] = add(sums[0], side, c)
                return weights

            rows_of = (q_refs, [g_ref] * chunks, v_refs, k_refs)
            write_side(spans, side, side == 0, weight_of, rows_of, part_refs, outs, held, sems)
            other = sums_of(1 - side)
            for c in range(chunks) if side == 1 else reversed(range(chunks)):
                for h in range(heads):
                    base_ref[c, h] = other[h]
                other = add(other, 1 - side, c)


def late_side_kernel(spans, heads, top, weight_ref, g_ref, base_ref, *refs):
    chunks = len(spans)
    levels, refs = refs[:GROUP], refs[GROUP:]
    q_refs, refs = refs[:chunks], refs[chunks:]
    k_refs, refs = refs[:chunks], refs[chunks:]
    v_refs, refs = refs[:chunks], refs[chunks:]
    part_refs, refs = refs[:chunks], refs[chunks:]
    outs, (held, mix_ref, sems) = refs[-7:-3], refs[-3:]
    block = g_ref.shape[0]
    reached = bit_of(lax.axis_index("seq"), top)
    for side in range(2):

        @pl.when(reached if side == 0 else jnp.logical_not(reached))
        def _():
            gather_mixes(levels, top, side, weight_ref, block, mix_ref)

            def weight_of(c):
                sums = [base_ref[c, h] + mix_ref[h] for h in range(heads)]
                return [pair_block(*sums[h : h + 2]) for h in range(0, heads, 2)]

            rows_of = (q_refs, [g_ref] * chunks, v_refs, k_refs)
            write_side(spans, side, False, weight_of, rows_of, part_refs, outs, held, sems)


def exchange(totals, sends, local, late):
    depth = lax.axis_size("seq").bit_length() - 1
    heads, square = totals.shape[1], totals.shape[2:]
    share = heads // GROUP
    last = depth - 1

    def nexts(bit):
        if bit == last:
            return [pltpu.VMEM((share, *square), BF16)]
        return [pltpu.VMEM((2, share, *square), BF16), pltpu.VMEM((2, share, *square), F32)]

    def spread(mine, other):
        return [mine, *[swap(mine if m == 1 else other, "seq", m) for m in range(1, GROUP)]]

    one = pltpu.VMEM((share, *square), BF16)
    got = [swap(send, "seq", m) for m, send in enumerate(sends, 1)]
    fillers = [local(c, sends[0]) for c in late]
    mine, other, sent, *sums = call(
        functools.partial(owner_kernel, last == 2),
        [pltpu.VMEM((share + heads, *square), BF16), one, *nexts(2)],
        [totals, *got, *fillers],
        [VMEM] * GROUP + [ANY] * len(fillers),
        10**6,
    )
    levels = spread(mine, other)
    for bit in range(2, last):
        found, sent, *sums = call(
            functools.partial(climb_kernel, bit, bit + 1 == last),
            [one, *nexts(bit + 1)],
            [swap(sent, "seq", 1 << bit), *sums],
            [VMEM] * 2,
            10**6,
        )
        levels += spread(found, found)
    found = tie(swap(sent, "seq", 1 << last), mine, flops=12 * 10**8)
    levels += spread(found, found)
    return levels, fillers


def per_device(inputs, w_qkv, level_weight, grad_out):
    rows, width = grad_out.shape
    heads = level_weight.shape[0]
    size = width // heads
    parts = lax.axis_size("head")
    edges = [rows * sum(SHARES[:c]) // sum(SHARES) for c in range(CHUNKS + 1)]
    spans = list(zip(edges[:-1], edges[1:]))
    depth = inputs.shape[1]
    mine = load(inputs, spans[:1])
    mine = [*mine, *load(inputs, spans[1:], mine)]
    grads, weights = call(
        functools.partial(load_weights_kernel, parts),
        [pltpu.VMEM((rows, width), BF16), pltpu.VMEM((parts * depth, 3 * width), BF16)],
        [
            pltpu.with_memory_space_constraint(grad_out, pltpu.HBM),
            pltpu.with_memory_space_constraint(w_qkv, pltpu.HBM),
            mine[1],
        ],
        [HBM, HBM, ANY],
        0,
        [pltpu.SemaphoreType.DMA((3 * parts + 1,))],
        limit=2,
        moved=4 * (grad_out.size + w_qkv.size),
    )
    top, *lows = [1 << b for b in reversed(range(parts.bit_length() - 1))]
    arrived = [swap(piece, "head", top) for piece in mine]
    arrived[0] = tie(arrived[0], weights)
    whole = {0: inputs}
    for low in lows:
        for k in sorted(whole):
            whole[k | low] = swap(whole[k], "head", low)
    state = pltpu.VMEM((2, heads, size, size), F32)
    qs, ks, vs, states, locals_ = [], [], [], [], []

    def local(c, after):
        chunk = spans[c][1] - spans[c][0]
        return call(
            functools.partial(local_kernel, spans[c], heads),
            [pltpu.VMEM((4, chunk, width), F32)],
            [level_weight, qs[c], ks[c], vs[c], grads, after],
            [SMEM] + [VMEM] * 4 + [ANY],
            100 * chunk * chunk * width if c >= CHUNKS - 2 else 0,
        )[0]

    after = None
    for c in range(CHUNKS):
        pieces = {**whole, 0: mine[c]}
        pieces[top] = arrived[c] if after is None else tie(arrived[c], after)
        for low in lows:
            for k in [k for k in sorted(pieces) if k & top]:
                pieces[k | low] = swap(pieces[k], "head", low)
        segments = [pieces[k] for k in sorted(pieces)]
        span = spans[c]
        chunk = span[1] - span[0]
        flat = pltpu.VMEM((chunk, width), BF16)
        if c < CHUNKS - 1:
            if c > 0:
                locals_.append(local(c - 1, pieces[top]))
            operands = [weights, grads, *segments, *locals_[-1:]]
            got = call(
                functools.partial(project_kernel, span, len(segments), heads),
                [flat, flat, flat, state],
                operands,
                [VMEM] * (2 + len(segments)) + [ANY] * len(locals_[-1:]),
                0,
            )
        else:
            operands = [weights, *segments[:-1], *states]
            begun, before = call(
                functools.partial(early_kernel, span, len(segments) - 1),
                [pltpu.VMEM((chunk, 3 * width), F32), state],
                operands,
                [VMEM] * len(operands),
                0,
            )
            got = call(
                functools.partial(last_kernel, span, heads),
                [
                    flat,
                    flat,
                    flat,
                    state,
                    state,
                    *[pltpu.VMEM((2, heads // GROUP, size, size), BF16)] * (GROUP - 1),
                ],
                [weights, grads, begun, before, segments[-1]],
                [VMEM] * 5,
                0,
            )
        qs.append(got[0])
        ks.append(got[1])
        vs.append(got[2])
        states.append(got[3])
        after = got[3]
    levels, fillers = exchange(got[4], got[5:], local, range(len(locals_), CHUNKS))
    locals_ += fillers
    shapes = [jax.ShapeDtypeStruct((rows, width), BF16)] * 4
    top = len(levels) // GROUP
    flats = [*qs, *ks, *vs]
    scratch = [
        pltpu.VMEM((2, rows, width), BF16),
        pltpu.VMEM((heads, size, size), F32),
        pltpu.SemaphoreType.DMA((2, CHUNKS)),
    ]
    operands = [level_weight, grads, *levels[:-GROUP], *flats, *states, *locals_]
    *written, base = call(
        functools.partial(early_side_kernel, spans, heads, top),
        [*shapes, pltpu.VMEM((CHUNKS, heads, size, size), F32)],
        operands,
        [SMEM] + [VMEM] * (len(operands) - 1),
        0,
        scratch,
        [ANY] * 4 + [VMEM],
        8,
    )
    operands = [level_weight, grads, base, *levels[-GROUP:], *flats, *locals_]
    return call(
        functools.partial(late_side_kernel, spans, heads, top),
        shapes,
        [*operands, *written],
        [SMEM] + [VMEM] * (len(operands) - 1) + [ANY] * 4,
        0,
        scratch,
        [ANY] * 4,
        8,
        aliases={len(operands) + j: j for j in range(4)},
    )


def solution(mesh):
    in_specs = (P("seq", "head"), P(None, None, "head"), P("head", None), P("seq", "head"))
    out_specs = (P("seq", "head"), P("seq", "head"), P("seq", "head"), P("seq", "head"))
    return jax.shard_map(
        per_device, mesh=mesh, in_specs=in_specs, out_specs=out_specs, check_vma=False
    )
```

```python
import functools
import math

import jax
import jax.numpy as jnp
from jax import lax
from jax.experimental import pallas as pl
from jax.experimental.pallas import tpu as pltpu
from jax.sharding import PartitionSpec as P

SHARES = (10, 12, 13, 14, 15)
CHUNKS = len(SHARES)
GROUP = 4
MIB = 2**20
VMEM = pl.BlockSpec(memory_space=pltpu.VMEM)
SMEM = pl.BlockSpec(memory_space=pltpu.SMEM)
ANY = pl.BlockSpec(memory_space=pl.ANY)
HBM = pl.BlockSpec(memory_space=pltpu.HBM)
NN = (((1,), (0,)), ((), ()))
NT = (((1,), (1,)), ((), ()))
TN = (((0,), (0,)), ((), ()))
BF16 = jnp.bfloat16
F32 = jnp.float32


def dot(a, b, dims=NN):
    return lax.dot_general(a, b, dims, preferred_element_type=F32)


def swap(value, axis, mask):
    pairs = [(source, source ^ mask) for source in range(lax.axis_size(axis))]
    return lax.ppermute(value, axis, pairs)


def bit_of(position, bit):
    return lax.rem(position // 2**bit, 2) == 1


def is_back(top):
    return jnp.logical_not(bit_of(lax.axis_index("seq"), top))


def rows_at(span, block, top):
    first, last = span
    start = jnp.where(is_back(top), block - last, first)
    return pl.ds(pl.multiple_of(start, 16), last - first)


def top_level():
    return lax.axis_size("seq").bit_length() - 2


def call(kernel, outs, operands, specs, flops, scratch=(), out_specs=None, limit=4, moved=0, aliases=()):
    return pl.pallas_call(
        kernel,
        out_shape=outs,
        in_specs=specs,
        out_specs=[VMEM] * len(outs) if out_specs is None else out_specs,
        scratch_shapes=scratch,
        input_output_aliases=dict(aliases),
        compiler_params=pltpu.CompilerParams(vmem_limit_bytes=limit * MIB),
        cost_estimate=pl.CostEstimate(flops=flops, bytes_accessed=moved, transcendentals=0),
    )(*operands)


def load_kernel(spans, x_ref, *refs):
    outs, sems = refs[-len(spans) - 1 : -1], refs[-1]
    copies = []
    for i, span in enumerate(spans):
        rows = x_ref.at[rows_at(span, x_ref.shape[0], top_level())]
        copies.append(pltpu.make_async_copy(rows, outs[i], sems.at[i]))
    for copy in copies:
        copy.start()
    for copy in copies:
        copy.wait()


def load(source, spans, after=()):
    return call(
        functools.partial(load_kernel, spans),
        [pltpu.VMEM((last - first, *source.shape[1:]), BF16) for first, last in spans],
        [pltpu.with_memory_space_constraint(source, pltpu.HBM), *after],
        [HBM] + [ANY] * len(after),
        0,
        [pltpu.SemaphoreType.DMA((len(spans),))],
        limit=2,
        moved=4 * source.size,
    )


def load_weights_kernel(parts, g_ref, w_ref, after_ref, g_out, w_out, sems):
    me = lax.axis_index("head")
    depth = w_ref.shape[1] // parts
    width = w_ref.shape[2]
    copies = [pltpu.make_async_copy(g_ref, g_out, sems.at[3 * parts])]
    for k in range(parts):
        rows = pl.ds(pl.multiple_of((me ^ k) * depth, depth), depth)
        for j in range(3):
            copies.append(
                pltpu.make_async_copy(
                    w_ref.at[j, rows],
                    w_out.at[pl.ds(k * depth, depth), pl.ds(j * width, width)],
                    sems.at[3 * k + j],
                )
            )
    for copy in copies:
        copy.start()
    for copy in copies:
        copy.wait()


def tie_kernel(value_ref, *refs):
    del value_ref, refs


def tie(value, *after, flops=0):
    return pl.pallas_call(
        tie_kernel,
        out_shape=pltpu.VMEM(value.shape, value.dtype),
        in_specs=[VMEM] + [ANY] * len(after),
        out_specs=VMEM,
        input_output_aliases={0: 0},
        compiler_params=pltpu.CompilerParams(vmem_limit_bytes=MIB),
        cost_estimate=pl.CostEstimate(flops=flops, bytes_accessed=0, transcendentals=0),
    )(value, *after)


def take(ref, span, cols):
    if ref.shape[0] == span[1] - span[0]:
        return ref[:, cols]
    return ref[rows_at(span, ref.shape[0], top_level()), cols]


def beside(refs, span):
    found = [take(ref, span, slice(None)) for ref in refs]
    return found[0] if len(found) == 1 else jnp.concatenate(found, axis=1)


def write_states(span, heads, q_ref, k_ref, v_ref, g_ref, state_ref):
    size = q_ref.shape[1] // heads
    for h in range(0, heads, 2):
        cols = slice(h * size, (h + 2) * size)
        for s, (left, right) in enumerate(((k_ref, v_ref), (q_ref, g_ref))):
            both = dot(left[:, cols], take(right, span, cols), TN)
            state_ref[s, h] = both[:size, :size]
            state_ref[s, h + 1] = both[size:, size:]


def early_kernel(span, count, w_ref, *refs):
    segments, states = refs[:count], refs[count:-2]
    total_ref, sum_ref = refs[-2:]
    rows = beside(segments, span)
    total_ref[...] = dot(rows, w_ref[: rows.shape[1], :])
    sums = states[0][...]
    for state in states[1:]:
        sums = sums + state[...]
    sum_ref[...] = sums


def project_kernel(span, count, heads, w_ref, g_ref, *refs):
    outs, state_ref = refs[-4:-1], refs[-1]
    width = outs[0].shape[1]
    total = dot(beside(refs[:count], span), w_ref[...])
    for j, out_ref in enumerate(outs):
        out_ref[...] = total[:, j * width : (j + 1) * width].astype(BF16)
    write_states(span, heads, *outs, g_ref, state_ref)


def last_kernel(span, heads, w_ref, g_ref, part_ref, sum_ref, late_ref, *refs):
    outs, state_ref, total_ref, sends = refs[:3], refs[3], refs[4], refs[5:]
    width = outs[0].shape[1]
    start = w_ref.shape[0] - late_ref.shape[1]
    total = part_ref[...] + dot(late_ref[...], w_ref[start:, :])
    for j, out_ref in enumerate(outs):
        out_ref[...] = total[:, j * width : (j + 1) * width].astype(BF16)
    write_states(span, heads, *outs, g_ref, state_ref)
    share = heads // GROUP
    place = lax.rem(lax.axis_index("seq"), GROUP)
    total_ref[...] = sum_ref[...] + state_ref[...]
    for m, send in enumerate(sends, 1):
        for s in range(2):
            for e in range(share):
                send[s, e] = total_ref[s, (place ^ m) * share + e].astype(BF16)


def local_kernel(span, heads, count, weight_ref, q_ref, k_ref, v_ref, g_ref, *refs):
    states, out_ref = refs[:count], refs[-1]
    rows = q_ref.shape[0]
    size = q_ref.shape[1] // heads
    norm = 1.0 / math.sqrt(size * g_ref.shape[0])
    at = lax.broadcasted_iota(jnp.int32, (rows, rows), 0)
    of = lax.broadcasted_iota(jnp.int32, (rows, rows), 1)
    columns = [slice(h * size, (h + 1) * size) for h in range(heads)]
    masked = []
    for h, cols in enumerate(columns):
        q, k, v = q_ref[:, cols], k_ref[:, cols], v_ref[:, cols]
        g = take(g_ref, span, cols)
        scale = weight_ref[h, 0] * norm
        found = []
        for left, right, causal in (
            (q, k, at >= of),
            (g, v, at >= of),
            (v, g, of >= at),
            (k, q, of >= at),
        ):
            found.append(jnp.where(causal, dot(left, right, NT) * scale, 0.0).astype(BF16))
        masked.append(found)
    for h, cols in enumerate(columns):
        q, k, v = q_ref[:, cols], k_ref[:, cols], v_ref[:, cols]
        g = take(g_ref, span, cols)
        for j, value in enumerate((v, k, q, g)):
            out_ref[j, :, cols] = dot(masked[h][j], value)
    if count == 0:
        return
    back = is_back(top_level())
    for side in range(2):

        @pl.when(back if side == 1 else jnp.logical_not(back))
        def _():
            for h in range(0, heads, 2):
                cols = slice(h * size, (h + 2) * size)
                sums = []
                for e in (h, h + 1):
                    total = states[0][side, e]
                    for state in states[1:]:
                        total = total + state[side, e]
                    sums.append(weight_ref[e, 0] * norm * total)
                weight = pair_block(*sums)
                for j in range(2):
                    left = (q_ref, g_ref, v_ref, k_ref)[2 * side + j]
                    term = dot(take(left, span, cols), weight, dims_of(side, j))
                    out_ref[2 * side + j, :, cols] = out_ref[2 * side + j, :, cols] + term


def dims_of(side, j):
    return NT if side != j else NN


def owner_kernel(final, total_ref, *refs):
    got, refs = refs[: GROUP - 1], refs[GROUP - 1 :]
    near_ref, far_ref, *nexts = refs[-3 if final else -4 :]
    position = lax.axis_index("seq")
    place = lax.rem(position, GROUP)
    heads = total_ref.shape[1]
    share = heads // GROUP
    odd, high = bit_of(position, 0), bit_of(position, 1)
    for e in range(share):
        mine, other = [], []
        for s in range(2):
            mine.append(total_ref[s, place * share + e] + got[0][s, e].astype(F32))
            other.append(got[1][s, e].astype(F32) + got[2][s, e].astype(F32))
        sums = [mine[s] + other[s] for s in range(2)]
        write_next(sums, e, 2, final, *nexts)
        near_ref[e] = jnp.where(high, other[0], other[1]).astype(BF16)
        far_ref[e] = jnp.where(high, mine[1], mine[0]).astype(BF16)
    for h in range(heads):
        near_ref[share + h] = jnp.where(odd, total_ref[1, h], total_ref[0, h]).astype(BF16)


def write_next(sums, e, bit, final, next_ref, sum_ref=None):
    if final:
        value = jnp.where(bit_of(lax.axis_index("seq"), bit), sums[1], sums[0])
        next_ref[e] = value.astype(BF16)
        return
    for s in range(2):
        sum_ref[s, e] = sums[s]
        next_ref[s, e] = sums[s].astype(BF16)


def climb_kernel(bit, next_final, got_ref, old_ref, level_ref, *nexts):
    on = bit_of(lax.axis_index("seq"), bit)
    for e in range(got_ref.shape[1]):
        both = [got_ref[s, e].astype(F32) for s in range(2)]
        level_ref[e] = jnp.where(on, both[0], both[1]).astype(BF16)
        sums = [old_ref[s, e] + both[s] for s in range(2)]
        write_next(sums, e, bit + 1, next_final, *nexts)


def pair_block(first, second):
    zero = jnp.zeros(first.shape, BF16)
    top = jnp.concatenate([first.astype(BF16), zero], axis=1)
    bottom = jnp.concatenate([zero, second.astype(BF16)], axis=1)
    return jnp.concatenate([top, bottom], axis=0)


def gather_mixes(levels, first, side, weight_ref, block, mix_ref):
    position = lax.axis_index("seq")
    place = lax.rem(position, GROUP)
    heads, size = mix_ref.shape[:2]
    share = heads // GROUP
    for m in range(GROUP):
        for e in range(share):
            h = (place ^ m) * share + e
            total = None
            for b in range(len(levels) // GROUP):
                level = first + b
                coef = weight_ref[h, level + 1] * (1.0 / math.sqrt(size * block * 2**level))
                taken = bit_of(position, level)
                if side == 1:
                    taken = jnp.logical_not(taken)
                term = jnp.where(taken, coef, 0.0) * levels[b * GROUP + m][e].astype(F32)
                total = term if total is None else total + term
            mix_ref[h] = total


def early_side_kernel(spans, heads, top, weight_ref, g_ref, *refs):
    chunks = len(spans)
    levels, refs = refs[: (top - 1) * GROUP], refs[(top - 1) * GROUP :]
    q_refs, refs = refs[:chunks], refs[chunks:]
    k_refs, refs = refs[:chunks], refs[chunks:]
    v_refs, refs = refs[:chunks], refs[chunks:]
    state_refs, refs = refs[:chunks], refs[chunks:]
    part_refs, refs = refs[:chunks], refs[chunks:]
    outs, (base_ref, held, mix_ref, sems) = refs[:4], refs[4:]
    position = lax.axis_index("seq")
    block = g_ref.shape[0]
    size = mix_ref.shape[-1]
    norm = 1.0 / math.sqrt(size * block)

    def sums_of(side):
        gather_mixes(levels, 1, side, weight_ref, block, mix_ref)
        taken = bit_of(position, 0)
        if side == 1:
            taken = jnp.logical_not(taken)
        found = []
        for h in range(heads):
            coef = jnp.where(taken, weight_ref[h, 1] * norm, 0.0)
            found.append(mix_ref[h] + coef * levels[1][heads // GROUP + h].astype(F32))
        return found

    back = is_back(top)
    for side in range(2):

        @pl.when(back if side == 0 else jnp.logical_not(back))
        def _():
            sums = sums_of(side)
            copies = []
            for c in reversed(range(chunks)):
                span = slice(*spans[c])
                weights = [pair_block(*sums[h : h + 2]) for h in range(0, heads, 2)]
                for j in range(2):
                    ref = (q_refs[c], g_ref, v_refs[c], k_refs[c])[2 * side + j]
                    for p, weight in enumerate(weights):
                        cols = slice(p * 2 * size, (p + 1) * 2 * size)
                        term = dot(take(ref, spans[c], cols), weight, dims_of(side, j))
                        part = part_refs[c][2 * side + j, :, cols]
                        held[j, span, cols] = (term + part).astype(BF16)
                    copies.append(copy_out(spans[c], held, outs, side, j, sems.at[j, c]))
                sums = [
                    total + weight_ref[h, 0] * norm * state_refs[c][side, h]
                    for h, total in enumerate(sums)
                ]
            for h, value in enumerate(sums_of(1 - side)):
                base_ref[h] = value
            for copy in copies:
                copy.wait()


def copy_out(span, held, outs, side, j, sem):
    out = outs[2 * side + j]
    target = out.at[rows_at(span, out.shape[0], top_level())]
    copy = pltpu.make_async_copy(held.at[j, slice(*span)], target, sem)
    copy.start()
    return copy


def late_side_kernel(spans, heads, top, weight_ref, g_ref, base_ref, *refs):
    chunks = len(spans)
    levels, refs = refs[:GROUP], refs[GROUP:]
    q_refs, refs = refs[:chunks], refs[chunks:]
    k_refs, refs = refs[:chunks], refs[chunks:]
    v_refs, refs = refs[:chunks], refs[chunks:]
    part_refs, refs = refs[:chunks], refs[chunks:]
    outs, (held, mix_ref, sems) = refs[-7:-3], refs[-3:]
    block = g_ref.shape[0]
    size = mix_ref.shape[-1]
    back = is_back(top)
    for side in range(2):

        @pl.when(back if side == 1 else jnp.logical_not(back))
        def _():
            gather_mixes(levels, top, side, weight_ref, block, mix_ref)
            sums = [base_ref[h] + mix_ref[h] for h in range(heads)]
            weights = [pair_block(*sums[h : h + 2]) for h in range(0, heads, 2)]
            copies = []
            for j in range(2):
                found = (q_refs, [g_ref] * chunks, v_refs, k_refs)[2 * side + j]
                for p, weight in enumerate(weights):
                    cols = slice(p * 2 * size, (p + 1) * 2 * size)
                    rows = [take(ref, span, cols) for ref, span in zip(found, spans)]
                    term = dot(jnp.concatenate(rows, axis=0), weight, dims_of(side, j))
                    for c, span in enumerate(spans):
                        part = part_refs[c][2 * side + j, :, cols]
                        held[j, slice(*span), cols] = (term[slice(*span)] + part).astype(BF16)
                for c, span in enumerate(spans):
                    copies.append(copy_out(span, held, outs, side, j, sems.at[j, c]))
            for copy in copies:
                copy.wait()


def exchange(totals, sends, local, late):
    depth = lax.axis_size("seq").bit_length() - 1
    heads, square = totals.shape[1], totals.shape[2:]
    share = heads // GROUP
    last = depth - 1

    def nexts(bit):
        if bit == last:
            return [pltpu.VMEM((share, *square), BF16)]
        return [pltpu.VMEM((2, share, *square), BF16), pltpu.VMEM((2, share, *square), F32)]

    def spread(mine, other):
        return [mine, *[swap(mine if m == 1 else other, "seq", m) for m in range(1, GROUP)]]

    one = pltpu.VMEM((share, *square), BF16)
    got = [swap(send, "seq", m) for m, send in enumerate(sends, 1)]
    fillers = [local(c, sends[0]) for c in late]
    mine, other, sent, *sums = call(
        functools.partial(owner_kernel, last == 2),
        [pltpu.VMEM((share + heads, *square), BF16), one, *nexts(2)],
        [totals, *got, *fillers],
        [VMEM] * GROUP + [ANY] * len(fillers),
        10**6,
    )
    levels = spread(mine, other)
    for bit in range(2, last):
        found, sent, *sums = call(
            functools.partial(climb_kernel, bit, bit + 1 == last),
            [one, *nexts(bit + 1)],
            [swap(sent, "seq", 1 << bit), *sums],
            [VMEM] * 2,
            10**6,
        )
        levels += spread(found, found)
    found = tie(swap(sent, "seq", 1 << last), mine, flops=12 * 10**8)
    levels += spread(found, found)
    return levels, fillers


def per_device(inputs, w_qkv, level_weight, grad_out):
    rows, width = grad_out.shape
    heads = level_weight.shape[0]
    size = width // heads
    parts = lax.axis_size("head")
    edges = [rows * sum(SHARES[:c]) // sum(SHARES) for c in range(CHUNKS + 1)]
    spans = list(zip(edges[:-1], edges[1:]))
    depth = inputs.shape[1]
    mine = load(inputs, spans[:1])
    mine = [*mine, *load(inputs, spans[1:], mine)]
    grads, weights = call(
        functools.partial(load_weights_kernel, parts),
        [pltpu.VMEM((rows, width), BF16), pltpu.VMEM((parts * depth, 3 * width), BF16)],
        [
            pltpu.with_memory_space_constraint(grad_out, pltpu.HBM),
            pltpu.with_memory_space_constraint(w_qkv, pltpu.HBM),
            mine[1],
        ],
        [HBM, HBM, ANY],
        0,
        [pltpu.SemaphoreType.DMA((3 * parts + 1,))],
        limit=2,
        moved=4 * (grad_out.size + w_qkv.size),
    )
    top, *lows = [1 << b for b in reversed(range(parts.bit_length() - 1))]
    arrived = [swap(piece, "head", top) for piece in mine]
    arrived[0] = tie(arrived[0], weights)
    whole = {0: inputs}
    for low in lows:
        for k in sorted(whole):
            whole[k | low] = swap(whole[k], "head", low)
    state = pltpu.VMEM((2, heads, size, size), F32)
    qs, ks, vs, states, locals_ = [], [], [], [], []

    def local(c, after):
        chunk = spans[c][1] - spans[c][0]
        return call(
            functools.partial(local_kernel, spans[c], heads, c),
            [pltpu.VMEM((4, chunk, width), F32)],
            [level_weight, qs[c], ks[c], vs[c], grads, *states[:c], after],
            [SMEM] + [VMEM] * (4 + c) + [ANY],
            100 * chunk * chunk * width if c >= CHUNKS - 2 else 0,
        )[0]

    after = None
    for c in range(CHUNKS):
        pieces = {**whole, 0: mine[c]}
        pieces[top] = arrived[c] if after is None else tie(arrived[c], after)
        for low in lows:
            for k in [k for k in sorted(pieces) if k & top]:
                pieces[k | low] = swap(pieces[k], "head", low)
        segments = [pieces[k] for k in sorted(pieces)]
        span = spans[c]
        chunk = span[1] - span[0]
        flat = pltpu.VMEM((chunk, width), BF16)
        if c < CHUNKS - 1:
            if c > 0:
                locals_.append(local(c - 1, pieces[top]))
            operands = [weights, grads, *segments, *locals_[-1:]]
            got = call(
                functools.partial(project_kernel, span, len(segments), heads),
                [flat, flat, flat, state],
                operands,
                [VMEM] * (2 + len(segments)) + [ANY] * len(locals_[-1:]),
                0,
            )
        else:
            operands = [weights, *segments[:-1], *states]
            begun, before = call(
                functools.partial(early_kernel, span, len(segments) - 1),
                [pltpu.VMEM((chunk, 3 * width), F32), state],
                operands,
                [VMEM] * len(operands),
                0,
            )
            got = call(
                functools.partial(last_kernel, span, heads),
                [
                    flat,
                    flat,
                    flat,
                    state,
                    state,
                    *[pltpu.VMEM((2, heads // GROUP, size, size), BF16)] * (GROUP - 1),
                ],
                [weights, grads, begun, before, segments[-1]],
                [VMEM] * 5,
                0,
            )
        qs.append(got[0])
        ks.append(got[1])
        vs.append(got[2])
        states.append(got[3])
        after = got[3]
    levels, fillers = exchange(got[4], got[5:], local, range(len(locals_), CHUNKS))
    locals_ += fillers
    shapes = [jax.ShapeDtypeStruct((rows, width), BF16)] * 4
    top = len(levels) // GROUP
    flats = [*qs, *ks, *vs]
    scratch = [
        pltpu.VMEM((2, rows, width), BF16),
        pltpu.VMEM((heads, size, size), F32),
        pltpu.SemaphoreType.DMA((2, CHUNKS)),
    ]
    operands = [level_weight, grads, *levels[:-GROUP], *flats, *states, *locals_]
    *written, base = call(
        functools.partial(early_side_kernel, spans, heads, top),
        [*shapes, pltpu.VMEM((heads, size, size), F32)],
        operands,
        [SMEM] + [VMEM] * (len(operands) - 1),
        0,
        scratch,
        [ANY] * 4 + [VMEM],
        8,
    )
    operands = [level_weight, grads, base, *levels[-GROUP:], *flats, *locals_]
    return call(
        functools.partial(late_side_kernel, spans, heads, top),
        shapes,
        [*operands, *written],
        [SMEM] + [VMEM] * (len(operands) - 1) + [ANY] * 4,
        0,
        scratch,
        [ANY] * 4,
        8,
        aliases={len(operands) + j: j for j in range(4)},
    )


def solution(mesh):
    in_specs = (P("seq", "head"), P(None, None, "head"), P("head", None), P("seq", "head"))
    out_specs = (P("seq", "head"), P("seq", "head"), P("seq", "head"), P("seq", "head"))
    return jax.shard_map(
        per_device, mesh=mesh, in_specs=in_specs, out_specs=out_specs, check_vma=False
    )
```

```python
import functools
import math

import jax
import jax.numpy as jnp
from jax import lax
from jax.experimental import pallas as pl
from jax.experimental.pallas import tpu as pltpu
from jax.sharding import PartitionSpec as P

SHARES = (10, 12, 13, 14, 15)
CHUNKS = len(SHARES)
GROUP = 4
FIRST = (3, 2, 1)
MIB = 2**20
VMEM = pl.BlockSpec(memory_space=pltpu.VMEM)
SMEM = pl.BlockSpec(memory_space=pltpu.SMEM)
ANY = pl.BlockSpec(memory_space=pl.ANY)
HBM = pl.BlockSpec(memory_space=pltpu.HBM)
NN = (((1,), (0,)), ((), ()))
NT = (((1,), (1,)), ((), ()))
TN = (((0,), (0,)), ((), ()))
BF16 = jnp.bfloat16
F32 = jnp.float32


def dot(a, b, dims=NN):
    return lax.dot_general(a, b, dims, preferred_element_type=F32)


def swap(value, axis, mask):
    pairs = [(source, source ^ mask) for source in range(lax.axis_size(axis))]
    return lax.ppermute(value, axis, pairs)


def bit_of(position, bit):
    return lax.rem(position // 2**bit, 2) == 1


def call(kernel, outs, operands, specs, flops, scratch=(), out_specs=None, limit=4, moved=0, aliases=()):
    return pl.pallas_call(
        kernel,
        out_shape=outs,
        in_specs=specs,
        out_specs=[VMEM] * len(outs) if out_specs is None else out_specs,
        scratch_shapes=scratch,
        input_output_aliases=dict(aliases),
        compiler_params=pltpu.CompilerParams(vmem_limit_bytes=limit * MIB),
        cost_estimate=pl.CostEstimate(flops=flops, bytes_accessed=moved, transcendentals=0),
    )(*operands)


def load_kernel(spans, x_ref, *refs):
    outs, sems = refs[-len(spans) - 1 : -1], refs[-1]
    copies = []
    for i, (first, last) in enumerate(spans):
        rows = x_ref.at[pl.ds(first, last - first)]
        copies.append(pltpu.make_async_copy(rows, outs[i], sems.at[i]))
    for copy in copies:
        copy.start()
    for copy in copies:
        copy.wait()


def load(source, spans, after=()):
    return call(
        functools.partial(load_kernel, spans),
        [pltpu.VMEM((last - first, *source.shape[1:]), BF16) for first, last in spans],
        [pltpu.with_memory_space_constraint(source, pltpu.HBM), *after],
        [HBM] + [ANY] * len(after),
        0,
        [pltpu.SemaphoreType.DMA((len(spans),))],
        limit=2,
        moved=4 * source.size,
    )


def load_weights_kernel(parts, g_ref, w_ref, after_ref, g_out, w_out, sems):
    me = lax.axis_index("head")
    depth = w_ref.shape[1] // parts
    width = w_ref.shape[2]
    copies = [pltpu.make_async_copy(g_ref, g_out, sems.at[3 * parts])]
    for k in range(parts):
        rows = pl.ds(pl.multiple_of((me ^ k) * depth, depth), depth)
        for j in range(3):
            copies.append(
                pltpu.make_async_copy(
                    w_ref.at[j, rows],
                    w_out.at[pl.ds(k * depth, depth), pl.ds(j * width, width)],
                    sems.at[3 * k + j],
                )
            )
    for copy in copies:
        copy.start()
    for copy in copies:
        copy.wait()


def tie_kernel(value_ref, *refs):
    del value_ref, refs


def tie(value, *after, flops=0):
    return pl.pallas_call(
        tie_kernel,
        out_shape=pltpu.VMEM(value.shape, value.dtype),
        in_specs=[VMEM] + [ANY] * len(after),
        out_specs=VMEM,
        input_output_aliases={0: 0},
        compiler_params=pltpu.CompilerParams(vmem_limit_bytes=MIB),
        cost_estimate=pl.CostEstimate(flops=flops, bytes_accessed=0, transcendentals=0),
    )(value, *after)


def beside(refs, span):
    count = span[1] - span[0]
    found = [ref[...] if ref.shape[0] == count else ref[span[0] : span[1], :] for ref in refs]
    return found[0] if len(found) == 1 else jnp.concatenate(found, axis=1)


def write_states(span, heads, q_ref, k_ref, v_ref, g_ref, state_ref):
    size = q_ref.shape[1] // heads
    for h in range(heads):
        cols = slice(h * size, (h + 1) * size)
        state_ref[0, h] = dot(k_ref[:, cols], v_ref[:, cols], TN)
        state_ref[1, h] = dot(q_ref[:, cols], g_ref[span[0] : span[1], cols], TN)


def early_kernel(span, count, w_ref, *refs):
    segments, states = refs[:count], refs[count:-2]
    total_ref, sum_ref = refs[-2:]
    rows = beside(segments, span)
    total_ref[...] = dot(rows, w_ref[: rows.shape[1], :])
    sums = states[0][...]
    for state in states[1:]:
        sums = sums + state[...]
    sum_ref[...] = sums


def project_kernel(span, count, heads, w_ref, g_ref, *refs):
    outs, state_ref = refs[-4:-1], refs[-1]
    width = outs[0].shape[1]
    total = dot(beside(refs[:count], span), w_ref[...])
    for j, out_ref in enumerate(outs):
        out_ref[...] = total[:, j * width : (j + 1) * width].astype(BF16)
    write_states(span, heads, *outs, g_ref, state_ref)


def last_kernel(span, heads, w_ref, g_ref, part_ref, sum_ref, late_ref, *refs):
    outs, state_ref, total_ref, sends = refs[:3], refs[3], refs[4], refs[5:]
    width = outs[0].shape[1]
    start = w_ref.shape[0] - late_ref.shape[1]
    total = part_ref[...] + dot(late_ref[...], w_ref[start:, :])
    for j, out_ref in enumerate(outs):
        out_ref[...] = total[:, j * width : (j + 1) * width].astype(BF16)
    write_states(span, heads, *outs, g_ref, state_ref)
    share = heads // GROUP
    place = lax.rem(lax.axis_index("seq"), GROUP)
    total_ref[...] = sum_ref[...] + state_ref[...]
    for m, send in enumerate(sends, 1):
        for s in range(2):
            for e in range(share):
                send[s, e] = total_ref[s, (place ^ m) * share + e].astype(BF16)


def local_kernel(span, heads, weight_ref, q_ref, k_ref, v_ref, g_ref, after_ref, out_ref):
    rows = q_ref.shape[0]
    size = q_ref.shape[1] // heads
    norm = 1.0 / math.sqrt(size * g_ref.shape[0])
    at = lax.broadcasted_iota(jnp.int32, (rows, rows), 0)
    of = lax.broadcasted_iota(jnp.int32, (rows, rows), 1)
    columns = [slice(h * size, (h + 1) * size) for h in range(heads)]
    masked = []
    for h, cols in enumerate(columns):
        q, k, v = q_ref[:, cols], k_ref[:, cols], v_ref[:, cols]
        g = g_ref[span[0] : span[1], cols]
        scale = weight_ref[h, 0] * norm
        found = []
        for left, right, causal in (
            (q, k, at >= of),
            (g, v, at >= of),
            (v, g, of >= at),
            (k, q, of >= at),
        ):
            found.append(jnp.where(causal, dot(left, right, NT) * scale, 0.0).astype(BF16))
        masked.append(found)
    for h, cols in enumerate(columns):
        q, k, v = q_ref[:, cols], k_ref[:, cols], v_ref[:, cols]
        g = g_ref[span[0] : span[1], cols]
        for j, value in enumerate((v, k, q, g)):
            out_ref[j, :, cols] = dot(masked[h][j], value)


def owner_kernel(final, total_ref, *refs):
    got, refs = dict(zip(FIRST, refs)), refs[GROUP - 1 :]
    near_ref, far_ref, *nexts = refs[-3 if final else -4 :]
    position = lax.axis_index("seq")
    place = lax.rem(position, GROUP)
    heads = total_ref.shape[1]
    share = heads // GROUP
    odd, high = bit_of(position, 0), bit_of(position, 1)
    for e in range(share):
        mine, other = [], []
        for s in range(2):
            mine.append(total_ref[s, place * share + e] + got[1][s, e].astype(F32))
            other.append(got[2][s, e].astype(F32) + got[3][s, e].astype(F32))
        sums = [mine[s] + other[s] for s in range(2)]
        write_next(sums, e, 2, final, *nexts)
        near_ref[e] = jnp.where(high, other[0], other[1]).astype(BF16)
        far_ref[e] = jnp.where(high, mine[1], mine[0]).astype(BF16)
    for h in range(heads):
        near_ref[share + h] = jnp.where(odd, total_ref[1, h], total_ref[0, h]).astype(BF16)


def write_next(sums, e, bit, final, next_ref, sum_ref=None):
    if final:
        value = jnp.where(bit_of(lax.axis_index("seq"), bit), sums[1], sums[0])
        next_ref[e] = value.astype(BF16)
        return
    for s in range(2):
        sum_ref[s, e] = sums[s]
        next_ref[s, e] = sums[s].astype(BF16)


def climb_kernel(bit, next_final, got_ref, old_ref, level_ref, *nexts):
    on = bit_of(lax.axis_index("seq"), bit)
    for e in range(got_ref.shape[1]):
        both = [got_ref[s, e].astype(F32) for s in range(2)]
        level_ref[e] = jnp.where(on, both[0], both[1]).astype(BF16)
        sums = [old_ref[s, e] + both[s] for s in range(2)]
        write_next(sums, e, bit + 1, next_final, *nexts)


def pair_block(first, second):
    zero = jnp.zeros(first.shape, BF16)
    top = jnp.concatenate([first.astype(BF16), zero], axis=1)
    bottom = jnp.concatenate([zero, second.astype(BF16)], axis=1)
    return jnp.concatenate([top, bottom], axis=0)


def gather_mixes(levels, first, side, weight_ref, block, mix_ref):
    position = lax.axis_index("seq")
    place = lax.rem(position, GROUP)
    heads, size = mix_ref.shape[:2]
    share = heads // GROUP
    for m in range(GROUP):
        for e in range(share):
            h = (place ^ m) * share + e
            total = None
            for b in range(len(levels) // GROUP):
                level = first + b
                coef = weight_ref[h, level + 1] * (1.0 / math.sqrt(size * block * 2**level))
                taken = bit_of(position, level)
                if side == 1:
                    taken = jnp.logical_not(taken)
                term = jnp.where(taken, coef, 0.0) * levels[b * GROUP + m][e].astype(F32)
                total = term if total is None else total + term
            mix_ref[h] = total


def write_side(spans, side, ascending, weight_of, rows_of, part_refs, outs, held, sems):
    chunks = len(spans)
    size = held.shape[-1]
    copies = []
    for c in range(chunks) if ascending else reversed(range(chunks)):
        span = slice(*spans[c])
        weights = weight_of(c)
        for j in range(2):
            ref = rows_of[2 * side + j][c]
            rows = span if ref.shape[0] != spans[c][1] - spans[c][0] else slice(None)
            for p, weight in enumerate(weights):
                cols = slice(p * weight.shape[0], (p + 1) * weight.shape[0])
                term = dot(ref[rows, cols], weight, NT if 2 * side + j in (1, 2) else NN)
                held[j, span, cols] = (term + part_refs[c][2 * side + j, :, cols]).astype(BF16)
            copy = pltpu.make_async_copy(
                held.at[j, span], outs[2 * side + j].at[span], sems.at[j, c]
            )
            copy.start()
            copies.append(copy)
    for copy in copies:
        copy.wait()


def early_side_kernel(spans, heads, top, weight_ref, g_ref, *refs):
    chunks = len(spans)
    levels, refs = refs[: (top - 1) * GROUP], refs[(top - 1) * GROUP :]
    q_refs, refs = refs[:chunks], refs[chunks:]
    k_refs, refs = refs[:chunks], refs[chunks:]
    v_refs, refs = refs[:chunks], refs[chunks:]
    state_refs, refs = refs[:chunks], refs[chunks:]
    part_refs, refs = refs[:chunks], refs[chunks:]
    outs, (base_ref, held, mix_ref, sems) = refs[:4], refs[4:]
    position = lax.axis_index("seq")
    block = g_ref.shape[0]
    size = mix_ref.shape[-1]
    norm = 1.0 / math.sqrt(size * block)

    def sums_of(side):
        gather_mixes(levels, 1, side, weight_ref, block, mix_ref)
        taken = bit_of(position, 0)
        if side == 1:
            taken = jnp.logical_not(taken)
        found = []
        for h in range(heads):
            coef = jnp.where(taken, weight_ref[h, 1] * norm, 0.0)
            found.append(mix_ref[h] + coef * levels[1][heads // GROUP + h].astype(F32))
        return found

    def add(sums, side, c):
        return [
            total + weight_ref[h, 0] * norm * state_refs[c][side, h] for h, total in enumerate(sums)
        ]

    for side in range(2):
        reached = bit_of(position, top)

        @pl.when(reached if side == 1 else jnp.logical_not(reached))
        def _():
            sums = [sums_of(side)]

            def weight_of(c):
                weights = [pair_block(*sums[0][h : h + 2]) for h in range(0, heads, 2)]
                sums[0] = add(sums[0], side, c)
                return weights

            rows_of = (q_refs, [g_ref] * chunks, v_refs, k_refs)
            write_side(spans, side, side == 0, weight_of, rows_of, part_refs, outs, held, sems)
            other = sums_of(1 - side)
            for c in range(chunks) if side == 1 else reversed(range(chunks)):
                for h in range(heads):
                    base_ref[c, h] = other[h]
                other = add(other, 1 - side, c)


def late_side_kernel(spans, heads, top, weight_ref, g_ref, base_ref, *refs):
    chunks = len(spans)
    levels, refs = refs[:GROUP], refs[GROUP:]
    q_refs, refs = refs[:chunks], refs[chunks:]
    k_refs, refs = refs[:chunks], refs[chunks:]
    v_refs, refs = refs[:chunks], refs[chunks:]
    part_refs, refs = refs[:chunks], refs[chunks:]
    outs, (held, mix_ref, sems) = refs[-7:-3], refs[-3:]
    block = g_ref.shape[0]
    reached = bit_of(lax.axis_index("seq"), top)
    for side in range(2):

        @pl.when(reached if side == 0 else jnp.logical_not(reached))
        def _():
            gather_mixes(levels, top, side, weight_ref, block, mix_ref)

            def weight_of(c):
                sums = [base_ref[c, h] + mix_ref[h] for h in range(heads)]
                return [pair_block(*sums[h : h + 2]) for h in range(0, heads, 2)]

            rows_of = (q_refs, [g_ref] * chunks, v_refs, k_refs)
            write_side(spans, side, False, weight_of, rows_of, part_refs, outs, held, sems)


def exchange(totals, sends, local, late):
    depth = lax.axis_size("seq").bit_length() - 1
    heads, square = totals.shape[1], totals.shape[2:]
    share = heads // GROUP
    last = depth - 1

    def nexts(bit):
        if bit == last:
            return [pltpu.VMEM((share, *square), BF16)]
        return [pltpu.VMEM((2, share, *square), BF16), pltpu.VMEM((2, share, *square), F32)]

    def spread(mine, other):
        return [mine, *[swap(mine if m == 1 else other, "seq", m) for m in range(1, GROUP)]]

    one = pltpu.VMEM((share, *square), BF16)
    got = [swap(sends[m - 1], "seq", m) for m in FIRST]
    fillers = [local(c, sends[0]) for c in late]
    mine, other, sent, *sums = call(
        functools.partial(owner_kernel, last == 2),
        [pltpu.VMEM((share + heads, *square), BF16), one, *nexts(2)],
        [totals, *got, *fillers],
        [VMEM] * GROUP + [ANY] * len(fillers),
        10**6,
    )
    levels = spread(mine, other)
    for bit in range(2, last):
        found, sent, *sums = call(
            functools.partial(climb_kernel, bit, bit + 1 == last),
            [one, *nexts(bit + 1)],
            [swap(sent, "seq", 1 << bit), *sums],
            [VMEM] * 2,
            10**6,
        )
        levels += spread(found, found)
    found = tie(swap(sent, "seq", 1 << last), mine, flops=12 * 10**8)
    levels += spread(found, found)
    return levels, fillers


def per_device(inputs, w_qkv, level_weight, grad_out):
    rows, width = grad_out.shape
    heads = level_weight.shape[0]
    size = width // heads
    parts = lax.axis_size("head")
    edges = [rows * sum(SHARES[:c]) // sum(SHARES) for c in range(CHUNKS + 1)]
    spans = list(zip(edges[:-1], edges[1:]))
    depth = inputs.shape[1]
    mine = load(inputs, spans[:1])
    mine = [*mine, *load(inputs, spans[1:], mine)]
    grads, weights = call(
        functools.partial(load_weights_kernel, parts),
        [pltpu.VMEM((rows, width), BF16), pltpu.VMEM((parts * depth, 3 * width), BF16)],
        [
            pltpu.with_memory_space_constraint(grad_out, pltpu.HBM),
            pltpu.with_memory_space_constraint(w_qkv, pltpu.HBM),
            mine[1],
        ],
        [HBM, HBM, ANY],
        0,
        [pltpu.SemaphoreType.DMA((3 * parts + 1,))],
        limit=2,
        moved=4 * (grad_out.size + w_qkv.size),
    )
    top, *lows = [1 << b for b in reversed(range(parts.bit_length() - 1))]
    arrived = [swap(piece, "head", top) for piece in mine]
    arrived[0] = tie(arrived[0], weights)
    whole = {0: inputs}
    for low in lows:
        for k in sorted(whole):
            whole[k | low] = swap(whole[k], "head", low)
    state = pltpu.VMEM((2, heads, size, size), F32)
    qs, ks, vs, states, locals_ = [], [], [], [], []

    def local(c, after):
        chunk = spans[c][1] - spans[c][0]
        return call(
            functools.partial(local_kernel, spans[c], heads),
            [pltpu.VMEM((4, chunk, width), F32)],
            [level_weight, qs[c], ks[c], vs[c], grads, after],
            [SMEM] + [VMEM] * 4 + [ANY],
            100 * chunk * chunk * width if c >= CHUNKS - 2 else 0,
        )[0]

    after = None
    for c in range(CHUNKS):
        pieces = {**whole, 0: mine[c]}
        pieces[top] = arrived[c] if after is None else tie(arrived[c], after)
        for low in lows:
            for k in [k for k in sorted(pieces) if k & top]:
                pieces[k | low] = swap(pieces[k], "head", low)
        segments = [pieces[k] for k in sorted(pieces)]
        span = spans[c]
        chunk = span[1] - span[0]
        flat = pltpu.VMEM((chunk, width), BF16)
        if c < CHUNKS - 1:
            if c > 0:
                locals_.append(local(c - 1, pieces[top]))
            operands = [weights, grads, *segments, *locals_[-1:]]
            got = call(
                functools.partial(project_kernel, span, len(segments), heads),
                [flat, flat, flat, state],
                operands,
                [VMEM] * (2 + len(segments)) + [ANY] * len(locals_[-1:]),
                0,
            )
        else:
            operands = [weights, *segments[:-1], *states]
            begun, before = call(
                functools.partial(early_kernel, span, len(segments) - 1),
                [pltpu.VMEM((chunk, 3 * width), F32), state],
                operands,
                [VMEM] * len(operands),
                0,
            )
            got = call(
                functools.partial(last_kernel, span, heads),
                [
                    flat,
                    flat,
                    flat,
                    state,
                    state,
                    *[pltpu.VMEM((2, heads // GROUP, size, size), BF16)] * (GROUP - 1),
                ],
                [weights, grads, begun, before, segments[-1]],
                [VMEM] * 5,
                0,
            )
        qs.append(got[0])
        ks.append(got[1])
        vs.append(got[2])
        states.append(got[3])
        after = got[3]
    levels, fillers = exchange(got[4], got[5:], local, range(len(locals_), CHUNKS))
    locals_ += fillers
    shapes = [jax.ShapeDtypeStruct((rows, width), BF16)] * 4
    top = len(levels) // GROUP
    flats = [*qs, *ks, *vs]
    scratch = [
        pltpu.VMEM((2, rows, width), BF16),
        pltpu.VMEM((heads, size, size), F32),
        pltpu.SemaphoreType.DMA((2, CHUNKS)),
    ]
    operands = [level_weight, grads, *levels[:-GROUP], *flats, *states, *locals_]
    *written, base = call(
        functools.partial(early_side_kernel, spans, heads, top),
        [*shapes, pltpu.VMEM((CHUNKS, heads, size, size), F32)],
        operands,
        [SMEM] + [VMEM] * (len(operands) - 1),
        0,
        scratch,
        [ANY] * 4 + [VMEM],
        8,
    )
    operands = [level_weight, grads, base, *levels[-GROUP:], *flats, *locals_]
    return call(
        functools.partial(late_side_kernel, spans, heads, top),
        shapes,
        [*operands, *written],
        [SMEM] + [VMEM] * (len(operands) - 1) + [ANY] * 4,
        0,
        scratch,
        [ANY] * 4,
        8,
        aliases={len(operands) + j: j for j in range(4)},
    )


def solution(mesh):
    in_specs = (P("seq", "head"), P(None, None, "head"), P("head", None), P("seq", "head"))
    out_specs = (P("seq", "head"), P("seq", "head"), P("seq", "head"), P("seq", "head"))
    return jax.shard_map(
        per_device, mesh=mesh, in_specs=in_specs, out_specs=out_specs, check_vma=False
    )
```

```python
import functools
import math

import jax
import jax.numpy as jnp
from jax import lax
from jax.experimental import pallas as pl
from jax.experimental.pallas import tpu as pltpu
from jax.sharding import PartitionSpec as P

SHARES = (10, 12, 13, 14, 15)
CHUNKS = len(SHARES)
GROUP = 4
FIRST = (3, 2, 1)
MIB = 2**20
VMEM = pl.BlockSpec(memory_space=pltpu.VMEM)
SMEM = pl.BlockSpec(memory_space=pltpu.SMEM)
ANY = pl.BlockSpec(memory_space=pl.ANY)
HBM = pl.BlockSpec(memory_space=pltpu.HBM)
NN = (((1,), (0,)), ((), ()))
NT = (((1,), (1,)), ((), ()))
TN = (((0,), (0,)), ((), ()))
BF16 = jnp.bfloat16
F32 = jnp.float32


def dot(a, b, dims=NN):
    return lax.dot_general(a, b, dims, preferred_element_type=F32)


def swap(value, axis, mask):
    pairs = [(source, source ^ mask) for source in range(lax.axis_size(axis))]
    return lax.ppermute(value, axis, pairs)


def bit_of(position, bit):
    return lax.rem(position // 2**bit, 2) == 1


def call(kernel, outs, operands, specs, flops, scratch=(), out_specs=None, limit=4, moved=0, aliases=()):
    return pl.pallas_call(
        kernel,
        out_shape=outs,
        in_specs=specs,
        out_specs=[VMEM] * len(outs) if out_specs is None else out_specs,
        scratch_shapes=scratch,
        input_output_aliases=dict(aliases),
        compiler_params=pltpu.CompilerParams(vmem_limit_bytes=limit * MIB),
        cost_estimate=pl.CostEstimate(flops=flops, bytes_accessed=moved, transcendentals=0),
    )(*operands)


def load_kernel(spans, x_ref, *refs):
    outs, sems = refs[-len(spans) - 1 : -1], refs[-1]
    copies = []
    for i, (first, last) in enumerate(spans):
        rows = x_ref.at[pl.ds(first, last - first)]
        copies.append(pltpu.make_async_copy(rows, outs[i], sems.at[i]))
    for copy in copies:
        copy.start()
    for copy in copies:
        copy.wait()


def load(source, spans, after=()):
    return call(
        functools.partial(load_kernel, spans),
        [pltpu.VMEM((last - first, *source.shape[1:]), BF16) for first, last in spans],
        [pltpu.with_memory_space_constraint(source, pltpu.HBM), *after],
        [HBM] + [ANY] * len(after),
        0,
        [pltpu.SemaphoreType.DMA((len(spans),))],
        limit=2,
        moved=4 * source.size,
    )


def load_weights_kernel(parts, g_ref, w_ref, after_ref, g_out, w_out, sems):
    me = lax.axis_index("head")
    depth = w_ref.shape[1] // parts
    width = w_ref.shape[2]
    copies = [pltpu.make_async_copy(g_ref, g_out, sems.at[3 * parts])]
    for k in range(parts):
        rows = pl.ds(pl.multiple_of((me ^ k) * depth, depth), depth)
        for j in range(3):
            copies.append(
                pltpu.make_async_copy(
                    w_ref.at[j, rows],
                    w_out.at[pl.ds(k * depth, depth), pl.ds(j * width, width)],
                    sems.at[3 * k + j],
                )
            )
    for copy in copies:
        copy.start()
    for copy in copies:
        copy.wait()


def tie_kernel(value_ref, *refs):
    del value_ref, refs


def tie(value, *after, flops=0):
    return pl.pallas_call(
        tie_kernel,
        out_shape=pltpu.VMEM(value.shape, value.dtype),
        in_specs=[VMEM] + [ANY] * len(after),
        out_specs=VMEM,
        input_output_aliases={0: 0},
        compiler_params=pltpu.CompilerParams(vmem_limit_bytes=MIB),
        cost_estimate=pl.CostEstimate(flops=flops, bytes_accessed=0, transcendentals=0),
    )(value, *after)


def beside(refs, span):
    count = span[1] - span[0]
    found = [ref[...] if ref.shape[0] == count else ref[span[0] : span[1], :] for ref in refs]
    return found[0] if len(found) == 1 else jnp.concatenate(found, axis=1)


def write_states(span, heads, q_ref, k_ref, v_ref, g_ref, state_ref):
    size = q_ref.shape[1] // heads
    for h in range(heads):
        cols = slice(h * size, (h + 1) * size)
        state_ref[0, h] = dot(k_ref[:, cols], v_ref[:, cols], TN)
        state_ref[1, h] = dot(q_ref[:, cols], g_ref[span[0] : span[1], cols], TN)


def early_kernel(span, count, w_ref, *refs):
    segments, states = refs[:count], refs[count:-2]
    total_ref, sum_ref = refs[-2:]
    rows = beside(segments, span)
    total_ref[...] = dot(rows, w_ref[: rows.shape[1], :])
    sums = states[0][...]
    for state in states[1:]:
        sums = sums + state[...]
    sum_ref[...] = sums


def project_kernel(span, count, heads, w_ref, g_ref, *refs):
    outs, state_ref = refs[-4:-1], refs[-1]
    width = outs[0].shape[1]
    total = dot(beside(refs[:count], span), w_ref[...])
    for j, out_ref in enumerate(outs):
        out_ref[...] = total[:, j * width : (j + 1) * width].astype(BF16)
    write_states(span, heads, *outs, g_ref, state_ref)


def last_kernel(span, heads, w_ref, g_ref, part_ref, sum_ref, late_ref, *refs):
    outs, state_ref, total_ref, sends = refs[:3], refs[3], refs[4], refs[5:]
    width = outs[0].shape[1]
    start = w_ref.shape[0] - late_ref.shape[1]
    total = part_ref[...] + dot(late_ref[...], w_ref[start:, :])
    for j, out_ref in enumerate(outs):
        out_ref[...] = total[:, j * width : (j + 1) * width].astype(BF16)
    write_states(span, heads, *outs, g_ref, state_ref)
    share = heads // GROUP
    place = lax.rem(lax.axis_index("seq"), GROUP)
    total_ref[...] = sum_ref[...] + state_ref[...]
    for m, send in enumerate(sends, 1):
        for s in range(2):
            for e in range(share):
                send[s, e] = total_ref[s, (place ^ m) * share + e].astype(BF16)


def local_kernel(span, heads, weight_ref, q_ref, k_ref, v_ref, g_ref, after_ref, out_ref):
    rows = q_ref.shape[0]
    size = q_ref.shape[1] // heads
    norm = 1.0 / math.sqrt(size * g_ref.shape[0])
    at = lax.broadcasted_iota(jnp.int32, (rows, rows), 0)
    of = lax.broadcasted_iota(jnp.int32, (rows, rows), 1)
    columns = [slice(h * size, (h + 1) * size) for h in range(heads)]
    masked = []
    for h, cols in enumerate(columns):
        q, k, v = q_ref[:, cols], k_ref[:, cols], v_ref[:, cols]
        g = g_ref[span[0] : span[1], cols]
        scale = weight_ref[h, 0] * norm
        pairs = [(q, k, at >= of), (g, v, at >= of)]
        if 2 * h >= heads:
            pairs += [(v, g, of >= at), (k, q, of >= at)]
        masked.append(
            [
                jnp.where(causal, dot(left, right, NT) * scale, 0.0).astype(BF16)
                for left, right, causal in pairs
            ]
        )
    for h, cols in enumerate(columns):
        q, k, v = q_ref[:, cols], k_ref[:, cols], v_ref[:, cols]
        g = g_ref[span[0] : span[1], cols]
        attend, grad = masked[h][:2]
        out_ref[0, :, cols] = dot(attend, v)
        out_ref[1, :, cols] = dot(grad, k)
        if 2 * h >= heads:
            out_ref[2, :, cols] = dot(masked[h][2], q)
            out_ref[3, :, cols] = dot(masked[h][3], g)
        else:
            out_ref[2, :, cols] = dot(grad, q, TN)
            out_ref[3, :, cols] = dot(attend, g, TN)


def owner_kernel(final, total_ref, *refs):
    got, refs = dict(zip(FIRST, refs)), refs[GROUP - 1 :]
    near_ref, far_ref, *nexts = refs[-3 if final else -4 :]
    position = lax.axis_index("seq")
    place = lax.rem(position, GROUP)
    heads = total_ref.shape[1]
    share = heads // GROUP
    odd, high = bit_of(position, 0), bit_of(position, 1)
    for e in range(share):
        mine, other = [], []
        for s in range(2):
            mine.append(total_ref[s, place * share + e] + got[1][s, e].astype(F32))
            other.append(got[2][s, e].astype(F32) + got[3][s, e].astype(F32))
        sums = [mine[s] + other[s] for s in range(2)]
        write_next(sums, e, 2, final, *nexts)
        near_ref[e] = jnp.where(high, other[0], other[1]).astype(BF16)
        far_ref[e] = jnp.where(high, mine[1], mine[0]).astype(BF16)
    for h in range(heads):
        near_ref[share + h] = jnp.where(odd, total_ref[1, h], total_ref[0, h]).astype(BF16)


def write_next(sums, e, bit, final, next_ref, sum_ref=None):
    if final:
        value = jnp.where(bit_of(lax.axis_index("seq"), bit), sums[1], sums[0])
        next_ref[e] = value.astype(BF16)
        return
    for s in range(2):
        sum_ref[s, e] = sums[s]
        next_ref[s, e] = sums[s].astype(BF16)


def climb_kernel(bit, next_final, got_ref, old_ref, level_ref, *nexts):
    on = bit_of(lax.axis_index("seq"), bit)
    for e in range(got_ref.shape[1]):
        both = [got_ref[s, e].astype(F32) for s in range(2)]
        level_ref[e] = jnp.where(on, both[0], both[1]).astype(BF16)
        sums = [old_ref[s, e] + both[s] for s in range(2)]
        write_next(sums, e, bit + 1, next_final, *nexts)


def pair_block(first, second):
    zero = jnp.zeros(first.shape, BF16)
    top = jnp.concatenate([first.astype(BF16), zero], axis=1)
    bottom = jnp.concatenate([zero, second.astype(BF16)], axis=1)
    return jnp.concatenate([top, bottom], axis=0)


def gather_mixes(levels, first, side, weight_ref, block, mix_ref):
    position = lax.axis_index("seq")
    place = lax.rem(position, GROUP)
    heads, size = mix_ref.shape[:2]
    share = heads // GROUP
    for m in range(GROUP):
        for e in range(share):
            h = (place ^ m) * share + e
            total = None
            for b in range(len(levels) // GROUP):
                level = first + b
                coef = weight_ref[h, level + 1] * (1.0 / math.sqrt(size * block * 2**level))
                taken = bit_of(position, level)
                if side == 1:
                    taken = jnp.logical_not(taken)
                term = jnp.where(taken, coef, 0.0) * levels[b * GROUP + m][e].astype(F32)
                total = term if total is None else total + term
            mix_ref[h] = total


def write_side(spans, side, ascending, weight_of, rows_of, part_refs, outs, held, sems):
    chunks = len(spans)
    size = held.shape[-1]
    copies = []
    for c in range(chunks) if ascending else reversed(range(chunks)):
        span = slice(*spans[c])
        weights = weight_of(c)
        for j in range(2):
            ref = rows_of[2 * side + j][c]
            rows = span if ref.shape[0] != spans[c][1] - spans[c][0] else slice(None)
            for p, weight in enumerate(weights):
                cols = slice(p * weight.shape[0], (p + 1) * weight.shape[0])
                term = dot(ref[rows, cols], weight, NT if 2 * side + j in (1, 2) else NN)
                held[j, span, cols] = (term + part_refs[c][2 * side + j, :, cols]).astype(BF16)
            copy = pltpu.make_async_copy(
                held.at[j, span], outs[2 * side + j].at[span], sems.at[j, c]
            )
            copy.start()
            copies.append(copy)
    for copy in copies:
        copy.wait()


def early_side_kernel(spans, heads, top, weight_ref, g_ref, *refs):
    chunks = len(spans)
    levels, refs = refs[: (top - 1) * GROUP], refs[(top - 1) * GROUP :]
    q_refs, refs = refs[:chunks], refs[chunks:]
    k_refs, refs = refs[:chunks], refs[chunks:]
    v_refs, refs = refs[:chunks], refs[chunks:]
    state_refs, refs = refs[:chunks], refs[chunks:]
    part_refs, refs = refs[:chunks], refs[chunks:]
    outs, (base_ref, held, mix_ref, sems) = refs[:4], refs[4:]
    position = lax.axis_index("seq")
    block = g_ref.shape[0]
    size = mix_ref.shape[-1]
    norm = 1.0 / math.sqrt(size * block)

    def sums_of(side):
        gather_mixes(levels, 1, side, weight_ref, block, mix_ref)
        taken = bit_of(position, 0)
        if side == 1:
            taken = jnp.logical_not(taken)
        found = []
        for h in range(heads):
            coef = jnp.where(taken, weight_ref[h, 1] * norm, 0.0)
            found.append(mix_ref[h] + coef * levels[1][heads // GROUP + h].astype(F32))
        return found

    def add(sums, side, c):
        return [
            total + weight_ref[h, 0] * norm * state_refs[c][side, h] for h, total in enumerate(sums)
        ]

    for side in range(2):
        reached = bit_of(position, top)

        @pl.when(reached if side == 1 else jnp.logical_not(reached))
        def _():
            sums = [sums_of(side)]

            def weight_of(c):
                weights = [pair_block(*sums[0][h : h + 2]) for h in range(0, heads, 2)]
                sums[0] = add(sums[0], side, c)
                return weights

            rows_of = (q_refs, [g_ref] * chunks, v_refs, k_refs)
            write_side(spans, side, side == 0, weight_of, rows_of, part_refs, outs, held, sems)
            other = sums_of(1 - side)
            for c in range(chunks) if side == 1 else reversed(range(chunks)):
                for h in range(heads):
                    base_ref[c, h] = other[h]
                other = add(other, 1 - side, c)


def late_side_kernel(spans, heads, top, weight_ref, g_ref, base_ref, *refs):
    chunks = len(spans)
    levels, refs = refs[:GROUP], refs[GROUP:]
    q_refs, refs = refs[:chunks], refs[chunks:]
    k_refs, refs = refs[:chunks], refs[chunks:]
    v_refs, refs = refs[:chunks], refs[chunks:]
    part_refs, refs = refs[:chunks], refs[chunks:]
    outs, (held, mix_ref, sems) = refs[-7:-3], refs[-3:]
    block = g_ref.shape[0]
    reached = bit_of(lax.axis_index("seq"), top)
    for side in range(2):

        @pl.when(reached if side == 0 else jnp.logical_not(reached))
        def _():
            gather_mixes(levels, top, side, weight_ref, block, mix_ref)

            def weight_of(c):
                sums = [base_ref[c, h] + mix_ref[h] for h in range(heads)]
                return [pair_block(*sums[h : h + 2]) for h in range(0, heads, 2)]

            rows_of = (q_refs, [g_ref] * chunks, v_refs, k_refs)
            write_side(spans, side, False, weight_of, rows_of, part_refs, outs, held, sems)


def exchange(totals, sends, local, late):
    depth = lax.axis_size("seq").bit_length() - 1
    heads, square = totals.shape[1], totals.shape[2:]
    share = heads // GROUP
    last = depth - 1

    def nexts(bit):
        if bit == last:
            return [pltpu.VMEM((share, *square), BF16)]
        return [pltpu.VMEM((2, share, *square), BF16), pltpu.VMEM((2, share, *square), F32)]

    def spread(mine, other):
        return [mine, *[swap(mine if m == 1 else other, "seq", m) for m in range(1, GROUP)]]

    one = pltpu.VMEM((share, *square), BF16)
    got = [swap(sends[m - 1], "seq", m) for m in FIRST]
    fillers = [local(c, sends[0]) for c in late]
    mine, other, sent, *sums = call(
        functools.partial(owner_kernel, last == 2),
        [pltpu.VMEM((share + heads, *square), BF16), one, *nexts(2)],
        [totals, *got, *fillers],
        [VMEM] * GROUP + [ANY] * len(fillers),
        10**6,
    )
    levels = spread(mine, other)
    for bit in range(2, last):
        found, sent, *sums = call(
            functools.partial(climb_kernel, bit, bit + 1 == last),
            [one, *nexts(bit + 1)],
            [swap(sent, "seq", 1 << bit), *sums],
            [VMEM] * 2,
            10**6,
        )
        levels += spread(found, found)
    found = tie(swap(sent, "seq", 1 << last), mine, flops=12 * 10**8)
    levels += spread(found, found)
    return levels, fillers


def per_device(inputs, w_qkv, level_weight, grad_out):
    rows, width = grad_out.shape
    heads = level_weight.shape[0]
    size = width // heads
    parts = lax.axis_size("head")
    edges = [rows * sum(SHARES[:c]) // sum(SHARES) for c in range(CHUNKS + 1)]
    spans = list(zip(edges[:-1], edges[1:]))
    depth = inputs.shape[1]
    mine = load(inputs, spans[:1])
    mine = [*mine, *load(inputs, spans[1:], mine)]
    grads, weights = call(
        functools.partial(load_weights_kernel, parts),
        [pltpu.VMEM((rows, width), BF16), pltpu.VMEM((parts * depth, 3 * width), BF16)],
        [
            pltpu.with_memory_space_constraint(grad_out, pltpu.HBM),
            pltpu.with_memory_space_constraint(w_qkv, pltpu.HBM),
            mine[1],
        ],
        [HBM, HBM, ANY],
        0,
        [pltpu.SemaphoreType.DMA((3 * parts + 1,))],
        limit=2,
        moved=4 * (grad_out.size + w_qkv.size),
    )
    top, *lows = [1 << b for b in reversed(range(parts.bit_length() - 1))]
    arrived = [swap(piece, "head", top) for piece in mine]
    arrived[0] = tie(arrived[0], weights)
    whole = {0: inputs}
    for low in lows:
        for k in sorted(whole):
            whole[k | low] = swap(whole[k], "head", low)
    state = pltpu.VMEM((2, heads, size, size), F32)
    qs, ks, vs, states, locals_ = [], [], [], [], []

    def local(c, after):
        chunk = spans[c][1] - spans[c][0]
        return call(
            functools.partial(local_kernel, spans[c], heads),
            [pltpu.VMEM((4, chunk, width), F32)],
            [level_weight, qs[c], ks[c], vs[c], grads, after],
            [SMEM] + [VMEM] * 4 + [ANY],
            100 * chunk * chunk * width if c >= CHUNKS - 2 else 0,
        )[0]

    after = None
    for c in range(CHUNKS):
        pieces = {**whole, 0: mine[c]}
        pieces[top] = arrived[c] if after is None else tie(arrived[c], after)
        for low in lows:
            for k in [k for k in sorted(pieces) if k & top]:
                pieces[k | low] = swap(pieces[k], "head", low)
        segments = [pieces[k] for k in sorted(pieces)]
        span = spans[c]
        chunk = span[1] - span[0]
        flat = pltpu.VMEM((chunk, width), BF16)
        if c < CHUNKS - 1:
            if c > 0:
                locals_.append(local(c - 1, pieces[top]))
            operands = [weights, grads, *segments, *locals_[-1:]]
            got = call(
                functools.partial(project_kernel, span, len(segments), heads),
                [flat, flat, flat, state],
                operands,
                [VMEM] * (2 + len(segments)) + [ANY] * len(locals_[-1:]),
                0,
            )
        else:
            operands = [weights, *segments[:-1], *states]
            begun, before = call(
                functools.partial(early_kernel, span, len(segments) - 1),
                [pltpu.VMEM((chunk, 3 * width), F32), state],
                operands,
                [VMEM] * len(operands),
                0,
            )
            got = call(
                functools.partial(last_kernel, span, heads),
                [
                    flat,
                    flat,
                    flat,
                    state,
                    state,
                    *[pltpu.VMEM((2, heads // GROUP, size, size), BF16)] * (GROUP - 1),
                ],
                [weights, grads, begun, before, segments[-1]],
                [VMEM] * 5,
                0,
            )
        qs.append(got[0])
        ks.append(got[1])
        vs.append(got[2])
        states.append(got[3])
        after = got[3]
    levels, fillers = exchange(got[4], got[5:], local, range(len(locals_), CHUNKS))
    locals_ += fillers
    shapes = [jax.ShapeDtypeStruct((rows, width), BF16)] * 4
    top = len(levels) // GROUP
    flats = [*qs, *ks, *vs]
    scratch = [
        pltpu.VMEM((2, rows, width), BF16),
        pltpu.VMEM((heads, size, size), F32),
        pltpu.SemaphoreType.DMA((2, CHUNKS)),
    ]
    operands = [level_weight, grads, *levels[:-GROUP], *flats, *states, *locals_]
    *written, base = call(
        functools.partial(early_side_kernel, spans, heads, top),
        [*shapes, pltpu.VMEM((CHUNKS, heads, size, size), F32)],
        operands,
        [SMEM] + [VMEM] * (len(operands) - 1),
        0,
        scratch,
        [ANY] * 4 + [VMEM],
        8,
    )
    operands = [level_weight, grads, base, *levels[-GROUP:], *flats, *locals_]
    return call(
        functools.partial(late_side_kernel, spans, heads, top),
        shapes,
        [*operands, *written],
        [SMEM] + [VMEM] * (len(operands) - 1) + [ANY] * 4,
        0,
        scratch,
        [ANY] * 4,
        8,
        aliases={len(operands) + j: j for j in range(4)},
    )


def solution(mesh):
    in_specs = (P("seq", "head"), P(None, None, "head"), P("head", None), P("seq", "head"))
    out_specs = (P("seq", "head"), P("seq", "head"), P("seq", "head"), P("seq", "head"))
    return jax.shard_map(
        per_device, mesh=mesh, in_specs=in_specs, out_specs=out_specs, check_vma=False
    )
```

```python
import functools
import math

import jax
import jax.numpy as jnp
from jax import lax
from jax.experimental import pallas as pl
from jax.experimental.pallas import tpu as pltpu
from jax.sharding import PartitionSpec as P

SHARES = (10, 12, 13, 14, 15)
CHUNKS = len(SHARES)
GROUP = 4
FIRST = (3, 2, 1)
MIB = 2**20
VMEM = pl.BlockSpec(memory_space=pltpu.VMEM)
SMEM = pl.BlockSpec(memory_space=pltpu.SMEM)
ANY = pl.BlockSpec(memory_space=pl.ANY)
HBM = pl.BlockSpec(memory_space=pltpu.HBM)
NN = (((1,), (0,)), ((), ()))
NT = (((1,), (1,)), ((), ()))
TN = (((0,), (0,)), ((), ()))
BF16 = jnp.bfloat16
F32 = jnp.float32


def dot(a, b, dims=NN):
    return lax.dot_general(a, b, dims, preferred_element_type=F32)


def swap(value, axis, mask):
    pairs = [(source, source ^ mask) for source in range(lax.axis_size(axis))]
    return lax.ppermute(value, axis, pairs)


def bit_of(position, bit):
    return lax.rem(position // 2**bit, 2) == 1


def call(kernel, outs, operands, specs, flops, scratch=(), out_specs=None, limit=4, moved=0, aliases=()):
    return pl.pallas_call(
        kernel,
        out_shape=outs,
        in_specs=specs,
        out_specs=[VMEM] * len(outs) if out_specs is None else out_specs,
        scratch_shapes=scratch,
        input_output_aliases=dict(aliases),
        compiler_params=pltpu.CompilerParams(vmem_limit_bytes=limit * MIB),
        cost_estimate=pl.CostEstimate(flops=flops, bytes_accessed=moved, transcendentals=0),
    )(*operands)


def load_kernel(spans, x_ref, *refs):
    outs, sems = refs[-len(spans) - 1 : -1], refs[-1]
    copies = []
    for i, (first, last) in enumerate(spans):
        rows = x_ref.at[pl.ds(first, last - first)]
        copies.append(pltpu.make_async_copy(rows, outs[i], sems.at[i]))
    for copy in copies:
        copy.start()
    for copy in copies:
        copy.wait()


def load(source, spans, after=()):
    return call(
        functools.partial(load_kernel, spans),
        [pltpu.VMEM((last - first, *source.shape[1:]), BF16) for first, last in spans],
        [pltpu.with_memory_space_constraint(source, pltpu.HBM), *after],
        [HBM] + [ANY] * len(after),
        0,
        [pltpu.SemaphoreType.DMA((len(spans),))],
        limit=2,
        moved=4 * source.size,
    )


def load_weights_kernel(parts, g_ref, w_ref, after_ref, g_out, w_out, sems):
    me = lax.axis_index("head")
    depth = w_ref.shape[1] // parts
    width = w_ref.shape[2]
    copies = [pltpu.make_async_copy(g_ref, g_out, sems.at[3 * parts])]
    for k in range(parts):
        rows = pl.ds(pl.multiple_of((me ^ k) * depth, depth), depth)
        for j in range(3):
            copies.append(
                pltpu.make_async_copy(
                    w_ref.at[j, rows],
                    w_out.at[pl.ds(k * depth, depth), pl.ds(j * width, width)],
                    sems.at[3 * k + j],
                )
            )
    for copy in copies:
        copy.start()
    for copy in copies:
        copy.wait()


def tie_kernel(value_ref, *refs):
    del value_ref, refs


def tie(value, *after, flops=0):
    return pl.pallas_call(
        tie_kernel,
        out_shape=pltpu.VMEM(value.shape, value.dtype),
        in_specs=[ANY] * (1 + len(after)),
        out_specs=ANY,
        input_output_aliases={0: 0},
        compiler_params=pltpu.CompilerParams(vmem_limit_bytes=MIB),
        cost_estimate=pl.CostEstimate(flops=flops, bytes_accessed=0, transcendentals=0),
    )(value, *after)


def beside(refs, span):
    count = span[1] - span[0]
    found = [ref[...] if ref.shape[0] == count else ref[span[0] : span[1], :] for ref in refs]
    return found[0] if len(found) == 1 else jnp.concatenate(found, axis=1)


def write_states(span, heads, q_ref, k_ref, v_ref, g_ref, state_ref):
    size = q_ref.shape[1] // heads
    for h in range(heads):
        cols = slice(h * size, (h + 1) * size)
        state_ref[0, h] = dot(k_ref[:, cols], v_ref[:, cols], TN)
        state_ref[1, h] = dot(q_ref[:, cols], g_ref[span[0] : span[1], cols], TN)


def early_kernel(span, count, w_ref, *refs):
    segments, states = refs[:count], refs[count:-2]
    total_ref, sum_ref = refs[-2:]
    rows = beside(segments, span)
    total_ref[...] = dot(rows, w_ref[: rows.shape[1], :])
    sums = states[0][...]
    for state in states[1:]:
        sums = sums + state[...]
    sum_ref[...] = sums


def project_kernel(span, count, heads, w_ref, g_ref, *refs):
    outs, state_ref = refs[-4:-1], refs[-1]
    width = outs[0].shape[1]
    total = dot(beside(refs[:count], span), w_ref[...])
    for j, out_ref in enumerate(outs):
        out_ref[...] = total[:, j * width : (j + 1) * width].astype(BF16)
    write_states(span, heads, *outs, g_ref, state_ref)


def last_kernel(span, heads, w_ref, g_ref, part_ref, sum_ref, late_ref, *refs):
    outs, state_ref, total_ref, sends = refs[:3], refs[3], refs[4], refs[5:]
    width = outs[0].shape[1]
    start = w_ref.shape[0] - late_ref.shape[1]
    total = part_ref[...] + dot(late_ref[...], w_ref[start:, :])
    for j, out_ref in enumerate(outs):
        out_ref[...] = total[:, j * width : (j + 1) * width].astype(BF16)
    write_states(span, heads, *outs, g_ref, state_ref)
    share = heads // GROUP
    place = lax.rem(lax.axis_index("seq"), GROUP)
    total_ref[...] = sum_ref[...] + state_ref[...]
    for m, send in enumerate(sends, 1):
        for s in range(2):
            for e in range(share):
                send[s, e] = total_ref[s, (place ^ m) * share + e].astype(BF16)


def local_kernel(span, heads, weight_ref, q_ref, k_ref, v_ref, g_ref, after_ref, out_ref):
    rows = q_ref.shape[0]
    size = q_ref.shape[1] // heads
    norm = 1.0 / math.sqrt(size * g_ref.shape[0])
    at = lax.broadcasted_iota(jnp.int32, (rows, rows), 0)
    of = lax.broadcasted_iota(jnp.int32, (rows, rows), 1)
    columns = [slice(h * size, (h + 1) * size) for h in range(heads)]
    masked = []
    for h, cols in enumerate(columns):
        q, k, v = q_ref[:, cols], k_ref[:, cols], v_ref[:, cols]
        g = g_ref[span[0] : span[1], cols]
        scale = weight_ref[h, 0] * norm
        masked.append(
            [
                jnp.where(at >= of, dot(left, right, NT) * scale, 0.0).astype(BF16)
                for left, right in ((q, k), (g, v))
            ]
        )
    for h, cols in enumerate(columns):
        q, k, v = q_ref[:, cols], k_ref[:, cols], v_ref[:, cols]
        g = g_ref[span[0] : span[1], cols]
        attend, grad = masked[h]
        out_ref[0, :, cols] = dot(attend, v)
        out_ref[1, :, cols] = dot(grad, k)
        out_ref[2, :, cols] = dot(grad, q, TN)
        out_ref[3, :, cols] = dot(attend, g, TN)


def owner_kernel(final, total_ref, *refs):
    got, refs = dict(zip(FIRST, refs)), refs[GROUP - 1 :]
    near_ref, far_ref, *nexts = refs[-3 if final else -4 :]
    position = lax.axis_index("seq")
    place = lax.rem(position, GROUP)
    heads = total_ref.shape[1]
    share = heads // GROUP
    odd, high = bit_of(position, 0), bit_of(position, 1)
    for e in range(share):
        mine, other = [], []
        for s in range(2):
            mine.append(total_ref[s, place * share + e] + got[1][s, e].astype(F32))
            other.append(got[2][s, e].astype(F32) + got[3][s, e].astype(F32))
        sums = [mine[s] + other[s] for s in range(2)]
        write_next(sums, e, 2, final, *nexts)
        near_ref[e] = jnp.where(high, other[0], other[1]).astype(BF16)
        far_ref[e] = jnp.where(high, mine[1], mine[0]).astype(BF16)
    for h in range(heads):
        near_ref[share + h] = jnp.where(odd, total_ref[1, h], total_ref[0, h]).astype(BF16)


def write_next(sums, e, bit, final, next_ref, sum_ref=None):
    if final:
        value = jnp.where(bit_of(lax.axis_index("seq"), bit), sums[1], sums[0])
        next_ref[e] = value.astype(BF16)
        return
    for s in range(2):
        sum_ref[s, e] = sums[s]
        next_ref[s, e] = sums[s].astype(BF16)


def climb_kernel(bit, next_final, got_ref, old_ref, level_ref, *nexts):
    on = bit_of(lax.axis_index("seq"), bit)
    for e in range(got_ref.shape[1]):
        both = [got_ref[s, e].astype(F32) for s in range(2)]
        level_ref[e] = jnp.where(on, both[0], both[1]).astype(BF16)
        sums = [old_ref[s, e] + both[s] for s in range(2)]
        write_next(sums, e, bit + 1, next_final, *nexts)


def pair_block(first, second):
    zero = jnp.zeros(first.shape, BF16)
    top = jnp.concatenate([first.astype(BF16), zero], axis=1)
    bottom = jnp.concatenate([zero, second.astype(BF16)], axis=1)
    return jnp.concatenate([top, bottom], axis=0)


def gather_mixes(levels, first, side, weight_ref, block, mix_ref):
    position = lax.axis_index("seq")
    place = lax.rem(position, GROUP)
    heads, size = mix_ref.shape[:2]
    share = heads // GROUP
    for m in range(GROUP):
        for e in range(share):
            h = (place ^ m) * share + e
            total = None
            for b in range(len(levels) // GROUP):
                level = first + b
                coef = weight_ref[h, level + 1] * (1.0 / math.sqrt(size * block * 2**level))
                taken = bit_of(position, level)
                if side == 1:
                    taken = jnp.logical_not(taken)
                term = jnp.where(taken, coef, 0.0) * levels[b * GROUP + m][e].astype(F32)
                total = term if total is None else total + term
            mix_ref[h] = total


def write_side(spans, side, ascending, weight_of, rows_of, part_refs, outs, held, sems):
    chunks = len(spans)
    size = held.shape[-1]
    copies = []
    for c in range(chunks) if ascending else reversed(range(chunks)):
        span = slice(*spans[c])
        weights = weight_of(c)
        for j in range(2):
            ref = rows_of[2 * side + j][c]
            rows = span if ref.shape[0] != spans[c][1] - spans[c][0] else slice(None)
            for p, weight in enumerate(weights):
                cols = slice(p * weight.shape[0], (p + 1) * weight.shape[0])
                term = dot(ref[rows, cols], weight, NT if 2 * side + j in (1, 2) else NN)
                held[j, span, cols] = (term + part_refs[c][2 * side + j, :, cols]).astype(BF16)
            copy = pltpu.make_async_copy(
                held.at[j, span], outs[2 * side + j].at[span], sems.at[j, c]
            )
            copy.start()
            copies.append(copy)
    for copy in copies:
        copy.wait()


def early_side_kernel(spans, heads, top, weight_ref, g_ref, *refs):
    chunks = len(spans)
    levels, refs = refs[: (top - 1) * GROUP], refs[(top - 1) * GROUP :]
    q_refs, refs = refs[:chunks], refs[chunks:]
    k_refs, refs = refs[:chunks], refs[chunks:]
    v_refs, refs = refs[:chunks], refs[chunks:]
    state_refs, refs = refs[:chunks], refs[chunks:]
    part_refs, refs = refs[:chunks], refs[chunks:]
    outs, (base_ref, held, mix_ref, sems) = refs[:4], refs[4:]
    position = lax.axis_index("seq")
    block = g_ref.shape[0]
    size = mix_ref.shape[-1]
    norm = 1.0 / math.sqrt(size * block)

    def sums_of(side):
        gather_mixes(levels, 1, side, weight_ref, block, mix_ref)
        taken = bit_of(position, 0)
        if side == 1:
            taken = jnp.logical_not(taken)
        found = []
        for h in range(heads):
            coef = jnp.where(taken, weight_ref[h, 1] * norm, 0.0)
            found.append(mix_ref[h] + coef * levels[1][heads // GROUP + h].astype(F32))
        return found

    def add(sums, side, c):
        return [
            total + weight_ref[h, 0] * norm * state_refs[c][side, h] for h, total in enumerate(sums)
        ]

    for side in range(2):
        reached = bit_of(position, top)

        @pl.when(reached if side == 1 else jnp.logical_not(reached))
        def _():
            sums = [sums_of(side)]

            def weight_of(c):
                weights = [pair_block(*sums[0][h : h + 2]) for h in range(0, heads, 2)]
                sums[0] = add(sums[0], side, c)
                return weights

            rows_of = (q_refs, [g_ref] * chunks, v_refs, k_refs)
            write_side(spans, side, side == 0, weight_of, rows_of, part_refs, outs, held, sems)
            other = sums_of(1 - side)
            for c in range(chunks) if side == 1 else reversed(range(chunks)):
                for h in range(heads):
                    base_ref[c, h] = other[h]
                other = add(other, 1 - side, c)


def late_side_kernel(spans, heads, top, weight_ref, g_ref, base_ref, *refs):
    chunks = len(spans)
    levels, refs = refs[:GROUP], refs[GROUP:]
    q_refs, refs = refs[:chunks], refs[chunks:]
    k_refs, refs = refs[:chunks], refs[chunks:]
    v_refs, refs = refs[:chunks], refs[chunks:]
    part_refs, refs = refs[:chunks], refs[chunks:]
    outs, (held, mix_ref, sems) = refs[-7:-3], refs[-3:]
    block = g_ref.shape[0]
    reached = bit_of(lax.axis_index("seq"), top)
    for side in range(2):

        @pl.when(reached if side == 0 else jnp.logical_not(reached))
        def _():
            gather_mixes(levels, top, side, weight_ref, block, mix_ref)

            def weight_of(c):
                sums = [base_ref[c, h] + mix_ref[h] for h in range(heads)]
                return [pair_block(*sums[h : h + 2]) for h in range(0, heads, 2)]

            rows_of = (q_refs, [g_ref] * chunks, v_refs, k_refs)
            write_side(spans, side, False, weight_of, rows_of, part_refs, outs, held, sems)


def exchange(totals, sends, local, late):
    depth = lax.axis_size("seq").bit_length() - 1
    heads, square = totals.shape[1], totals.shape[2:]
    share = heads // GROUP
    last = depth - 1

    def nexts(bit):
        if bit == last:
            return [pltpu.VMEM((share, *square), BF16)]
        return [pltpu.VMEM((2, share, *square), BF16), pltpu.VMEM((2, share, *square), F32)]

    def spread(mine, other):
        return [mine, *[swap(mine if m == 1 else other, "seq", m) for m in range(1, GROUP)]]

    one = pltpu.VMEM((share, *square), BF16)
    got = [swap(sends[m - 1], "seq", m) for m in FIRST]
    fillers = [local(c, sends[0]) for c in late]
    mine, other, sent, *sums = call(
        functools.partial(owner_kernel, last == 2),
        [pltpu.VMEM((share + heads, *square), BF16), one, *nexts(2)],
        [totals, *got, *fillers],
        [VMEM] * GROUP + [ANY] * len(fillers),
        10**6,
    )
    levels = spread(mine, other)
    for bit in range(2, last):
        found, sent, *sums = call(
            functools.partial(climb_kernel, bit, bit + 1 == last),
            [one, *nexts(bit + 1)],
            [swap(sent, "seq", 1 << bit), *sums],
            [VMEM] * 2,
            10**6,
        )
        levels += spread(found, found)
    found = tie(swap(sent, "seq", 1 << last), mine, flops=12 * 10**8)
    levels += spread(found, found)
    return levels, fillers


def per_device(inputs, w_qkv, level_weight, grad_out):
    rows, width = grad_out.shape
    heads = level_weight.shape[0]
    size = width // heads
    parts = lax.axis_size("head")
    edges = [rows * sum(SHARES[:c]) // sum(SHARES) for c in range(CHUNKS + 1)]
    spans = list(zip(edges[:-1], edges[1:]))
    depth = inputs.shape[1]
    mine = load(inputs, spans[:1])
    mine = [*mine, *load(inputs, spans[1:], mine)]
    grads, weights = call(
        functools.partial(load_weights_kernel, parts),
        [pltpu.VMEM((rows, width), BF16), pltpu.VMEM((parts * depth, 3 * width), BF16)],
        [
            pltpu.with_memory_space_constraint(grad_out, pltpu.HBM),
            pltpu.with_memory_space_constraint(w_qkv, pltpu.HBM),
            mine[1],
        ],
        [HBM, HBM, ANY],
        0,
        [pltpu.SemaphoreType.DMA((3 * parts + 1,))],
        limit=2,
        moved=4 * (grad_out.size + w_qkv.size),
    )
    top, *lows = [1 << b for b in reversed(range(parts.bit_length() - 1))]
    arrived = [swap(piece, "head", top) for piece in mine]
    arrived[0] = tie(arrived[0], weights)
    whole = {0: inputs}
    for low in lows:
        for k in sorted(whole):
            whole[k | low] = swap(whole[k], "head", low)
    state = pltpu.VMEM((2, heads, size, size), F32)
    qs, ks, vs, states, locals_ = [], [], [], [], []

    def local(c, after):
        chunk = spans[c][1] - spans[c][0]
        return call(
            functools.partial(local_kernel, spans[c], heads),
            [pltpu.VMEM((4, chunk, width), F32)],
            [level_weight, qs[c], ks[c], vs[c], grads, after],
            [SMEM] + [VMEM] * 4 + [ANY],
            100 * chunk * chunk * width if c >= CHUNKS - 2 else 0,
        )[0]

    after = None
    for c in range(CHUNKS):
        pieces = {**whole, 0: mine[c]}
        pieces[top] = arrived[c] if after is None else tie(arrived[c], after)
        for low in lows:
            for k in [k for k in sorted(pieces) if k & top]:
                pieces[k | low] = swap(pieces[k], "head", low)
        segments = [pieces[k] for k in sorted(pieces)]
        span = spans[c]
        chunk = span[1] - span[0]
        flat = pltpu.VMEM((chunk, width), BF16)
        if c < CHUNKS - 1:
            if c > 0:
                locals_.append(local(c - 1, pieces[top]))
            operands = [weights, grads, *segments, *locals_[-1:]]
            got = call(
                functools.partial(project_kernel, span, len(segments), heads),
                [flat, flat, flat, state],
                operands,
                [VMEM] * (2 + len(segments)) + [ANY] * len(locals_[-1:]),
                0,
            )
        else:
            operands = [weights, *segments[:-1], *states]
            begun, before = call(
                functools.partial(early_kernel, span, len(segments) - 1),
                [pltpu.VMEM((chunk, 3 * width), F32), state],
                operands,
                [VMEM] * len(operands),
                0,
            )
            got = call(
                functools.partial(last_kernel, span, heads),
                [
                    flat,
                    flat,
                    flat,
                    state,
                    state,
                    *[pltpu.VMEM((2, heads // GROUP, size, size), BF16)] * (GROUP - 1),
                ],
                [weights, grads, begun, before, segments[-1]],
                [VMEM] * 5,
                0,
            )
        qs.append(got[0])
        ks.append(got[1])
        vs.append(got[2])
        states.append(got[3])
        after = got[3]
    levels, fillers = exchange(got[4], got[5:], local, range(len(locals_), CHUNKS))
    locals_ += fillers
    shapes = [jax.ShapeDtypeStruct((rows, width), BF16)] * 4
    top = len(levels) // GROUP
    flats = [*qs, *ks, *vs]
    scratch = [
        pltpu.VMEM((2, rows, width), BF16),
        pltpu.VMEM((heads, size, size), F32),
        pltpu.SemaphoreType.DMA((2, CHUNKS)),
    ]
    operands = [level_weight, grads, *levels[:-GROUP], *flats, *states, *locals_]
    *written, base = call(
        functools.partial(early_side_kernel, spans, heads, top),
        [*shapes, pltpu.VMEM((CHUNKS, heads, size, size), F32)],
        operands,
        [SMEM] + [VMEM] * (len(operands) - 1),
        0,
        scratch,
        [ANY] * 4 + [VMEM],
        8,
    )
    operands = [level_weight, grads, base, *levels[-GROUP:], *flats, *locals_]
    return call(
        functools.partial(late_side_kernel, spans, heads, top),
        shapes,
        [*operands, *written],
        [SMEM] + [VMEM] * (len(operands) - 1) + [ANY] * 4,
        0,
        scratch,
        [ANY] * 4,
        8,
        aliases={len(operands) + j: j for j in range(4)},
    )


def solution(mesh):
    in_specs = (P("seq", "head"), P(None, None, "head"), P("head", None), P("seq", "head"))
    out_specs = (P("seq", "head"), P("seq", "head"), P("seq", "head"), P("seq", "head"))
    return jax.shard_map(
        per_device, mesh=mesh, in_specs=in_specs, out_specs=out_specs, check_vma=False
    )
```

```python
import functools
import math

import jax
import jax.numpy as jnp
from jax import lax
from jax.experimental import pallas as pl
from jax.experimental.pallas import tpu as pltpu
from jax.sharding import PartitionSpec as P

SHARES = (10, 12, 13, 14, 15)
CHUNKS = len(SHARES)
GROUP = 4
FIRST = (3, 2, 1)
MIB = 2**20
VMEM = pl.BlockSpec(memory_space=pltpu.VMEM)
SMEM = pl.BlockSpec(memory_space=pltpu.SMEM)
ANY = pl.BlockSpec(memory_space=pl.ANY)
HBM = pl.BlockSpec(memory_space=pltpu.HBM)
NN = (((1,), (0,)), ((), ()))
NT = (((1,), (1,)), ((), ()))
TN = (((0,), (0,)), ((), ()))
BF16 = jnp.bfloat16
F32 = jnp.float32


def dot(a, b, dims=NN):
    return lax.dot_general(a, b, dims, preferred_element_type=F32)


def swap(value, axis, mask):
    pairs = [(source, source ^ mask) for source in range(lax.axis_size(axis))]
    return lax.ppermute(value, axis, pairs)


def bit_of(position, bit):
    return lax.rem(position // 2**bit, 2) == 1


def call(kernel, outs, operands, specs, flops, scratch=(), out_specs=None, limit=4, moved=0, aliases=()):
    return pl.pallas_call(
        kernel,
        out_shape=outs,
        in_specs=specs,
        out_specs=[VMEM] * len(outs) if out_specs is None else out_specs,
        scratch_shapes=scratch,
        input_output_aliases=dict(aliases),
        compiler_params=pltpu.CompilerParams(vmem_limit_bytes=limit * MIB),
        cost_estimate=pl.CostEstimate(flops=flops, bytes_accessed=moved, transcendentals=0),
    )(*operands)


def load_kernel(spans, x_ref, *refs):
    outs, sems = refs[-len(spans) - 1 : -1], refs[-1]
    copies = []
    for i, (first, last) in enumerate(spans):
        rows = x_ref.at[pl.ds(first, last - first)]
        copies.append(pltpu.make_async_copy(rows, outs[i], sems.at[i]))
    for copy in copies:
        copy.start()
    for copy in copies:
        copy.wait()


def load(source, spans, after=()):
    return call(
        functools.partial(load_kernel, spans),
        [pltpu.VMEM((last - first, *source.shape[1:]), BF16) for first, last in spans],
        [pltpu.with_memory_space_constraint(source, pltpu.HBM), *after],
        [HBM] + [ANY] * len(after),
        0,
        [pltpu.SemaphoreType.DMA((len(spans),))],
        limit=2,
        moved=4 * source.size,
    )


def load_weights_kernel(parts, g_ref, w_ref, after_ref, g_out, w_out, sems):
    me = lax.axis_index("head")
    depth = w_ref.shape[1] // parts
    width = w_ref.shape[2]
    copies = [pltpu.make_async_copy(g_ref, g_out, sems.at[3 * parts])]
    for k in range(parts):
        rows = pl.ds(pl.multiple_of((me ^ k) * depth, depth), depth)
        for j in range(3):
            copies.append(
                pltpu.make_async_copy(
                    w_ref.at[j, rows],
                    w_out.at[pl.ds(k * depth, depth), pl.ds(j * width, width)],
                    sems.at[3 * k + j],
                )
            )
    for copy in copies:
        copy.start()
    for copy in copies:
        copy.wait()


def tie_kernel(value_ref, *refs):
    del value_ref, refs


def tie(value, *after, flops=0):
    return pl.pallas_call(
        tie_kernel,
        out_shape=pltpu.VMEM(value.shape, value.dtype),
        in_specs=[ANY] * (1 + len(after)),
        out_specs=ANY,
        input_output_aliases={0: 0},
        compiler_params=pltpu.CompilerParams(vmem_limit_bytes=MIB),
        cost_estimate=pl.CostEstimate(flops=flops, bytes_accessed=0, transcendentals=0),
    )(value, *after)


def beside(refs, span):
    count = span[1] - span[0]
    found = [ref[...] if ref.shape[0] == count else ref[span[0] : span[1], :] for ref in refs]
    return found[0] if len(found) == 1 else jnp.concatenate(found, axis=1)


def write_states(span, heads, q_ref, k_ref, v_ref, g_ref, state_ref):
    size = q_ref.shape[1] // heads
    for h in range(0, heads, 2):
        cols = slice(h * size, (h + 2) * size)
        for s, (left, right) in enumerate(
            ((k_ref[:, cols], v_ref[:, cols]), (q_ref[:, cols], g_ref[span[0] : span[1], cols]))
        ):
            both = dot(left, right, TN)
            state_ref[s, h] = both[:size, :size]
            state_ref[s, h + 1] = both[size:, size:]


def early_kernel(span, count, w_ref, *refs):
    segments, states = refs[:count], refs[count:-2]
    total_ref, sum_ref = refs[-2:]
    rows = beside(segments, span)
    total_ref[...] = dot(rows, w_ref[: rows.shape[1], :])
    sums = states[0][...]
    for state in states[1:]:
        sums = sums + state[...]
    sum_ref[...] = sums


def project_kernel(span, count, heads, w_ref, g_ref, *refs):
    outs, state_ref = refs[-4:-1], refs[-1]
    width = outs[0].shape[1]
    total = dot(beside(refs[:count], span), w_ref[...])
    for j, out_ref in enumerate(outs):
        out_ref[...] = total[:, j * width : (j + 1) * width].astype(BF16)
    write_states(span, heads, *outs, g_ref, state_ref)


def last_kernel(span, heads, w_ref, g_ref, part_ref, sum_ref, late_ref, *refs):
    outs, state_ref, total_ref, sends = refs[:3], refs[3], refs[4], refs[5:]
    width = outs[0].shape[1]
    start = w_ref.shape[0] - late_ref.shape[1]
    total = part_ref[...] + dot(late_ref[...], w_ref[start:, :])
    for j, out_ref in enumerate(outs):
        out_ref[...] = total[:, j * width : (j + 1) * width].astype(BF16)
    write_states(span, heads, *outs, g_ref, state_ref)
    share = heads // GROUP
    place = lax.rem(lax.axis_index("seq"), GROUP)
    total_ref[...] = sum_ref[...] + state_ref[...]
    for m, send in enumerate(sends, 1):
        for s in range(2):
            for e in range(share):
                send[s, e] = total_ref[s, (place ^ m) * share + e].astype(BF16)


def local_kernel(span, heads, weight_ref, q_ref, k_ref, v_ref, g_ref, after_ref, out_ref):
    rows = q_ref.shape[0]
    size = q_ref.shape[1] // heads
    norm = 1.0 / math.sqrt(size * g_ref.shape[0])
    at = lax.broadcasted_iota(jnp.int32, (rows, rows), 0)
    of = lax.broadcasted_iota(jnp.int32, (rows, rows), 1)
    columns = [slice(h * size, (h + 1) * size) for h in range(heads)]
    masked = []
    for h, cols in enumerate(columns):
        q, k, v = q_ref[:, cols], k_ref[:, cols], v_ref[:, cols]
        g = g_ref[span[0] : span[1], cols]
        scale = weight_ref[h, 0] * norm
        masked.append(
            [
                jnp.where(at >= of, dot(left, right, NT) * scale, 0.0).astype(BF16)
                for left, right in ((q, k), (g, v))
            ]
        )
    for h, cols in enumerate(columns):
        q, k, v = q_ref[:, cols], k_ref[:, cols], v_ref[:, cols]
        g = g_ref[span[0] : span[1], cols]
        attend, grad = masked[h]
        out_ref[0, :, cols] = dot(attend, v)
        out_ref[1, :, cols] = dot(grad, k)
        out_ref[2, :, cols] = dot(grad, q, TN)
        out_ref[3, :, cols] = dot(attend, g, TN)


def owner_kernel(final, total_ref, *refs):
    got, refs = dict(zip(FIRST, refs)), refs[GROUP - 1 :]
    near_ref, far_ref, *nexts = refs[-3 if final else -4 :]
    position = lax.axis_index("seq")
    place = lax.rem(position, GROUP)
    heads = total_ref.shape[1]
    share = heads // GROUP
    odd, high = bit_of(position, 0), bit_of(position, 1)
    for e in range(share):
        mine, other = [], []
        for s in range(2):
            mine.append(total_ref[s, place * share + e] + got[1][s, e].astype(F32))
            other.append(got[2][s, e].astype(F32) + got[3][s, e].astype(F32))
        sums = [mine[s] + other[s] for s in range(2)]
        write_next(sums, e, 2, final, *nexts)
        near_ref[e] = jnp.where(high, other[0], other[1]).astype(BF16)
        far_ref[e] = jnp.where(high, mine[1], mine[0]).astype(BF16)
    for h in range(heads):
        near_ref[share + h] = jnp.where(odd, total_ref[1, h], total_ref[0, h]).astype(BF16)


def write_next(sums, e, bit, final, next_ref, sum_ref=None):
    if final:
        value = jnp.where(bit_of(lax.axis_index("seq"), bit), sums[1], sums[0])
        next_ref[e] = value.astype(BF16)
        return
    for s in range(2):
        sum_ref[s, e] = sums[s]
        next_ref[s, e] = sums[s].astype(BF16)


def climb_kernel(bit, next_final, got_ref, old_ref, level_ref, *nexts):
    on = bit_of(lax.axis_index("seq"), bit)
    for e in range(got_ref.shape[1]):
        both = [got_ref[s, e].astype(F32) for s in range(2)]
        level_ref[e] = jnp.where(on, both[0], both[1]).astype(BF16)
        sums = [old_ref[s, e] + both[s] for s in range(2)]
        write_next(sums, e, bit + 1, next_final, *nexts)


def pair_block(first, second):
    zero = jnp.zeros(first.shape, BF16)
    top = jnp.concatenate([first.astype(BF16), zero], axis=1)
    bottom = jnp.concatenate([zero, second.astype(BF16)], axis=1)
    return jnp.concatenate([top, bottom], axis=0)


def gather_mixes(levels, first, side, weight_ref, block, mix_ref):
    position = lax.axis_index("seq")
    place = lax.rem(position, GROUP)
    heads, size = mix_ref.shape[:2]
    share = heads // GROUP
    for m in range(GROUP):
        for e in range(share):
            h = (place ^ m) * share + e
            total = None
            for b in range(len(levels) // GROUP):
                level = first + b
                coef = weight_ref[h, level + 1] * (1.0 / math.sqrt(size * block * 2**level))
                taken = bit_of(position, level)
                if side == 1:
                    taken = jnp.logical_not(taken)
                term = jnp.where(taken, coef, 0.0) * levels[b * GROUP + m][e].astype(F32)
                total = term if total is None else total + term
            mix_ref[h] = total


def write_side(spans, side, ascending, weight_of, rows_of, part_refs, outs, held, sems):
    chunks = len(spans)
    size = held.shape[-1]
    copies = []
    for c in range(chunks) if ascending else reversed(range(chunks)):
        span = slice(*spans[c])
        weights = weight_of(c)
        for j in range(2):
            ref = rows_of[2 * side + j][c]
            rows = span if ref.shape[0] != spans[c][1] - spans[c][0] else slice(None)
            for p, weight in enumerate(weights):
                cols = slice(p * weight.shape[0], (p + 1) * weight.shape[0])
                term = dot(ref[rows, cols], weight, NT if 2 * side + j in (1, 2) else NN)
                held[j, span, cols] = (term + part_refs[c][2 * side + j, :, cols]).astype(BF16)
            copy = pltpu.make_async_copy(
                held.at[j, span], outs[2 * side + j].at[span], sems.at[j, c]
            )
            copy.start()
            copies.append(copy)
    for copy in copies:
        copy.wait()


def early_side_kernel(spans, heads, top, weight_ref, g_ref, *refs):
    chunks = len(spans)
    levels, refs = refs[: (top - 1) * GROUP], refs[(top - 1) * GROUP :]
    q_refs, refs = refs[:chunks], refs[chunks:]
    k_refs, refs = refs[:chunks], refs[chunks:]
    v_refs, refs = refs[:chunks], refs[chunks:]
    state_refs, refs = refs[:chunks], refs[chunks:]
    part_refs, refs = refs[:chunks], refs[chunks:]
    outs, (base_ref, held, mix_ref, sems) = refs[:4], refs[4:]
    position = lax.axis_index("seq")
    block = g_ref.shape[0]
    size = mix_ref.shape[-1]
    norm = 1.0 / math.sqrt(size * block)

    def sums_of(side):
        gather_mixes(levels, 1, side, weight_ref, block, mix_ref)
        taken = bit_of(position, 0)
        if side == 1:
            taken = jnp.logical_not(taken)
        found = []
        for h in range(heads):
            coef = jnp.where(taken, weight_ref[h, 1] * norm, 0.0)
            found.append(mix_ref[h] + coef * levels[1][heads // GROUP + h].astype(F32))
        return found

    def add(sums, side, c):
        return [
            total + weight_ref[h, 0] * norm * state_refs[c][side, h] for h, total in enumerate(sums)
        ]

    for side in range(2):
        reached = bit_of(position, top)

        @pl.when(reached if side == 1 else jnp.logical_not(reached))
        def _():
            sums = [sums_of(side)]

            def weight_of(c):
                weights = [pair_block(*sums[0][h : h + 2]) for h in range(0, heads, 2)]
                sums[0] = add(sums[0], side, c)
                return weights

            rows_of = (q_refs, [g_ref] * chunks, v_refs, k_refs)
            write_side(spans, side, side == 0, weight_of, rows_of, part_refs, outs, held, sems)
            other = sums_of(1 - side)
            for c in range(chunks) if side == 1 else reversed(range(chunks)):
                for h in range(heads):
                    base_ref[c, h] = other[h]
                other = add(other, 1 - side, c)


def late_side_kernel(spans, heads, top, weight_ref, g_ref, base_ref, *refs):
    chunks = len(spans)
    levels, refs = refs[:GROUP], refs[GROUP:]
    q_refs, refs = refs[:chunks], refs[chunks:]
    k_refs, refs = refs[:chunks], refs[chunks:]
    v_refs, refs = refs[:chunks], refs[chunks:]
    part_refs, refs = refs[:chunks], refs[chunks:]
    outs, (held, mix_ref, sems) = refs[-7:-3], refs[-3:]
    block = g_ref.shape[0]
    reached = bit_of(lax.axis_index("seq"), top)
    for side in range(2):

        @pl.when(reached if side == 0 else jnp.logical_not(reached))
        def _():
            gather_mixes(levels, top, side, weight_ref, block, mix_ref)

            def weight_of(c):
                sums = [base_ref[c, h] + mix_ref[h] for h in range(heads)]
                return [pair_block(*sums[h : h + 2]) for h in range(0, heads, 2)]

            rows_of = (q_refs, [g_ref] * chunks, v_refs, k_refs)
            write_side(spans, side, True, weight_of, rows_of, part_refs, outs, held, sems)


def exchange(totals, sends, local, late):
    depth = lax.axis_size("seq").bit_length() - 1
    heads, square = totals.shape[1], totals.shape[2:]
    share = heads // GROUP
    last = depth - 1

    def nexts(bit):
        if bit == last:
            return [pltpu.VMEM((share, *square), BF16)]
        return [pltpu.VMEM((2, share, *square), BF16), pltpu.VMEM((2, share, *square), F32)]

    def spread(mine, other):
        return [mine, *[swap(mine if m == 1 else other, "seq", m) for m in range(1, GROUP)]]

    one = pltpu.VMEM((share, *square), BF16)
    got = [swap(sends[m - 1], "seq", m) for m in FIRST]
    fillers = [local(c, sends[0]) for c in late]
    mine, other, sent, *sums = call(
        functools.partial(owner_kernel, last == 2),
        [pltpu.VMEM((share + heads, *square), BF16), one, *nexts(2)],
        [totals, *got, *fillers],
        [VMEM] * GROUP + [ANY] * len(fillers),
        10**6,
    )
    levels = spread(mine, other)
    for bit in range(2, last):
        found, sent, *sums = call(
            functools.partial(climb_kernel, bit, bit + 1 == last),
            [one, *nexts(bit + 1)],
            [swap(sent, "seq", 1 << bit), *sums],
            [VMEM] * 2,
            10**6,
        )
        levels += spread(found, found)
    found = tie(swap(sent, "seq", 1 << last), mine, flops=12 * 10**8)
    levels += spread(found, found)
    return levels, fillers


def per_device(inputs, w_qkv, level_weight, grad_out):
    rows, width = grad_out.shape
    heads = level_weight.shape[0]
    size = width // heads
    parts = lax.axis_size("head")
    edges = [rows * sum(SHARES[:c]) // sum(SHARES) for c in range(CHUNKS + 1)]
    spans = list(zip(edges[:-1], edges[1:]))
    depth = inputs.shape[1]
    mine = load(inputs, spans[:1])
    mine = [*mine, *load(inputs, spans[1:], mine)]
    grads, weights = call(
        functools.partial(load_weights_kernel, parts),
        [pltpu.VMEM((rows, width), BF16), pltpu.VMEM((parts * depth, 3 * width), BF16)],
        [
            pltpu.with_memory_space_constraint(grad_out, pltpu.HBM),
            pltpu.with_memory_space_constraint(w_qkv, pltpu.HBM),
            mine[1],
        ],
        [HBM, HBM, ANY],
        0,
        [pltpu.SemaphoreType.DMA((3 * parts + 1,))],
        limit=2,
        moved=4 * (grad_out.size + w_qkv.size),
    )
    top, *lows = [1 << b for b in reversed(range(parts.bit_length() - 1))]
    arrived = [swap(piece, "head", top) for piece in mine]
    arrived[0] = tie(arrived[0], weights)
    whole = {0: inputs}
    for low in lows:
        for k in sorted(whole):
            whole[k | low] = swap(whole[k], "head", low)
    state = pltpu.VMEM((2, heads, size, size), F32)
    qs, ks, vs, states, locals_ = [], [], [], [], []

    def local(c, after):
        chunk = spans[c][1] - spans[c][0]
        return call(
            functools.partial(local_kernel, spans[c], heads),
            [pltpu.VMEM((4, chunk, width), F32)],
            [level_weight, qs[c], ks[c], vs[c], grads, after],
            [SMEM] + [VMEM] * 4 + [ANY],
            100 * chunk * chunk * width if c >= CHUNKS - 2 else 0,
        )[0]

    after = None
    for c in range(CHUNKS):
        pieces = {**whole, 0: mine[c]}
        pieces[top] = arrived[c] if after is None else tie(arrived[c], after)
        for low in lows:
            for k in [k for k in sorted(pieces) if k & top]:
                pieces[k | low] = swap(pieces[k], "head", low)
        segments = [pieces[k] for k in sorted(pieces)]
        span = spans[c]
        chunk = span[1] - span[0]
        flat = pltpu.VMEM((chunk, width), BF16)
        if c < CHUNKS - 1:
            if c > 0:
                locals_.append(local(c - 1, pieces[top]))
            operands = [weights, grads, *segments, *locals_[-1:]]
            got = call(
                functools.partial(project_kernel, span, len(segments), heads),
                [flat, flat, flat, state],
                operands,
                [VMEM] * (2 + len(segments)) + [ANY] * len(locals_[-1:]),
                0,
            )
        else:
            operands = [weights, *segments[:-1], *states]
            begun, before = call(
                functools.partial(early_kernel, span, len(segments) - 1),
                [pltpu.VMEM((chunk, 3 * width), F32), state],
                operands,
                [VMEM] * len(operands),
                0,
            )
            got = call(
                functools.partial(last_kernel, span, heads),
                [
                    flat,
                    flat,
                    flat,
                    state,
                    state,
                    *[pltpu.VMEM((2, heads // GROUP, size, size), BF16)] * (GROUP - 1),
                ],
                [weights, grads, begun, before, segments[-1]],
                [VMEM] * 5,
                0,
            )
        qs.append(got[0])
        ks.append(got[1])
        vs.append(got[2])
        states.append(got[3])
        after = got[3]
    levels, fillers = exchange(got[4], got[5:], local, range(len(locals_), CHUNKS))
    locals_ += fillers
    shapes = [jax.ShapeDtypeStruct((rows, width), BF16)] * 4
    top = len(levels) // GROUP
    flats = [*qs, *ks, *vs]
    scratch = [
        pltpu.VMEM((2, rows, width), BF16),
        pltpu.VMEM((heads, size, size), F32),
        pltpu.SemaphoreType.DMA((2, CHUNKS)),
    ]
    operands = [level_weight, grads, *levels[:-GROUP], *flats, *states, *locals_]
    *written, base = call(
        functools.partial(early_side_kernel, spans, heads, top),
        [*shapes, pltpu.VMEM((CHUNKS, heads, size, size), F32)],
        operands,
        [SMEM] + [VMEM] * (len(operands) - 1),
        0,
        scratch,
        [ANY] * 4 + [VMEM],
        8,
    )
    operands = [level_weight, grads, base, *levels[-GROUP:], *flats, *locals_]
    return call(
        functools.partial(late_side_kernel, spans, heads, top),
        shapes,
        [*operands, *written],
        [SMEM] + [VMEM] * (len(operands) - 1) + [ANY] * 4,
        0,
        scratch,
        [ANY] * 4,
        8,
        aliases={len(operands) + j: j for j in range(4)},
    )


def solution(mesh):
    in_specs = (P("seq", "head"), P(None, None, "head"), P("head", None), P("seq", "head"))
    out_specs = (P("seq", "head"), P("seq", "head"), P("seq", "head"), P("seq", "head"))
    return jax.shard_map(
        per_device, mesh=mesh, in_specs=in_specs, out_specs=out_specs, check_vma=False
    )
```

```python
import functools
import math

import jax
import jax.numpy as jnp
from jax import lax
from jax.experimental import pallas as pl
from jax.experimental.pallas import tpu as pltpu
from jax.sharding import PartitionSpec as P

SHARES = (10, 12, 13, 14, 15)
CHUNKS = len(SHARES)
GROUP = 4
FIRST = (3, 2, 1)
MIB = 2**20
VMEM = pl.BlockSpec(memory_space=pltpu.VMEM)
SMEM = pl.BlockSpec(memory_space=pltpu.SMEM)
ANY = pl.BlockSpec(memory_space=pl.ANY)
HBM = pl.BlockSpec(memory_space=pltpu.HBM)
NN = (((1,), (0,)), ((), ()))
NT = (((1,), (1,)), ((), ()))
TN = (((0,), (0,)), ((), ()))
BF16 = jnp.bfloat16
F32 = jnp.float32


def dot(a, b, dims=NN):
    return lax.dot_general(a, b, dims, preferred_element_type=F32)


def swap(value, axis, mask):
    pairs = [(source, source ^ mask) for source in range(lax.axis_size(axis))]
    return lax.ppermute(value, axis, pairs)


def bit_of(position, bit):
    return lax.rem(position // 2**bit, 2) == 1


def call(kernel, outs, operands, specs, flops, scratch=(), out_specs=None, limit=4, moved=0, aliases=()):
    return pl.pallas_call(
        kernel,
        out_shape=outs,
        in_specs=specs,
        out_specs=[VMEM] * len(outs) if out_specs is None else out_specs,
        scratch_shapes=scratch,
        input_output_aliases=dict(aliases),
        compiler_params=pltpu.CompilerParams(vmem_limit_bytes=limit * MIB),
        cost_estimate=pl.CostEstimate(flops=flops, bytes_accessed=moved, transcendentals=0),
    )(*operands)


def load_kernel(spans, x_ref, *refs):
    outs, sems = refs[-len(spans) - 1 : -1], refs[-1]
    copies = []
    for i, (first, last) in enumerate(spans):
        rows = x_ref.at[pl.ds(first, last - first)]
        copies.append(pltpu.make_async_copy(rows, outs[i], sems.at[i]))
    for copy in copies:
        copy.start()
    for copy in copies:
        copy.wait()


def load(source, spans, after=()):
    return call(
        functools.partial(load_kernel, spans),
        [pltpu.VMEM((last - first, *source.shape[1:]), BF16) for first, last in spans],
        [pltpu.with_memory_space_constraint(source, pltpu.HBM), *after],
        [HBM] + [ANY] * len(after),
        0,
        [pltpu.SemaphoreType.DMA((len(spans),))],
        limit=2,
        moved=4 * source.size,
    )


def load_weights_kernel(parts, g_ref, w_ref, after_ref, g_out, w_out, sems):
    me = lax.axis_index("head")
    depth = w_ref.shape[1] // parts
    width = w_ref.shape[2]
    copies = [pltpu.make_async_copy(g_ref, g_out, sems.at[3 * parts])]
    for k in range(parts):
        rows = pl.ds(pl.multiple_of((me ^ k) * depth, depth), depth)
        for j in range(3):
            copies.append(
                pltpu.make_async_copy(
                    w_ref.at[j, rows],
                    w_out.at[pl.ds(k * depth, depth), pl.ds(j * width, width)],
                    sems.at[3 * k + j],
                )
            )
    for copy in copies:
        copy.start()
    for copy in copies:
        copy.wait()


def tie_kernel(value_ref, *refs):
    del value_ref, refs


def tie(value, *after, flops=0):
    return pl.pallas_call(
        tie_kernel,
        out_shape=pltpu.VMEM(value.shape, value.dtype),
        in_specs=[ANY] * (1 + len(after)),
        out_specs=ANY,
        input_output_aliases={0: 0},
        compiler_params=pltpu.CompilerParams(vmem_limit_bytes=MIB),
        cost_estimate=pl.CostEstimate(flops=flops, bytes_accessed=0, transcendentals=0),
    )(value, *after)


def beside(refs, span):
    count = span[1] - span[0]
    found = [ref[...] if ref.shape[0] == count else ref[span[0] : span[1], :] for ref in refs]
    return found[0] if len(found) == 1 else jnp.concatenate(found, axis=1)


def write_states(span, heads, q_ref, k_ref, v_ref, g_ref, state_ref):
    size = q_ref.shape[1] // heads
    for h in range(0, heads, 2):
        cols = slice(h * size, (h + 2) * size)
        for s, (left, right) in enumerate(
            ((k_ref[:, cols], v_ref[:, cols]), (q_ref[:, cols], g_ref[span[0] : span[1], cols]))
        ):
            both = dot(left, right, TN)
            state_ref[s, h] = both[:size, :size]
            state_ref[s, h + 1] = both[size:, size:]


def early_kernel(span, count, w_ref, *refs):
    segments, states = refs[:count], refs[count:-2]
    total_ref, sum_ref = refs[-2:]
    rows = beside(segments, span)
    total_ref[...] = dot(rows, w_ref[: rows.shape[1], :])
    sums = states[0][...]
    for state in states[1:]:
        sums = sums + state[...]
    sum_ref[...] = sums


def project_kernel(span, count, heads, w_ref, g_ref, *refs):
    outs, state_ref = refs[-4:-1], refs[-1]
    width = outs[0].shape[1]
    total = dot(beside(refs[:count], span), w_ref[...])
    for j, out_ref in enumerate(outs):
        out_ref[...] = total[:, j * width : (j + 1) * width].astype(BF16)
    write_states(span, heads, *outs, g_ref, state_ref)


def last_kernel(span, heads, w_ref, g_ref, part_ref, sum_ref, late_ref, *refs):
    outs, state_ref, total_ref, sends = refs[:3], refs[3], refs[4], refs[5:]
    width = outs[0].shape[1]
    start = w_ref.shape[0] - late_ref.shape[1]
    total = part_ref[...] + dot(late_ref[...], w_ref[start:, :])
    for j, out_ref in enumerate(outs):
        out_ref[...] = total[:, j * width : (j + 1) * width].astype(BF16)
    write_states(span, heads, *outs, g_ref, state_ref)
    share = heads // GROUP
    place = lax.rem(lax.axis_index("seq"), GROUP)
    total_ref[...] = sum_ref[...] + state_ref[...]
    for m, send in enumerate(sends, 1):
        for s in range(2):
            for e in range(share):
                send[s, e] = total_ref[s, (place ^ m) * share + e].astype(BF16)


def local_kernel(span, heads, weight_ref, q_ref, k_ref, v_ref, g_ref, after_ref, out_ref):
    rows = q_ref.shape[0]
    size = q_ref.shape[1] // heads
    norm = 1.0 / math.sqrt(size * g_ref.shape[0])
    at = lax.broadcasted_iota(jnp.int32, (rows, rows), 0)
    of = lax.broadcasted_iota(jnp.int32, (rows, rows), 1)
    columns = [slice(h * size, (h + 1) * size) for h in range(heads)]
    masked = []
    for h, cols in enumerate(columns):
        q, k, v = q_ref[:, cols], k_ref[:, cols], v_ref[:, cols]
        g = g_ref[span[0] : span[1], cols]
        scale = weight_ref[h, 0] * norm
        masked.append(
            [
                jnp.where(at >= of, dot(left, right, NT) * scale, 0.0).astype(BF16)
                for left, right in ((q, k), (g, v))
            ]
        )
    for h, cols in enumerate(columns):
        q, k, v = q_ref[:, cols], k_ref[:, cols], v_ref[:, cols]
        g = g_ref[span[0] : span[1], cols]
        attend, grad = masked[h]
        out_ref[0, :, cols] = dot(attend, v)
        out_ref[1, :, cols] = dot(grad, k)
        out_ref[2, :, cols] = dot(grad, q, TN)
        out_ref[3, :, cols] = dot(attend, g, TN)


def owner_kernel(final, total_ref, *refs):
    got, refs = dict(zip(FIRST, refs)), refs[GROUP - 1 :]
    near_ref, far_ref, *nexts = refs[-3 if final else -4 :]
    position = lax.axis_index("seq")
    place = lax.rem(position, GROUP)
    heads = total_ref.shape[1]
    share = heads // GROUP
    odd, high = bit_of(position, 0), bit_of(position, 1)
    for e in range(share):
        mine, other = [], []
        for s in range(2):
            mine.append(total_ref[s, place * share + e] + got[1][s, e].astype(F32))
            other.append(got[2][s, e].astype(F32) + got[3][s, e].astype(F32))
        sums = [mine[s] + other[s] for s in range(2)]
        write_next(sums, e, 2, final, *nexts)
        near_ref[e] = jnp.where(high, other[0], other[1]).astype(BF16)
        far_ref[e] = jnp.where(high, mine[1], mine[0]).astype(BF16)
    for h in range(heads):
        near_ref[share + h] = jnp.where(odd, total_ref[1, h], total_ref[0, h]).astype(BF16)


def write_next(sums, e, bit, final, next_ref, sum_ref=None):
    if final:
        value = jnp.where(bit_of(lax.axis_index("seq"), bit), sums[1], sums[0])
        next_ref[e] = value.astype(BF16)
        return
    for s in range(2):
        sum_ref[s, e] = sums[s]
        next_ref[s, e] = sums[s].astype(BF16)


def climb_kernel(bit, next_final, got_ref, old_ref, level_ref, *nexts):
    on = bit_of(lax.axis_index("seq"), bit)
    for e in range(got_ref.shape[1]):
        both = [got_ref[s, e].astype(F32) for s in range(2)]
        level_ref[e] = jnp.where(on, both[0], both[1]).astype(BF16)
        sums = [old_ref[s, e] + both[s] for s in range(2)]
        write_next(sums, e, bit + 1, next_final, *nexts)


def pair_block(first, second):
    zero = jnp.zeros(first.shape, BF16)
    top = jnp.concatenate([first.astype(BF16), zero], axis=1)
    bottom = jnp.concatenate([zero, second.astype(BF16)], axis=1)
    return jnp.concatenate([top, bottom], axis=0)


def gather_mixes(levels, first, side, weight_ref, block, mix_ref):
    position = lax.axis_index("seq")
    place = lax.rem(position, GROUP)
    heads, size = mix_ref.shape[:2]
    share = heads // GROUP
    for m in range(GROUP):
        for e in range(share):
            h = (place ^ m) * share + e
            total = None
            for b in range(len(levels) // GROUP):
                level = first + b
                coef = weight_ref[h, level + 1] * (1.0 / math.sqrt(size * block * 2**level))
                taken = bit_of(position, level)
                if side == 1:
                    taken = jnp.logical_not(taken)
                term = jnp.where(taken, coef, 0.0) * levels[b * GROUP + m][e].astype(F32)
                total = term if total is None else total + term
            mix_ref[h] = total


def write_side(spans, side, ascending, weight_of, rows_of, part_refs, outs, held, sems):
    chunks = len(spans)
    size = held.shape[-1]
    copies = []
    for c in range(chunks) if ascending else reversed(range(chunks)):
        span = slice(*spans[c])
        weights = weight_of(c)
        for j in range(2):
            ref = rows_of[2 * side + j][c]
            rows = span if ref.shape[0] != spans[c][1] - spans[c][0] else slice(None)
            for p, weight in enumerate(weights):
                cols = slice(p * weight.shape[0], (p + 1) * weight.shape[0])
                term = dot(ref[rows, cols], weight, NT if 2 * side + j in (1, 2) else NN)
                held[j, span, cols] = (term + part_refs[c][2 * side + j, :, cols]).astype(BF16)
            copy = pltpu.make_async_copy(
                held.at[j, span], outs[2 * side + j].at[span], sems.at[j, c]
            )
            copy.start()
            copies.append(copy)
    for copy in copies:
        copy.wait()


def early_side_kernel(spans, heads, top, weight_ref, g_ref, *refs):
    chunks = len(spans)
    levels, refs = refs[: (top - 1) * GROUP], refs[(top - 1) * GROUP :]
    q_refs, refs = refs[:chunks], refs[chunks:]
    k_refs, refs = refs[:chunks], refs[chunks:]
    v_refs, refs = refs[:chunks], refs[chunks:]
    state_refs, refs = refs[:chunks], refs[chunks:]
    part_refs, refs = refs[:chunks], refs[chunks:]
    outs, (base_ref, held, mix_ref, sems) = refs[:4], refs[4:]
    position = lax.axis_index("seq")
    block = g_ref.shape[0]
    size = mix_ref.shape[-1]
    norm = 1.0 / math.sqrt(size * block)

    def sums_of(side):
        gather_mixes(levels, 1, side, weight_ref, block, mix_ref)
        taken = bit_of(position, 0)
        if side == 1:
            taken = jnp.logical_not(taken)
        found = []
        for h in range(heads):
            coef = jnp.where(taken, weight_ref[h, 1] * norm, 0.0)
            found.append(mix_ref[h] + coef * levels[1][heads // GROUP + h].astype(F32))
        return found

    def add(sums, side, c):
        return [
            total + weight_ref[h, 0] * norm * state_refs[c][side, h] for h, total in enumerate(sums)
        ]

    for side in range(2):
        reached = bit_of(position, top)

        @pl.when(reached if side == 1 else jnp.logical_not(reached))
        def _():
            sums = [sums_of(side)]

            def weight_of(c):
                weights = [pair_block(*sums[0][h : h + 2]) for h in range(0, heads, 2)]
                sums[0] = add(sums[0], side, c)
                return weights

            rows_of = (q_refs, [g_ref] * chunks, v_refs, k_refs)
            write_side(spans, side, side == 0, weight_of, rows_of, part_refs, outs, held, sems)
            other = sums_of(1 - side)
            for c in range(chunks) if side == 1 else reversed(range(chunks)):
                for h in range(heads):
                    base_ref[c, h] = other[h]
                other = add(other, 1 - side, c)


def late_side_kernel(spans, heads, top, weight_ref, g_ref, base_ref, *refs):
    chunks = len(spans)
    levels, refs = refs[:GROUP], refs[GROUP:]
    q_refs, refs = refs[:chunks], refs[chunks:]
    k_refs, refs = refs[:chunks], refs[chunks:]
    v_refs, refs = refs[:chunks], refs[chunks:]
    part_refs, refs = refs[:chunks], refs[chunks:]
    outs, (held, mix_ref, sems) = refs[-7:-3], refs[-3:]
    block = g_ref.shape[0]
    reached = bit_of(lax.axis_index("seq"), top)
    for side in range(2):

        @pl.when(reached if side == 0 else jnp.logical_not(reached))
        def _():
            gather_mixes(levels, top, side, weight_ref, block, mix_ref)

            def weight_of(c):
                sums = [base_ref[c, h] + mix_ref[h] for h in range(heads)]
                return [pair_block(*sums[h : h + 2]) for h in range(0, heads, 2)]

            rows_of = (q_refs, [g_ref] * chunks, v_refs, k_refs)
            write_side(spans, side, False, weight_of, rows_of, part_refs, outs, held, sems)


def exchange(totals, sends, local, late):
    depth = lax.axis_size("seq").bit_length() - 1
    heads, square = totals.shape[1], totals.shape[2:]
    share = heads // GROUP
    last = depth - 1

    def nexts(bit):
        if bit == last:
            return [pltpu.VMEM((share, *square), BF16)]
        return [pltpu.VMEM((2, share, *square), BF16), pltpu.VMEM((2, share, *square), F32)]

    def spread(mine, other):
        return [mine, *[swap(mine if m == 1 else other, "seq", m) for m in range(1, GROUP)]]

    one = pltpu.VMEM((share, *square), BF16)
    got = [swap(sends[m - 1], "seq", m) for m in FIRST]
    fillers = [local(c, sends[0]) for c in late]
    mine, other, sent, *sums = call(
        functools.partial(owner_kernel, last == 2),
        [pltpu.VMEM((share + heads, *square), BF16), one, *nexts(2)],
        [totals, *got, *fillers],
        [VMEM] * GROUP + [ANY] * len(fillers),
        10**6,
    )
    levels = spread(mine, other)
    for bit in range(2, last):
        found, sent, *sums = call(
            functools.partial(climb_kernel, bit, bit + 1 == last),
            [one, *nexts(bit + 1)],
            [swap(sent, "seq", 1 << bit), *sums],
            [VMEM] * 2,
            10**6,
        )
        levels += spread(found, found)
    found = tie(swap(sent, "seq", 1 << last), mine, flops=12 * 10**8)
    levels += spread(found, found)
    return levels, fillers


def per_device(inputs, w_qkv, level_weight, grad_out):
    rows, width = grad_out.shape
    heads = level_weight.shape[0]
    size = width // heads
    parts = lax.axis_size("head")
    edges = [rows * sum(SHARES[:c]) // sum(SHARES) for c in range(CHUNKS + 1)]
    spans = list(zip(edges[:-1], edges[1:]))
    depth = inputs.shape[1]
    mine = load(inputs, spans[:1])
    mine = [*mine, *load(inputs, spans[1:], mine)]
    grads, weights = call(
        functools.partial(load_weights_kernel, parts),
        [pltpu.VMEM((rows, width), BF16), pltpu.VMEM((parts * depth, 3 * width), BF16)],
        [
            pltpu.with_memory_space_constraint(grad_out, pltpu.HBM),
            pltpu.with_memory_space_constraint(w_qkv, pltpu.HBM),
            mine[1],
        ],
        [HBM, HBM, ANY],
        0,
        [pltpu.SemaphoreType.DMA((3 * parts + 1,))],
        limit=2,
        moved=4 * (grad_out.size + w_qkv.size),
    )
    top, *lows = [1 << b for b in reversed(range(parts.bit_length() - 1))]
    arrived = [swap(piece, "head", top) for piece in mine]
    arrived[0] = tie(arrived[0], weights)
    whole = {0: inputs}
    for low in lows:
        for k in sorted(whole):
            whole[k | low] = swap(whole[k], "head", low)
    state = pltpu.VMEM((2, heads, size, size), F32)
    qs, ks, vs, states, locals_ = [], [], [], [], []

    def local(c, after):
        chunk = spans[c][1] - spans[c][0]
        return call(
            functools.partial(local_kernel, spans[c], heads),
            [pltpu.VMEM((4, chunk, width), F32)],
            [level_weight, qs[c], ks[c], vs[c], grads, after],
            [SMEM] + [VMEM] * 4 + [ANY],
            100 * chunk * chunk * width if c >= CHUNKS - 2 else 0,
        )[0]

    after = None
    for c in range(CHUNKS):
        pieces = {**whole, 0: mine[c]}
        pieces[top] = arrived[c] if after is None else tie(arrived[c], after)
        for low in lows:
            for k in [k for k in sorted(pieces) if k & top]:
                pieces[k | low] = swap(pieces[k], "head", low)
        segments = [pieces[k] for k in sorted(pieces)]
        span = spans[c]
        chunk = span[1] - span[0]
        flat = pltpu.VMEM((chunk, width), BF16)
        if c < CHUNKS - 1:
            if c > 0:
                locals_.append(local(c - 1, pieces[top]))
            operands = [weights, grads, *segments, *locals_[-1:]]
            got = call(
                functools.partial(project_kernel, span, len(segments), heads),
                [flat, flat, flat, state],
                operands,
                [VMEM] * (2 + len(segments)) + [ANY] * len(locals_[-1:]),
                0,
            )
        else:
            operands = [weights, *segments[:-1], *states]
            begun, before = call(
                functools.partial(early_kernel, span, len(segments) - 1),
                [pltpu.VMEM((chunk, 3 * width), F32), state],
                operands,
                [VMEM] * len(operands),
                0,
            )
            got = call(
                functools.partial(last_kernel, span, heads),
                [
                    flat,
                    flat,
                    flat,
                    state,
                    state,
                    *[pltpu.VMEM((2, heads // GROUP, size, size), BF16)] * (GROUP - 1),
                ],
                [weights, grads, begun, before, segments[-1]],
                [VMEM] * 5,
                0,
            )
        qs.append(got[0])
        ks.append(got[1])
        vs.append(got[2])
        states.append(got[3])
        after = got[3]
    levels, fillers = exchange(got[4], got[5:], local, range(len(locals_), CHUNKS))
    locals_ += fillers
    shapes = [jax.ShapeDtypeStruct((rows, width), BF16)] * 4
    top = len(levels) // GROUP
    flats = [*qs, *ks, *vs]
    scratch = [
        pltpu.VMEM((2, rows, width), BF16),
        pltpu.VMEM((heads, size, size), F32),
        pltpu.SemaphoreType.DMA((2, CHUNKS)),
    ]
    operands = [level_weight, grads, *levels[:-GROUP], *flats, *states, *locals_]
    *written, base = call(
        functools.partial(early_side_kernel, spans, heads, top),
        [*shapes, pltpu.VMEM((CHUNKS, heads, size, size), F32)],
        operands,
        [SMEM] + [VMEM] * (len(operands) - 1),
        0,
        scratch,
        [ANY] * 4 + [VMEM],
        8,
    )
    operands = [level_weight, grads, base, *levels[-GROUP:], *flats, *locals_]
    return call(
        functools.partial(late_side_kernel, spans, heads, top),
        shapes,
        [*operands, *written],
        [SMEM] + [VMEM] * (len(operands) - 1) + [ANY] * 4,
        0,
        scratch,
        [ANY] * 4,
        8,
        aliases={len(operands) + j: j for j in range(4)},
    )


def solution(mesh):
    in_specs = (P("seq", "head"), P(None, None, "head"), P("head", None), P("seq", "head"))
    out_specs = (P("seq", "head"), P("seq", "head"), P("seq", "head"), P("seq", "head"))
    return jax.shard_map(
        per_device, mesh=mesh, in_specs=in_specs, out_specs=out_specs, check_vma=False
    )
```

```python
import functools
import math

import jax
import jax.numpy as jnp
from jax import lax
from jax.experimental import pallas as pl
from jax.experimental.pallas import tpu as pltpu
from jax.sharding import PartitionSpec as P

SHARES = (10, 12, 13, 14, 15)
CHUNKS = len(SHARES)
GROUP = 4
FIRST = (3, 2, 1)
MIB = 2**20
VMEM = pl.BlockSpec(memory_space=pltpu.VMEM)
SMEM = pl.BlockSpec(memory_space=pltpu.SMEM)
ANY = pl.BlockSpec(memory_space=pl.ANY)
HBM = pl.BlockSpec(memory_space=pltpu.HBM)
NN = (((1,), (0,)), ((), ()))
NT = (((1,), (1,)), ((), ()))
TN = (((0,), (0,)), ((), ()))
BF16 = jnp.bfloat16
F32 = jnp.float32


def dot(a, b, dims=NN):
    return lax.dot_general(a, b, dims, preferred_element_type=F32)


def swap(value, axis, mask):
    pairs = [(source, source ^ mask) for source in range(lax.axis_size(axis))]
    return lax.ppermute(value, axis, pairs)


def bit_of(position, bit):
    return lax.rem(position // 2**bit, 2) == 1


def call(kernel, outs, operands, specs, flops, scratch=(), out_specs=None, limit=4, moved=0, aliases=()):
    return pl.pallas_call(
        kernel,
        out_shape=outs,
        in_specs=specs,
        out_specs=[VMEM] * len(outs) if out_specs is None else out_specs,
        scratch_shapes=scratch,
        input_output_aliases=dict(aliases),
        compiler_params=pltpu.CompilerParams(vmem_limit_bytes=limit * MIB),
        cost_estimate=pl.CostEstimate(flops=flops, bytes_accessed=moved, transcendentals=0),
    )(*operands)


def load_kernel(spans, x_ref, *refs):
    outs, sems = refs[-len(spans) - 1 : -1], refs[-1]
    copies = []
    for i, (first, last) in enumerate(spans):
        rows = x_ref.at[pl.ds(first, last - first)]
        copies.append(pltpu.make_async_copy(rows, outs[i], sems.at[i]))
    for copy in copies:
        copy.start()
    for copy in copies:
        copy.wait()


def load(source, spans, after=()):
    return call(
        functools.partial(load_kernel, spans),
        [pltpu.VMEM((last - first, *source.shape[1:]), BF16) for first, last in spans],
        [pltpu.with_memory_space_constraint(source, pltpu.HBM), *after],
        [HBM] + [ANY] * len(after),
        0,
        [pltpu.SemaphoreType.DMA((len(spans),))],
        limit=2,
        moved=4 * source.size,
    )


def load_weights_kernel(parts, g_ref, w_ref, after_ref, g_out, w_out, sems):
    me = lax.axis_index("head")
    depth = w_ref.shape[1] // parts
    width = w_ref.shape[2]
    copies = [pltpu.make_async_copy(g_ref, g_out, sems.at[3 * parts])]
    for k in range(parts):
        rows = pl.ds(pl.multiple_of((me ^ k) * depth, depth), depth)
        for j in range(3):
            copies.append(
                pltpu.make_async_copy(
                    w_ref.at[j, rows],
                    w_out.at[pl.ds(k * depth, depth), pl.ds(j * width, width)],
                    sems.at[3 * k + j],
                )
            )
    for copy in copies:
        copy.start()
    for copy in copies:
        copy.wait()


def tie_kernel(value_ref, *refs):
    del value_ref, refs


def tie(value, *after, flops=0):
    return pl.pallas_call(
        tie_kernel,
        out_shape=pltpu.VMEM(value.shape, value.dtype),
        in_specs=[ANY] * (1 + len(after)),
        out_specs=ANY,
        input_output_aliases={0: 0},
        compiler_params=pltpu.CompilerParams(vmem_limit_bytes=MIB),
        cost_estimate=pl.CostEstimate(flops=flops, bytes_accessed=0, transcendentals=0),
    )(value, *after)


def beside(refs, span):
    count = span[1] - span[0]
    found = [ref[...] if ref.shape[0] == count else ref[span[0] : span[1], :] for ref in refs]
    return found[0] if len(found) == 1 else jnp.concatenate(found, axis=1)


def write_states(span, heads, q_ref, k_ref, v_ref, g_ref, state_ref):
    size = q_ref.shape[1] // heads
    for h in range(0, heads, 2):
        cols = slice(h * size, (h + 2) * size)
        for s, (left, right) in enumerate(
            ((k_ref[:, cols], v_ref[:, cols]), (q_ref[:, cols], g_ref[span[0] : span[1], cols]))
        ):
            both = dot(left, right, TN)
            state_ref[s, h] = both[:size, :size]
            state_ref[s, h + 1] = both[size:, size:]


def early_kernel(span, count, w_ref, *refs):
    segments, states = refs[:count], refs[count:-2]
    total_ref, sum_ref = refs[-2:]
    rows = beside(segments, span)
    total_ref[...] = dot(rows, w_ref[: rows.shape[1], :])
    sums = states[0][...]
    for state in states[1:]:
        sums = sums + state[...]
    sum_ref[...] = sums


def more_kernel(span, start, w_ref, part_ref, *refs):
    rows = beside(refs[:-1], span)
    refs[-1][...] = part_ref[...] + dot(rows, w_ref[start : start + rows.shape[1], :])


def project_kernel(span, count, heads, w_ref, g_ref, *refs):
    outs, state_ref = refs[-4:-1], refs[-1]
    width = outs[0].shape[1]
    total = dot(beside(refs[:count], span), w_ref[...])
    for j, out_ref in enumerate(outs):
        out_ref[...] = total[:, j * width : (j + 1) * width].astype(BF16)
    write_states(span, heads, *outs, g_ref, state_ref)


def last_kernel(span, heads, w_ref, g_ref, part_ref, sum_ref, late_ref, *refs):
    outs, state_ref, total_ref, sends = refs[:3], refs[3], refs[4], refs[5:]
    width = outs[0].shape[1]
    start = w_ref.shape[0] - late_ref.shape[1]
    total = part_ref[...] + dot(late_ref[...], w_ref[start:, :])
    for j, out_ref in enumerate(outs):
        out_ref[...] = total[:, j * width : (j + 1) * width].astype(BF16)
    write_states(span, heads, *outs, g_ref, state_ref)
    share = heads // GROUP
    place = lax.rem(lax.axis_index("seq"), GROUP)
    total_ref[...] = sum_ref[...] + state_ref[...]
    for m, send in enumerate(sends, 1):
        for s in range(2):
            for e in range(share):
                send[s, e] = total_ref[s, (place ^ m) * share + e].astype(BF16)


def local_kernel(span, heads, weight_ref, q_ref, k_ref, v_ref, g_ref, after_ref, out_ref):
    rows = q_ref.shape[0]
    size = q_ref.shape[1] // heads
    norm = 1.0 / math.sqrt(size * g_ref.shape[0])
    at = lax.broadcasted_iota(jnp.int32, (rows, rows), 0)
    of = lax.broadcasted_iota(jnp.int32, (rows, rows), 1)
    columns = [slice(h * size, (h + 1) * size) for h in range(heads)]
    masked = []
    for h, cols in enumerate(columns):
        q, k, v = q_ref[:, cols], k_ref[:, cols], v_ref[:, cols]
        g = g_ref[span[0] : span[1], cols]
        scale = weight_ref[h, 0] * norm
        masked.append(
            [
                jnp.where(at >= of, dot(left, right, NT) * scale, 0.0).astype(BF16)
                for left, right in ((q, k), (g, v))
            ]
        )
    for h, cols in enumerate(columns):
        q, k, v = q_ref[:, cols], k_ref[:, cols], v_ref[:, cols]
        g = g_ref[span[0] : span[1], cols]
        attend, grad = masked[h]
        out_ref[0, :, cols] = dot(attend, v)
        out_ref[1, :, cols] = dot(grad, k)
        out_ref[2, :, cols] = dot(grad, q, TN)
        out_ref[3, :, cols] = dot(attend, g, TN)


def owner_kernel(final, total_ref, *refs):
    got, refs = dict(zip(FIRST, refs)), refs[GROUP - 1 :]
    near_ref, far_ref, *nexts = refs[-3 if final else -4 :]
    position = lax.axis_index("seq")
    place = lax.rem(position, GROUP)
    heads = total_ref.shape[1]
    share = heads // GROUP
    odd, high = bit_of(position, 0), bit_of(position, 1)
    for e in range(share):
        mine, other = [], []
        for s in range(2):
            mine.append(total_ref[s, place * share + e] + got[1][s, e].astype(F32))
            other.append(got[2][s, e].astype(F32) + got[3][s, e].astype(F32))
        sums = [mine[s] + other[s] for s in range(2)]
        write_next(sums, e, 2, final, *nexts)
        near_ref[e] = jnp.where(high, other[0], other[1]).astype(BF16)
        far_ref[e] = jnp.where(high, mine[1], mine[0]).astype(BF16)
    for h in range(heads):
        near_ref[share + h] = jnp.where(odd, total_ref[1, h], total_ref[0, h]).astype(BF16)


def write_next(sums, e, bit, final, next_ref, sum_ref=None):
    if final:
        value = jnp.where(bit_of(lax.axis_index("seq"), bit), sums[1], sums[0])
        next_ref[e] = value.astype(BF16)
        return
    for s in range(2):
        sum_ref[s, e] = sums[s]
        next_ref[s, e] = sums[s].astype(BF16)


def climb_kernel(bit, next_final, got_ref, old_ref, level_ref, *nexts):
    on = bit_of(lax.axis_index("seq"), bit)
    for e in range(got_ref.shape[1]):
        both = [got_ref[s, e].astype(F32) for s in range(2)]
        level_ref[e] = jnp.where(on, both[0], both[1]).astype(BF16)
        sums = [old_ref[s, e] + both[s] for s in range(2)]
        write_next(sums, e, bit + 1, next_final, *nexts)


def pair_block(first, second):
    zero = jnp.zeros(first.shape, BF16)
    top = jnp.concatenate([first.astype(BF16), zero], axis=1)
    bottom = jnp.concatenate([zero, second.astype(BF16)], axis=1)
    return jnp.concatenate([top, bottom], axis=0)


def gather_mixes(levels, first, side, weight_ref, block, mix_ref):
    position = lax.axis_index("seq")
    place = lax.rem(position, GROUP)
    heads, size = mix_ref.shape[:2]
    share = heads // GROUP
    for m in range(GROUP):
        for e in range(share):
            h = (place ^ m) * share + e
            total = None
            for b in range(len(levels) // GROUP):
                level = first + b
                coef = weight_ref[h, level + 1] * (1.0 / math.sqrt(size * block * 2**level))
                taken = bit_of(position, level)
                if side == 1:
                    taken = jnp.logical_not(taken)
                term = jnp.where(taken, coef, 0.0) * levels[b * GROUP + m][e].astype(F32)
                total = term if total is None else total + term
            mix_ref[h] = total


def write_side(spans, side, ascending, weight_of, rows_of, part_refs, outs, held, sems):
    chunks = len(spans)
    size = held.shape[-1]
    copies = []
    for c in range(chunks) if ascending else reversed(range(chunks)):
        span = slice(*spans[c])
        weights = weight_of(c)
        for j in range(2):
            ref = rows_of[2 * side + j][c]
            rows = span if ref.shape[0] != spans[c][1] - spans[c][0] else slice(None)
            for p, weight in enumerate(weights):
                cols = slice(p * weight.shape[0], (p + 1) * weight.shape[0])
                term = dot(ref[rows, cols], weight, NT if 2 * side + j in (1, 2) else NN)
                held[j, span, cols] = (term + part_refs[c][2 * side + j, :, cols]).astype(BF16)
            copy = pltpu.make_async_copy(
                held.at[j, span], outs[2 * side + j].at[span], sems.at[j, c]
            )
            copy.start()
            copies.append(copy)
    for copy in copies:
        copy.wait()


def early_side_kernel(spans, heads, top, weight_ref, g_ref, *refs):
    chunks = len(spans)
    levels, refs = refs[: (top - 1) * GROUP], refs[(top - 1) * GROUP :]
    q_refs, refs = refs[:chunks], refs[chunks:]
    k_refs, refs = refs[:chunks], refs[chunks:]
    v_refs, refs = refs[:chunks], refs[chunks:]
    state_refs, refs = refs[:chunks], refs[chunks:]
    part_refs, refs = refs[:chunks], refs[chunks:]
    outs, (base_ref, held, mix_ref, sems) = refs[:4], refs[4:]
    position = lax.axis_index("seq")
    block = g_ref.shape[0]
    size = mix_ref.shape[-1]
    norm = 1.0 / math.sqrt(size * block)

    def sums_of(side):
        gather_mixes(levels, 1, side, weight_ref, block, mix_ref)
        taken = bit_of(position, 0)
        if side == 1:
            taken = jnp.logical_not(taken)
        found = []
        for h in range(heads):
            coef = jnp.where(taken, weight_ref[h, 1] * norm, 0.0)
            found.append(mix_ref[h] + coef * levels[1][heads // GROUP + h].astype(F32))
        return found

    def add(sums, side, c):
        return [
            total + weight_ref[h, 0] * norm * state_refs[c][side, h] for h, total in enumerate(sums)
        ]

    for side in range(2):
        reached = bit_of(position, top)

        @pl.when(reached if side == 1 else jnp.logical_not(reached))
        def _():
            sums = [sums_of(side)]

            def weight_of(c):
                weights = [pair_block(*sums[0][h : h + 2]) for h in range(0, heads, 2)]
                sums[0] = add(sums[0], side, c)
                return weights

            rows_of = (q_refs, [g_ref] * chunks, v_refs, k_refs)
            write_side(spans, side, side == 0, weight_of, rows_of, part_refs, outs, held, sems)
            other = sums_of(1 - side)
            for c in range(chunks) if side == 1 else reversed(range(chunks)):
                for h in range(heads):
                    base_ref[c, h] = other[h]
                other = add(other, 1 - side, c)


def late_side_kernel(spans, heads, top, weight_ref, g_ref, base_ref, *refs):
    chunks = len(spans)
    levels, refs = refs[:GROUP], refs[GROUP:]
    q_refs, refs = refs[:chunks], refs[chunks:]
    k_refs, refs = refs[:chunks], refs[chunks:]
    v_refs, refs = refs[:chunks], refs[chunks:]
    part_refs, refs = refs[:chunks], refs[chunks:]
    outs, (held, mix_ref, sems) = refs[-7:-3], refs[-3:]
    block = g_ref.shape[0]
    reached = bit_of(lax.axis_index("seq"), top)
    for side in range(2):

        @pl.when(reached if side == 0 else jnp.logical_not(reached))
        def _():
            gather_mixes(levels, top, side, weight_ref, block, mix_ref)

            def weight_of(c):
                sums = [base_ref[c, h] + mix_ref[h] for h in range(heads)]
                return [pair_block(*sums[h : h + 2]) for h in range(0, heads, 2)]

            rows_of = (q_refs, [g_ref] * chunks, v_refs, k_refs)
            write_side(spans, side, False, weight_of, rows_of, part_refs, outs, held, sems)


def exchange(totals, sends, local, late):
    depth = lax.axis_size("seq").bit_length() - 1
    heads, square = totals.shape[1], totals.shape[2:]
    share = heads // GROUP
    last = depth - 1

    def nexts(bit):
        if bit == last:
            return [pltpu.VMEM((share, *square), BF16)]
        return [pltpu.VMEM((2, share, *square), BF16), pltpu.VMEM((2, share, *square), F32)]

    def spread(mine, other):
        return [mine, *[swap(mine if m == 1 else other, "seq", m) for m in range(1, GROUP)]]

    one = pltpu.VMEM((share, *square), BF16)
    got = [swap(sends[m - 1], "seq", m) for m in FIRST]
    fillers = [local(c, sends[0]) for c in late]
    mine, other, sent, *sums = call(
        functools.partial(owner_kernel, last == 2),
        [pltpu.VMEM((share + heads, *square), BF16), one, *nexts(2)],
        [totals, *got, *fillers],
        [VMEM] * GROUP + [ANY] * len(fillers),
        10**6,
    )
    levels = spread(mine, other)
    for bit in range(2, last):
        found, sent, *sums = call(
            functools.partial(climb_kernel, bit, bit + 1 == last),
            [one, *nexts(bit + 1)],
            [swap(sent, "seq", 1 << bit), *sums],
            [VMEM] * 2,
            10**6,
        )
        levels += spread(found, found)
    found = tie(swap(sent, "seq", 1 << last), mine, flops=12 * 10**8)
    levels += spread(found, found)
    return levels, fillers


def per_device(inputs, w_qkv, level_weight, grad_out):
    rows, width = grad_out.shape
    heads = level_weight.shape[0]
    size = width // heads
    parts = lax.axis_size("head")
    edges = [rows * sum(SHARES[:c]) // sum(SHARES) for c in range(CHUNKS + 1)]
    spans = list(zip(edges[:-1], edges[1:]))
    depth = inputs.shape[1]
    mine = load(inputs, spans[:1])
    mine = [*mine, *load(inputs, spans[1:], mine)]
    grads, weights = call(
        functools.partial(load_weights_kernel, parts),
        [pltpu.VMEM((rows, width), BF16), pltpu.VMEM((parts * depth, 3 * width), BF16)],
        [
            pltpu.with_memory_space_constraint(grad_out, pltpu.HBM),
            pltpu.with_memory_space_constraint(w_qkv, pltpu.HBM),
            mine[1],
        ],
        [HBM, HBM, ANY],
        0,
        [pltpu.SemaphoreType.DMA((3 * parts + 1,))],
        limit=2,
        moved=4 * (grad_out.size + w_qkv.size),
    )
    top, *lows = [1 << b for b in reversed(range(parts.bit_length() - 1))]
    arrived = [swap(piece, "head", top) for piece in mine]
    arrived[0] = tie(arrived[0], weights)
    whole = {0: inputs}
    for low in lows:
        for k in sorted(whole):
            whole[k | low] = swap(whole[k], "head", low)
    state = pltpu.VMEM((2, heads, size, size), F32)
    qs, ks, vs, states, locals_ = [], [], [], [], []

    def local(c, after):
        chunk = spans[c][1] - spans[c][0]
        return call(
            functools.partial(local_kernel, spans[c], heads),
            [pltpu.VMEM((4, chunk, width), F32)],
            [level_weight, qs[c], ks[c], vs[c], grads, after],
            [SMEM] + [VMEM] * 4 + [ANY],
            100 * chunk * chunk * width if c >= CHUNKS - 2 else 0,
        )[0]

    after = None
    for c in range(CHUNKS):
        pieces = {**whole, 0: mine[c]}
        span = spans[c]
        chunk = span[1] - span[0]
        ready = [after] if c else []
        if c == CHUNKS - 1:
            near = [pieces[k] for k in sorted(pieces)]
            begun, before = call(
                functools.partial(early_kernel, span, len(near)),
                [pltpu.VMEM((chunk, 3 * width), F32), state],
                [weights, *near, *states],
                [VMEM] * (1 + len(near) + len(states)),
                0,
            )
            ready.append(begun)
        pieces[top] = tie(arrived[c], *ready) if ready else arrived[c]
        for low in lows:
            for k in [k for k in sorted(pieces) if k & top]:
                pieces[k | low] = swap(pieces[k], "head", low)
        segments = [pieces[k] for k in sorted(pieces)]
        flat = pltpu.VMEM((chunk, width), BF16)
        if c < CHUNKS - 1:
            if c > 0:
                locals_.append(local(c - 1, pieces[top]))
            operands = [weights, grads, *segments, *locals_[-1:]]
            got = call(
                functools.partial(project_kernel, span, len(segments), heads),
                [flat, flat, flat, state],
                operands,
                [VMEM] * (2 + len(segments)) + [ANY] * len(locals_[-1:]),
                0,
            )
        else:
            middle = segments[len(near) : -1]
            if middle:
                (begun,) = call(
                    functools.partial(more_kernel, span, len(near) * inputs.shape[1]),
                    [pltpu.VMEM((chunk, 3 * width), F32)],
                    [weights, begun, *middle],
                    [VMEM] * (2 + len(middle)),
                    0,
                )
            got = call(
                functools.partial(last_kernel, span, heads),
                [
                    flat,
                    flat,
                    flat,
                    state,
                    state,
                    *[pltpu.VMEM((2, heads // GROUP, size, size), BF16)] * (GROUP - 1),
                ],
                [weights, grads, begun, before, segments[-1]],
                [VMEM] * 5,
                0,
            )
        qs.append(got[0])
        ks.append(got[1])
        vs.append(got[2])
        states.append(got[3])
        after = got[3]
    levels, fillers = exchange(got[4], got[5:], local, range(len(locals_), CHUNKS))
    locals_ += fillers
    shapes = [jax.ShapeDtypeStruct((rows, width), BF16)] * 4
    top = len(levels) // GROUP
    flats = [*qs, *ks, *vs]
    scratch = [
        pltpu.VMEM((2, rows, width), BF16),
        pltpu.VMEM((heads, size, size), F32),
        pltpu.SemaphoreType.DMA((2, CHUNKS)),
    ]
    operands = [level_weight, grads, *levels[:-GROUP], *flats, *states, *locals_]
    *written, base = call(
        functools.partial(early_side_kernel, spans, heads, top),
        [*shapes, pltpu.VMEM((CHUNKS, heads, size, size), F32)],
        operands,
        [SMEM] + [VMEM] * (len(operands) - 1),
        0,
        scratch,
        [ANY] * 4 + [VMEM],
        8,
    )
    operands = [level_weight, grads, base, *levels[-GROUP:], *flats, *locals_]
    return call(
        functools.partial(late_side_kernel, spans, heads, top),
        shapes,
        [*operands, *written],
        [SMEM] + [VMEM] * (len(operands) - 1) + [ANY] * 4,
        0,
        scratch,
        [ANY] * 4,
        8,
        aliases={len(operands) + j: j for j in range(4)},
    )


def solution(mesh):
    in_specs = (P("seq", "head"), P(None, None, "head"), P("head", None), P("seq", "head"))
    out_specs = (P("seq", "head"), P("seq", "head"), P("seq", "head"), P("seq", "head"))
    return jax.shard_map(
        per_device, mesh=mesh, in_specs=in_specs, out_specs=out_specs, check_vma=False
    )
```
